32 devices in a mesh: ctx: 4 (over y, x), ch: 8 (over z, core).
Axes of the slice: x: 2, y: 2, z: 4, core: 2. Of those that a mesh axis runs over, the one named last changes fastest.
Arguments:
- qkv: bfloat16 [3, 512, 4096], P(None, 'ch', 'ctx'), may hold values from -6 to 6
- short_taps: float32 [3, 512, 7], P(None, 'ch'), may hold values from -2 to 2
- long_filter: float32 [512, 4096], P('ch', 'ctx'), may hold values from -0.09375 to 0.09375
- skip_gain: float32 [512], P('ch'), may hold values from -4 to 4
- out_weight: bfloat16 [8192, 512], P('ch'), may hold values from -0.25 to 0.25
Outputs:
- projected: bfloat16 [8192, 4096], P('ch', 'ctx')
The draws below stay inside these ranges and needn't reach their ends.
All inputs are finite; a program needn't handle non-finite values.
Results may differ from the reference program's by a relative error of at most 0.0049.
Values may be sent and summed in bfloat16 or wider, within the bound.
No kernel may reach another device: no remote copies, remote signals or barrier semaphores. Data moves between devices by JAX's collectives and lax.ppermute only.
A program may use at most 64 MiB of HBM per device.

```python
import jax
import jax.numpy as jnp
from jax import lax

DMODEL = 8192
CHANNELS = 512
TAPS = 7
SEQ = 4096


def level_of(stream_key, shape, shards, least, high):
    loudness, own = 1.0, jax.random.fold_in(stream_key, 6)
    for dim, parts in shards:
        steps = jnp.exp(jax.random.uniform(jax.random.fold_in(own, dim), (parts,), jnp.float32, least / len(shards), high / len(shards)))
        loudness = loudness * jnp.repeat(steps, shape[dim] // parts).reshape([-1 if axis == dim else 1 for axis in range(len(shape))])
    return loudness


def gaussian(stream_key, dims, scale, bound, pieces=(), kind=jnp.bfloat16):
    values = jax.random.normal(stream_key, dims, jnp.float32) * scale
    if len(pieces) > 0:
        values = level_of(stream_key, dims, pieces, -0.22, 0.18) * values
    return jnp.clip(values, min=-bound, max=bound).astype(kind)


def setup_inputs(seed: int = 0) -> dict:
    keys = jax.random.split(jax.random.key(seed), 6)
    qkv = gaussian(keys[0], (3, CHANNELS, SEQ), 1.0, 6.0, ((1, 8), (2, 4)))
    short_taps = gaussian(keys[1], (3, CHANNELS, TAPS), TAPS ** -0.5, 2.0, ((1, 8),), jnp.float32)
    long_filter = gaussian(keys[2], (CHANNELS, SEQ), SEQ ** -0.5, 0.09375, ((0, 8), (1, 4)), jnp.float32)
    skip_gain = gaussian(keys[3], (CHANNELS,), 1.0, 4.0, ((0, 8),), jnp.float32)
    out_weight = gaussian(keys[4], (DMODEL, CHANNELS), CHANNELS ** -0.5, 0.25, ((0, 8),))
    return {"qkv": qkv, "short_taps": short_taps, "long_filter": long_filter, "skip_gain": skip_gain, "out_weight": out_weight}


def short_conv(padded, short_taps, length):
    tap_count = short_taps.shape[2]
    result = jnp.zeros(padded.shape[:2] + (length,), jnp.float32)
    for offset in range(tap_count):
        begin_at = tap_count - 1 - offset
        result = result + short_taps[:, :, offset:offset + 1] * padded[:, :, begin_at:begin_at + length]
    return result


def long_conv(signal, kernel):
    length = signal.shape[1]

    def one_group(members):
        sig_rows, ker_rows = members
        spectrum = jnp.fft.rfft(sig_rows, n=2 * length, axis=-1) * jnp.fft.rfft(ker_rows, n=2 * length, axis=-1)
        return jnp.fft.irfft(spectrum, n=2 * length, axis=-1)[:, :length]

    grouped = lax.map(one_group, (signal.reshape(-1, 16, length), kernel.reshape(-1, 16, length)))
    return grouped.reshape(signal.shape)


def reference(qkv, short_taps, long_filter, skip_gain, out_weight):
    tap_count = short_taps.shape[2]
    padded = jnp.pad(qkv.astype(jnp.float32), ((0, 0), (0, 0), (tap_count - 1, 0)))
    featured = short_conv(padded, short_taps, qkv.shape[2])
    product = featured[1] * featured[2]
    mixed = long_conv(product, long_filter) + skip_gain[:, None] * product
    gated = (featured[0] * mixed).astype(jnp.bfloat16)
    return jnp.dot(out_weight, gated, preferred_element_type=jnp.float32).astype(jnp.bfloat16)
```

```python
import math

import numpy as np

import jax
import jax.numpy as jnp
from jax import lax
from jax.experimental import pallas as pl
from jax.experimental.pallas import tpu as pltpu
from jax.sharding import PartitionSpec as P

LANES = 128
PAD = 8


def split_table(table):
    high = table.astype(jnp.bfloat16)
    low = (table - high.astype(np.float64)).astype(jnp.bfloat16)
    return high, low


def dft_tables(rows):
    total = 2 * rows * LANES
    block = np.arange(rows, dtype=np.float64)
    freq = np.arange(rows, dtype=np.float64) + 0.5
    lane = np.arange(LANES, dtype=np.float64)
    head = 2.0 * math.pi * np.outer(freq, block) / (2 * rows)
    head_high, head_low = split_table(np.concatenate([np.cos(head), -np.sin(head)], axis=0))
    first = np.concatenate([head_high, head_high, head_low], axis=1)
    turn = 2.0 * math.pi * np.outer(freq, lane) / total
    twist = np.concatenate([np.cos(turn), np.sin(turn)], axis=1).astype(np.float32)
    inner = 2.0 * math.pi * np.outer(lane, lane) / LANES
    square = np.block([[np.cos(inner), -np.sin(inner)], [np.sin(inner), np.cos(inner)]])
    second = np.concatenate(split_table(square), axis=1)
    tail = head.T
    tail_high, tail_low = split_table(
        (2.0 / total) * np.concatenate([np.cos(tail), np.sin(tail)], axis=1)
    )
    last = np.concatenate([tail_high, tail_high, tail_low], axis=1)
    return first, twist, second, last


def halves(value):
    high = value.astype(jnp.bfloat16)
    low = (value - high.astype(jnp.float32)).astype(jnp.bfloat16)
    return high, low


def dot(left, right):
    return jnp.dot(left, right, preferred_element_type=jnp.float32)


def long_kernel(
    nodes, chans, per_node, taps_ref, skip_ref, first_ref, twist_ref, second_ref, last_ref, *refs
):
    pieces = refs[:nodes]
    outs = refs[nodes : 2 * nodes]
    raw, query, prod, mid, spec, unturned, final = refs[2 * nodes :]
    rows = nodes * per_node
    pitch = rows + PAD
    place = lax.axis_index("ctx")
    base = place * chans
    tap_count = taps_ref.shape[2]

    for stream in range(4):
        raw[stream, pl.ds(PAD - 1, chans, stride=pitch), :] = jnp.zeros((chans, LANES), jnp.float32)
    for mask in range(nodes):
        start = (place ^ mask) * per_node + PAD
        for stream in range(4):
            for tile in range(per_node):
                raw[stream, pl.ds(start + tile, chans, stride=pitch), :] = pieces[mask][
                    stream, :, tile * LANES : (tile + 1) * LANES
                ].astype(jnp.float32)

    lane = lax.broadcasted_iota(jnp.int32, (rows, LANES), 1)

    def featured(stream, chan):
        begin = chan * pitch + PAD
        now = raw[stream, begin : begin + rows, :]
        before = raw[stream, begin - 1 : begin - 1 + rows, :]
        total = taps_ref[stream, base + chan, 0] * now
        for shift in range(1, tap_count):
            mixed = jnp.where(lane >= LANES - shift, before, now)
            total = total + taps_ref[stream, base + chan, shift] * pltpu.roll(mixed, shift, 1)
        return total

    cos_twist = twist_ref[:, :LANES]
    sin_twist = twist_ref[:, LANES:]
    zero = jnp.zeros((rows, LANES), jnp.bfloat16)
    for chan in range(chans):
        query[chan * rows : (chan + 1) * rows, :] = featured(0, chan)
        product = featured(1, chan) * featured(2, chan)
        prod[chan * rows : (chan + 1) * rows, :] = product
        high, low = halves(product)
        begin = chan * pitch + PAD
        filt = raw[3, begin : begin + rows, :].astype(jnp.bfloat16)
        operand = jnp.concatenate(
            [
                jnp.concatenate([high, filt], axis=1),
                jnp.concatenate([low, zero], axis=1),
                jnp.concatenate([high, filt], axis=1),
            ],
            axis=0,
        )
        section = dot(first_ref[...], operand)
        for part in range(2):
            real = section[:rows, part * LANES : (part + 1) * LANES]
            imag = section[rows:, part * LANES : (part + 1) * LANES]
            turned = jnp.concatenate(
                [
                    real * cos_twist + imag * sin_twist,
                    imag * cos_twist - real * sin_twist,
                ],
                axis=1,
            )
            high, low = halves(turned)
            at = (part * chans + chan) * rows
            mid[0, at : at + rows, :] = high
            mid[1, at : at + rows, :] = low

    def inner(high, low):
        table_high = second_ref[:, : 2 * LANES]
        table_low = second_ref[:, 2 * LANES :]
        return dot(high, table_high) + dot(low, table_high) + dot(high, table_low)

    spec[...] = inner(mid[0], mid[1])
    for chan in range(chans):
        sig = spec[chan * rows : (chan + 1) * rows, :]
        fil = spec[(chans + chan) * rows : (chans + chan + 1) * rows, :]
        sig_real, sig_imag = sig[:, :LANES], sig[:, LANES:]
        fil_real, fil_imag = fil[:, :LANES], fil[:, LANES:]
        joined = jnp.concatenate(
            [
                sig_real * fil_real - sig_imag * fil_imag,
                -(sig_real * fil_imag + sig_imag * fil_real),
            ],
            axis=1,
        )
        high, low = halves(joined)
        mid[0, chan * rows : (chan + 1) * rows, :] = high
        mid[1, chan * rows : (chan + 1) * rows, :] = low
    half = chans * rows
    unturned[...] = inner(mid[0, :half, :], mid[1, :half, :])
    for chan in range(chans):
        back = unturned[chan * rows : (chan + 1) * rows, :]
        real, imag = back[:, :LANES], back[:, LANES:]
        turned = jnp.concatenate(
            [real * cos_twist + imag * sin_twist, imag * cos_twist - real * sin_twist], axis=0
        )
        high, low = halves(turned)
        convolved = dot(last_ref[...], jnp.concatenate([high, low, high], axis=0))
        span = slice(chan * rows, (chan + 1) * rows)
        mixed = convolved + skip_ref[base + chan] * prod[span, :]
        final[span, :] = query[span, :] * mixed
    for mask in range(nodes):
        start = (place ^ mask) * per_node
        for tile in range(per_node):
            outs[mask][:, tile * LANES : (tile + 1) * LANES] = final[
                pl.ds(start + tile, chans, stride=rows), :
            ].astype(jnp.bfloat16)


def long_mix(pieces, short_taps, skip_gain):
    nodes = len(pieces)
    _, chans, block = pieces[0].shape
    per_node = block // LANES
    rows = nodes * per_node
    first, twist, second, last = dft_tables(rows)
    whole = pl.BlockSpec(memory_space=pltpu.VMEM)
    scalars = pl.BlockSpec(memory_space=pltpu.SMEM)
    return pl.pallas_call(
        lambda *refs: long_kernel(nodes, chans, per_node, *refs),
        out_shape=[jax.ShapeDtypeStruct((chans, block), jnp.bfloat16)] * nodes,
        in_specs=[scalars, scalars] + [whole] * (4 + nodes),
        out_specs=[whole] * nodes,
        scratch_shapes=[
            pltpu.VMEM((4, chans * (rows + PAD), LANES), jnp.float32),
            pltpu.VMEM((chans * rows, LANES), jnp.float32),
            pltpu.VMEM((chans * rows, LANES), jnp.float32),
            pltpu.VMEM((2, 2 * chans * rows, 2 * LANES), jnp.bfloat16),
            pltpu.VMEM((2 * chans * rows, 2 * LANES), jnp.float32),
            pltpu.VMEM((chans * rows, 2 * LANES), jnp.float32),
            pltpu.VMEM((chans * rows, LANES), jnp.float32),
        ],
        compiler_params=pltpu.CompilerParams(vmem_limit_bytes=40 << 20),
        name="long_mix",
    )(short_taps, skip_gain, first, twist, second, last, *pieces)


def project_kernel(nodes, stacks, weight_ref, *refs):
    blocks = refs[: 2 * stacks]
    out_ref, gathered = refs[2 * stacks :]
    place = lax.axis_index("ctx")
    spot = lax.axis_index("ch")
    chans = blocks[0].shape[1]

    @pl.when(pl.program_id(0) == 0)
    def _():
        for index in range(2 * stacks):
            core, depth = index // stacks, index % stacks
            owner = spot ^ (2 * depth + core)
            for mask in range(nodes):
                row = (owner * nodes + (place ^ mask)) * chans
                gathered[pl.ds(pl.multiple_of(row, chans), chans), :] = blocks[index][mask]

    out_ref[...] = dot(weight_ref[...], gathered[...]).astype(jnp.bfloat16)


def project(blocks, out_weight, tile):
    nodes, _, block = blocks[0].shape
    features, channels = out_weight.shape
    whole = pl.BlockSpec(memory_space=pltpu.VMEM)
    return pl.pallas_call(
        lambda *refs: project_kernel(nodes, len(blocks) // 2, *refs),
        grid=(features // tile,),
        out_shape=jax.ShapeDtypeStruct((features, block), jnp.bfloat16),
        in_specs=[pl.BlockSpec((tile, channels), lambda i: (i, 0))] + [whole] * len(blocks),
        out_specs=pl.BlockSpec((tile, block), lambda i: (i, 0)),
        scratch_shapes=[pltpu.VMEM((channels, block), jnp.bfloat16)],
        compiler_params=pltpu.CompilerParams(vmem_limit_bytes=40 << 20),
        name="project",
    )(out_weight, *blocks)


def project_plain(blocks, out_weight):
    nodes, chans, block = blocks[0].shape
    stacks = len(blocks) // 2
    place = lax.axis_index("ctx")
    spot = lax.axis_index("ch")
    found = jnp.stack(blocks).reshape(2, stacks, nodes, chans, block)
    index = jnp.arange(2 * stacks, dtype=jnp.int32) ^ spot
    found = found[index % 2, index // 2]
    found = found[:, jnp.arange(nodes, dtype=jnp.int32) ^ place]
    summed = jnp.dot(
        out_weight, found.reshape(-1, block), preferred_element_type=jnp.float32
    )
    return summed.astype(jnp.bfloat16)


def local(qkv, short_taps, long_filter, skip_gain, out_weight):
    nodes = lax.axis_size("ctx")
    spread = lax.axis_size("ch")
    stacks = spread // 2
    place = lax.axis_index("ctx")
    streams, chan_dev, block = qkv.shape
    chans = chan_dev // nodes

    by_node = qkv.reshape(streams, nodes, chans, block)
    filters = long_filter.reshape(nodes, chans, block)
    pieces = []
    for mask in range(nodes):
        target = place ^ mask
        piece = jnp.concatenate(
            [
                lax.dynamic_index_in_dim(by_node, target, 1, False),
                lax.dynamic_index_in_dim(filters, target, 0, True).astype(jnp.bfloat16),
            ],
            axis=0,
        )
        if mask:
            piece = lax.ppermute(piece, "ctx", [(i, i ^ mask) for i in range(nodes)])
        pieces.append(piece)

    gated = long_mix(pieces, short_taps, skip_gain)

    mine = [gated[0]] + [
        lax.ppermute(gated[mask], "ctx", [(i, i ^ mask) for i in range(nodes)])
        for mask in range(1, nodes)
    ]
    mine = jnp.stack(mine)
    column = [mine] + [
        lax.ppermute(mine, "ch", [(i, i ^ (2 * depth)) for i in range(spread)])
        for depth in range(1, stacks)
    ]
    other = [lax.ppermute(part, "ch", [(i, i ^ 1) for i in range(spread)]) for part in column]
    if chans % 16:
        return project_plain(column + other, out_weight)
    return project(column + other, out_weight, 256)


def solution(mesh):
    placed = (P(None, "ch", "ctx"), P(None, "ch", None), P("ch", "ctx"), P("ch"), P("ch", None))
    return jax.shard_map(
        local, mesh=mesh, in_specs=placed, out_specs=P("ch", "ctx"), check_vma=False
    )
```

```python
import math

import numpy as np

import jax
import jax.numpy as jnp
from jax import lax
from jax.experimental import pallas as pl
from jax.experimental.pallas import tpu as pltpu
from jax.sharding import PartitionSpec as P

LANES = 128
PAD = 8
LANE_V = 16
LANE_Q = 32


def split_table(table):
    high = table.astype(jnp.bfloat16)
    low = (table - high.astype(np.float64)).astype(jnp.bfloat16)
    return high, low


def dft_tables(rows):
    total = 2 * rows * LANES
    block = np.arange(rows, dtype=np.float64)
    freq = np.arange(rows, dtype=np.float64) + 0.5
    lane = np.arange(LANES, dtype=np.float64)
    head = 2.0 * math.pi * np.outer(freq, block) / (2 * rows)
    first = np.concatenate(
        split_table(np.concatenate([np.cos(head), -np.sin(head)], axis=0)), axis=1
    )
    turn = 2.0 * math.pi * np.outer(freq, lane) / total
    twist = np.concatenate([np.cos(turn), np.sin(turn)], axis=1).astype(np.float32)
    inner = 2.0 * math.pi * np.outer(lane, lane) / LANES
    square = np.block([[np.cos(inner), -np.sin(inner)], [np.sin(inner), np.cos(inner)]])
    second = np.concatenate(split_table(square), axis=1)
    tail = head.T
    tail_high, tail_low = split_table(
        (2.0 / total) * np.concatenate([np.cos(tail), np.sin(tail)], axis=1)
    )
    last = np.concatenate([tail_high, tail_high, tail_low], axis=1)
    return first, twist, second, last


def halves(value):
    high = value.astype(jnp.bfloat16)
    low = (value - high.astype(jnp.float32)).astype(jnp.bfloat16)
    return high, low


def dot(left, right):
    return jnp.dot(left, right, preferred_element_type=jnp.float32)


def rolled_taps(values, taps):
    total = taps[:, :1] * values
    for shift in range(1, taps.shape[1]):
        total = total + taps[:, shift : shift + 1] * pltpu.roll(values, shift, 1)
    return total


def in_hbm(*arrays):
    return [pltpu.with_memory_space_constraint(array, pltpu.HBM) for array in arrays]


def tables_kernel(count, *refs):
    sources, skip_ref = refs[:count], refs[count]
    outs, column_ref = refs[count + 2 : 2 * count + 2], refs[2 * count + 2]
    skips, sems = refs[2 * count + 3 :]
    moves = [
        pltpu.make_async_copy(source, out, sems.at[index])
        for index, (source, out) in enumerate(zip(sources, outs))
    ]
    moves.append(pltpu.make_async_copy(skip_ref, skips, sems.at[count]))
    for move in moves:
        move.start()
    moves[count].wait()
    column_ref[...] = jnp.broadcast_to(skips[...].reshape(1, -1), (8, skips.shape[0])).T
    for move in moves[:count]:
        move.wait()


def near_tables(rows, skip_gain, after):
    tables = dft_tables(rows)
    count = len(tables)
    far = pl.BlockSpec(memory_space=pltpu.HBM)
    near = pl.BlockSpec(memory_space=pltpu.VMEM)
    return pl.pallas_call(
        lambda *refs: tables_kernel(count, *refs),
        out_shape=[jax.ShapeDtypeStruct(table.shape, table.dtype) for table in tables]
        + [jax.ShapeDtypeStruct((skip_gain.shape[0], 8), jnp.float32)],
        in_specs=[far] * (count + 1) + [near],
        out_specs=[near] * (count + 1),
        scratch_shapes=[
            pltpu.VMEM(skip_gain.shape, jnp.float32),
            pltpu.SemaphoreType.DMA((count + 1,)),
        ],
        compiler_params=pltpu.CompilerParams(vmem_limit_bytes=16 << 20),
        name="near_tables",
    )(*in_hbm(*[jnp.asarray(table) for table in tables], skip_gain), after)


def pack_kernel(nodes, chans, qkv_ref, filter_ref, flat_ref, *refs):
    outs = refs[:nodes]
    query_ref, taps_ref = refs[nodes : nodes + 2]
    filters, streams, flat, sems = refs[nodes + 2 :]
    place = lax.axis_index("ctx")
    block = qkv_ref.shape[2]
    rim = taps_ref.shape[2] - 1
    moves = [
        pltpu.make_async_copy(flat_ref, flat, sems.at[3]),
        pltpu.make_async_copy(qkv_ref.at[pl.ds(1, 2)], streams, sems.at[0]),
        pltpu.make_async_copy(qkv_ref.at[0], query_ref, sems.at[1]),
        pltpu.make_async_copy(filter_ref, filters, sems.at[2]),
    ]
    for move in moves:
        move.start()
    lane = lax.broadcasted_iota(jnp.int32, (chans, LANES), 1)

    def place_at(tile, source, target, size, under):
        moved = pltpu.roll(tile, (target - source) % LANES, 1)
        return jnp.where((lane >= target) & (lane < target + size), moved, under)

    moves[0].wait()
    for stream in range(3):
        taps_ref[stream] = flat[stream].T
    moves[1].wait()
    for mask in range(nodes):
        rows = pl.ds(pl.multiple_of((place ^ mask) * chans, chans), chans)
        edge = jnp.zeros((chans, LANES), jnp.float32)
        product = None
        for stream in range(2):
            values = streams[stream, rows, :].astype(jnp.float32)
            at = stream * LANE_V
            edge = place_at(values[:, block - LANES :], LANES - rim, at, rim, edge)
            edge = place_at(values[:, :LANES], 0, at + rim, rim, edge)
            featured = rolled_taps(values, taps_ref[1 + stream, rows, :])
            product = featured if product is None else product * featured
        outs[mask][:, :block] = product.astype(jnp.bfloat16)
        outs[mask][:, 2 * block :] = edge.astype(jnp.bfloat16)
    moves[2].wait()
    queries = jnp.zeros((chans, LANES), jnp.float32)
    for share in range(nodes):
        tile = query_ref[share * chans : (share + 1) * chans, block - LANES :]
        queries = place_at(
            tile.astype(jnp.float32), LANES - rim, LANE_Q + share * rim, rim, queries
        )
    for mask in range(nodes):
        edge = outs[mask][:, 2 * block :].astype(jnp.float32)
        outs[mask][:, 2 * block :] = jnp.where(lane >= LANE_Q, queries, edge).astype(jnp.bfloat16)
    moves[3].wait()
    for mask in range(nodes):
        rows = pl.ds(pl.multiple_of((place ^ mask) * chans, chans), chans)
        outs[mask][:, block : 2 * block] = filters[rows, :].astype(jnp.bfloat16)


def pack(qkv, long_filter, short_taps, nodes, chans):
    _, every, block = qkv.shape
    far = pl.BlockSpec(memory_space=pltpu.HBM)
    near = pl.BlockSpec(memory_space=pltpu.VMEM)
    flat = jnp.swapaxes(short_taps, 1, 2)
    *pieces, query, taps = pl.pallas_call(
        lambda *refs: pack_kernel(nodes, chans, *refs),
        out_shape=[jax.ShapeDtypeStruct((chans, 2 * block + LANES), jnp.bfloat16)] * nodes
        + [
            jax.ShapeDtypeStruct((every, block), jnp.bfloat16),
            jax.ShapeDtypeStruct(short_taps.shape, jnp.float32),
        ],
        in_specs=[far] * 3,
        out_specs=[near] * (nodes + 2),
        scratch_shapes=[
            pltpu.VMEM((every, block), jnp.float32),
            pltpu.VMEM((2, every, block), jnp.bfloat16),
            pltpu.VMEM(flat.shape, jnp.float32),
            pltpu.SemaphoreType.DMA((4,)),
        ],
        compiler_params=pltpu.CompilerParams(vmem_limit_bytes=16 << 20),
        name="pack",
    )(*in_hbm(qkv, long_filter, flat))
    return pieces, query, taps


def query_kernel(nodes, query_ref, taps_ref, *refs):
    pieces = refs[:nodes]
    out_ref = refs[nodes]
    place = lax.axis_index("ctx")
    _, chans, block = out_ref.shape
    rim = taps_ref.shape[2] - 1
    lane = lax.broadcasted_iota(jnp.int32, (chans, LANES), 1)
    edge = jnp.zeros((chans, LANES), jnp.float32)
    for mask in range(1, nodes):
        before = (place ^ mask) == place - 1
        found = pieces[mask][:, pieces[mask].shape[1] - LANES :].astype(jnp.float32)
        edge = jnp.where(before, found, edge)
    for mask in range(nodes):
        share = place ^ mask
        rows = pl.ds(pl.multiple_of(share * chans, chans), chans)
        taps = taps_ref[0, rows, :]
        values = query_ref[rows, :].astype(jnp.float32)
        history = pltpu.roll(edge, LANES - LANE_Q - (share + 1) * rim, 1)
        first = taps[:, :1] * values[:, :LANES]
        for shift in range(1, rim + 1):
            joined = jnp.where(lane >= LANES - shift, history, values[:, :LANES])
            first = first + taps[:, shift : shift + 1] * pltpu.roll(joined, shift, 1)
        out_ref[mask] = rolled_taps(values, taps)
        out_ref[mask, :, :LANES] = first


def query_features(query, short_taps, pieces, nodes, chans):
    near = pl.BlockSpec(memory_space=pltpu.VMEM)
    return pl.pallas_call(
        lambda *refs: query_kernel(nodes, *refs),
        out_shape=jax.ShapeDtypeStruct((nodes, chans, query.shape[1]), jnp.float32),
        in_specs=[near] * (2 + nodes),
        out_specs=near,
        compiler_params=pltpu.CompilerParams(vmem_limit_bytes=16 << 20),
        name="query_features",
    )(query, short_taps, *pieces)


def long_kernel(
    nodes, chans, per_node, repair, taps_ref, first_ref, twist_ref, second_ref, last_ref, skip_ref, *refs
):
    pieces = refs[:nodes]
    outs = refs[nodes : 2 * nodes]
    raw, edges, mid, spec, unturned, final = refs[2 * nodes :]
    rows = nodes * per_node
    pitch = rows + PAD
    place = lax.axis_index("ctx")
    base = place * chans
    block = per_node * LANES

    for mask in range(nodes):
        start = (place ^ mask) * per_node
        for part in range(2):
            for tile in range(per_node):
                at = part * block + tile * LANES
                raw[part, pl.ds(start + tile, chans, stride=pitch), :] = pieces[mask][
                    :, at : at + LANES
                ].astype(jnp.float32)
        if repair:
            edges[(place ^ mask) + 1] = pieces[mask][:, 2 * block :].astype(jnp.float32)
    if repair:
        rim = taps_ref.shape[2] - 1
        lane = lax.broadcasted_iota(jnp.int32, (chans, LANES), 1)
        own = pl.ds(pl.multiple_of(base, chans), chans)
        edges[0] = jnp.zeros((chans, LANES), jnp.float32)
        for node in range(nodes):
            before, now = edges[node], edges[node + 1]
            product = None
            for stream in range(2):
                back = (LANES - stream * LANE_V) % LANES
                joined = jnp.where(lane < stream * LANE_V + rim, before, now)
                if back:
                    joined = pltpu.roll(joined, back, 1)
                featured = rolled_taps(joined, taps_ref[1 + stream, own, :])
                product = featured if product is None else product * featured
            product = pltpu.roll(product, LANES - rim, 1).astype(jnp.bfloat16).astype(jnp.float32)
            spot = pl.ds(node * per_node, chans, stride=pitch)
            raw[0, spot, :] = jnp.where(lane < rim, product, raw[0, spot, :])

    cos_twist = twist_ref[:, :LANES]
    sin_twist = twist_ref[:, LANES:]
    for chan in range(chans):
        span = slice(chan * pitch, chan * pitch + rows)
        both = jnp.concatenate([raw[0, span, :], raw[1, span, :]], axis=1).astype(jnp.bfloat16)
        section = dot(first_ref[...], jnp.concatenate([both, both], axis=0))
        for part in range(2):
            real = section[:rows, part * LANES : (part + 1) * LANES]
            imag = section[rows:, part * LANES : (part + 1) * LANES]
            turned = jnp.concatenate(
                [
                    real * cos_twist + imag * sin_twist,
                    imag * cos_twist - real * sin_twist,
                ],
                axis=1,
            )
            high, low = halves(turned)
            at = (part * chans + chan) * rows
            mid[0, at : at + rows, :] = high
            mid[1, at : at + rows, :] = low

    def inner(high, low):
        table_high = second_ref[:, : 2 * LANES]
        table_low = second_ref[:, 2 * LANES :]
        return dot(high, table_high) + dot(low, table_high) + dot(high, table_low)

    spec[...] = inner(mid[0], mid[1])
    for chan in range(chans):
        sig = spec[chan * rows : (chan + 1) * rows, :]
        fil = spec[(chans + chan) * rows : (chans + chan + 1) * rows, :]
        sig_real, sig_imag = sig[:, :LANES], sig[:, LANES:]
        fil_real, fil_imag = fil[:, :LANES], fil[:, LANES:]
        joined = jnp.concatenate(
            [
                sig_real * fil_real - sig_imag * fil_imag,
                -(sig_real * fil_imag + sig_imag * fil_real),
            ],
            axis=1,
        )
        high, low = halves(joined)
        mid[0, chan * rows : (chan + 1) * rows, :] = high
        mid[1, chan * rows : (chan + 1) * rows, :] = low
    skips = skip_ref[pl.ds(pl.multiple_of(base, chans), chans), :]
    half = chans * rows
    unturned[...] = inner(mid[0, :half, :], mid[1, :half, :])
    for chan in range(chans):
        back = unturned[chan * rows : (chan + 1) * rows, :]
        real, imag = back[:, :LANES], back[:, LANES:]
        turned = jnp.concatenate(
            [real * cos_twist + imag * sin_twist, imag * cos_twist - real * sin_twist], axis=0
        )
        high, low = halves(turned)
        convolved = dot(last_ref[...], jnp.concatenate([high, low, high], axis=0))
        product = raw[0, chan * pitch : chan * pitch + rows, :]
        final[chan * rows : (chan + 1) * rows, :] = convolved + skips[chan : chan + 1, :1] * product
    for mask in range(nodes):
        start = (place ^ mask) * per_node
        for tile in range(per_node):
            outs[mask][:, tile * LANES : (tile + 1) * LANES] = final[
                pl.ds(start + tile, chans, stride=rows), :
            ].astype(jnp.bfloat16)


def long_mix(pieces, taps, tables, block):
    nodes = len(pieces)
    chans, width = pieces[0].shape
    per_node = block // LANES
    rows = nodes * per_node
    near = pl.BlockSpec(memory_space=pltpu.VMEM)
    return pl.pallas_call(
        lambda *refs: long_kernel(nodes, chans, per_node, width > 2 * block, *refs),
        out_shape=[jax.ShapeDtypeStruct((chans, block), jnp.bfloat16)] * nodes,
        in_specs=[near] * (1 + len(tables) + nodes),
        out_specs=[near] * nodes,
        scratch_shapes=[
            pltpu.VMEM((2, chans * (rows + PAD), LANES), jnp.float32),
            pltpu.VMEM((nodes + 1, chans, LANES), jnp.float32),
            pltpu.VMEM((2, 2 * chans * rows, 2 * LANES), jnp.bfloat16),
            pltpu.VMEM((2 * chans * rows, 2 * LANES), jnp.float32),
            pltpu.VMEM((chans * rows, 2 * LANES), jnp.float32),
            pltpu.VMEM((chans * rows, LANES), jnp.float32),
        ],
        compiler_params=pltpu.CompilerParams(vmem_limit_bytes=24 << 20),
        name="long_mix",
    )(taps, *tables, *pieces)


def project_kernel(nodes, weight_ref, *refs):
    stacks = (len(refs) - 4) // 2
    blocks = refs[: 2 * stacks]
    out_ref, gathered, held, sems = refs[2 * stacks :]
    place = lax.axis_index("ctx")
    spot = lax.axis_index("ch")
    chans = blocks[0].shape[1]
    for index in range(2 * stacks):
        owner = spot ^ (2 * (index % stacks) + index // stacks)
        for mask in range(nodes):
            row = (owner * nodes + (place ^ mask)) * chans
            gathered[pl.ds(pl.multiple_of(row, chans), chans), :] = blocks[index][mask]

    parts = held.shape[0]
    rows = held.shape[1]
    copies = []
    for part in range(parts):
        span = slice(part * rows, (part + 1) * rows)
        held[part] = dot(weight_ref[span, :], gathered[...]).astype(jnp.bfloat16)
        copies.append(
            pltpu.make_async_copy(held.at[part], out_ref.at[pl.ds(part * rows, rows), :], sems.at[part])
        )
        copies[-1].start()
    for copy in copies:
        copy.wait()


def project(blocks, out_weight, parts):
    nodes, _, block = blocks[0].shape
    features, channels = out_weight.shape
    whole = pl.BlockSpec(memory_space=pltpu.VMEM)
    return pl.pallas_call(
        lambda *refs: project_kernel(nodes, *refs),
        out_shape=jax.ShapeDtypeStruct((features, block), jnp.bfloat16),
        in_specs=[whole] * (1 + len(blocks)),
        out_specs=pl.BlockSpec(memory_space=pl.ANY),
        scratch_shapes=[
            pltpu.VMEM((channels, block), jnp.bfloat16),
            pltpu.VMEM((parts, features // parts, block), jnp.bfloat16),
            pltpu.SemaphoreType.DMA((parts,)),
        ],
        compiler_params=pltpu.CompilerParams(vmem_limit_bytes=16 << 20),
        name="project",
    )(out_weight, *blocks)


def project_plain(blocks, out_weight):
    nodes, chans, block = blocks[0].shape
    stacks = len(blocks) // 2
    place = lax.axis_index("ctx")
    spot = lax.axis_index("ch")
    found = jnp.stack(blocks).reshape(2, stacks, nodes, chans, block)
    index = jnp.arange(2 * stacks, dtype=jnp.int32) ^ spot
    found = found[index % 2, index // 2]
    found = found[:, jnp.arange(nodes, dtype=jnp.int32) ^ place]
    summed = jnp.dot(
        out_weight, found.reshape(-1, block), preferred_element_type=jnp.float32
    )
    return summed.astype(jnp.bfloat16)


def features_plain(qkv, short_taps):
    block = qkv.shape[2]
    tap_count = short_taps.shape[2]
    devices = lax.axis_size("ctx")
    route = [(i, i + 1) for i in range(devices - 1)]
    history = lax.ppermute(qkv[:, :, block - (tap_count - 1) :], "ctx", route)
    extended = jnp.concatenate([history, qkv], axis=2).astype(jnp.float32)
    result = jnp.zeros(qkv.shape, jnp.float32)
    for offset in range(tap_count):
        begin = tap_count - 1 - offset
        result = (
            result
            + short_taps[:, :, offset : offset + 1] * extended[:, :, begin : begin + block]
        )
    return result


def swapped(block, mask, axis):
    if mask == 0:
        return block
    return lax.ppermute(block, axis, [(i, i ^ mask) for i in range(lax.axis_size(axis))])


def local(qkv, short_taps, long_filter, skip_gain, out_weight):
    nodes = lax.axis_size("ctx")
    spread = lax.axis_size("ch")
    stacks = spread // 2
    place = lax.axis_index("ctx")
    _, every, block = qkv.shape
    chans = every // nodes
    fits = chans % 16 == 0

    if fits:
        pieces, query, taps = pack(qkv, long_filter, short_taps, nodes, chans)
    else:
        taps = short_taps
        query, key, value = features_plain(qkv, short_taps)
        both = jnp.concatenate([key * value, long_filter], axis=1).astype(jnp.bfloat16)
        both = both.reshape(nodes, chans, 2 * block)
        pieces = [lax.dynamic_index_in_dim(both, place ^ mask, 0, False) for mask in range(nodes)]
    pieces = [swapped(pieces[mask], mask, "ctx") for mask in range(nodes)]
    tables = near_tables(nodes * block // LANES, skip_gain, pieces[0])
    mixed = long_mix(pieces, taps, tables, block)

    if fits:
        tied = lax.optimization_barrier((pieces, mixed[0]))[0]
        featured = query_features(query, taps, tied, nodes, chans)
    else:
        featured = query.reshape(nodes, chans, block)[jnp.arange(nodes, dtype=jnp.int32) ^ place]
    mixed = jnp.stack([swapped(mixed[mask], mask, "ctx") for mask in range(nodes)])
    gated = (featured * mixed.astype(jnp.float32)).astype(jnp.bfloat16)

    column = [swapped(gated, 2 * depth, "ch") for depth in range(stacks)]
    blocks = column + [swapped(part, 1, "ch") for part in column]
    if fits:
        return project(blocks, out_weight, 4)
    return project_plain(blocks, out_weight)


def solution(mesh):
    placed = (P(None, "ch", "ctx"), P(None, "ch", None), P("ch", "ctx"), P("ch"), P("ch", None))
    return jax.shard_map(
        local, mesh=mesh, in_specs=placed, out_specs=P("ch", "ctx"), check_vma=False
    )
```

```python
import math

import numpy as np

import jax
import jax.numpy as jnp
from jax import lax
from jax.experimental import pallas as pl
from jax.experimental.pallas import tpu as pltpu
from jax.sharding import PartitionSpec as P

LANES = 128
PAD = 8
LANE_V = 16
LANE_Q = 32


def split_table(table):
    high = table.astype(jnp.bfloat16)
    low = (table - high.astype(np.float64)).astype(jnp.bfloat16)
    return high, low


def dft_tables(rows):
    total = 2 * rows * LANES
    block = np.arange(rows, dtype=np.float64)
    freq = np.arange(rows, dtype=np.float64) + 0.5
    lane = np.arange(LANES, dtype=np.float64)
    head = 2.0 * math.pi * np.outer(freq, block) / (2 * rows)
    first = np.concatenate(
        split_table(np.concatenate([np.cos(head), -np.sin(head)], axis=0)), axis=1
    )
    turn = 2.0 * math.pi * np.outer(freq, lane) / total
    twist = np.concatenate([np.cos(turn), np.sin(turn)], axis=1).astype(np.float32)
    inner = 2.0 * math.pi * np.outer(lane, lane) / LANES
    square = np.block([[np.cos(inner), -np.sin(inner)], [np.sin(inner), np.cos(inner)]])
    square_high, square_low = split_table(square)
    second = np.concatenate([square_high, square_high, square_low], axis=0)
    tail = head.T
    tail_high, tail_low = split_table(
        (2.0 / total) * np.concatenate([np.cos(tail), np.sin(tail)], axis=1)
    )
    last = np.concatenate([tail_high, tail_high, tail_low], axis=1)
    return first, twist, second, last


def halves(value):
    high = value.astype(jnp.bfloat16)
    low = (value - high.astype(jnp.float32)).astype(jnp.bfloat16)
    return high, low


def dot(left, right):
    return jnp.dot(left, right, preferred_element_type=jnp.float32)


def rolled_taps(values, taps):
    total = taps[:, :1] * values
    for shift in range(1, taps.shape[1]):
        total = total + taps[:, shift : shift + 1] * pltpu.roll(values, shift, 1)
    return total


def in_hbm(*arrays):
    return [pltpu.with_memory_space_constraint(array, pltpu.HBM) for array in arrays]


def tables_kernel(count, *refs):
    sources, skip_ref = refs[:count], refs[count]
    outs, column_ref = refs[count + 2 : 2 * count + 2], refs[2 * count + 2]
    skips, sems = refs[2 * count + 3 :]
    moves = [
        pltpu.make_async_copy(source, out, sems.at[index])
        for index, (source, out) in enumerate(zip(sources, outs))
    ]
    moves.append(pltpu.make_async_copy(skip_ref, skips, sems.at[count]))
    for move in moves:
        move.start()
    moves[count].wait()
    column_ref[...] = jnp.broadcast_to(skips[...].reshape(1, -1), (8, skips.shape[0])).T
    for move in moves[:count]:
        move.wait()


def near_tables(rows, skip_gain, out_weight, after):
    tables = [out_weight] + [jnp.asarray(table) for table in dft_tables(rows)]
    count = len(tables)
    far = pl.BlockSpec(memory_space=pltpu.HBM)
    near = pl.BlockSpec(memory_space=pltpu.VMEM)
    return pl.pallas_call(
        lambda *refs: tables_kernel(count, *refs),
        out_shape=[jax.ShapeDtypeStruct(table.shape, table.dtype) for table in tables]
        + [jax.ShapeDtypeStruct((skip_gain.shape[0], 8), jnp.float32)],
        in_specs=[far] * (count + 1) + [near],
        out_specs=[near] * (count + 1),
        scratch_shapes=[
            pltpu.VMEM(skip_gain.shape, jnp.float32),
            pltpu.SemaphoreType.DMA((count + 1,)),
        ],
        compiler_params=pltpu.CompilerParams(vmem_limit_bytes=16 << 20),
        name="near_tables",
    )(*in_hbm(*tables, skip_gain), after)


def pack_kernel(nodes, chans, qkv_ref, filter_ref, flat_ref, *refs):
    outs = refs[:nodes]
    query_ref, taps_ref = refs[nodes : nodes + 2]
    filters, streams, flat, sems = refs[nodes + 2 :]
    place = lax.axis_index("ctx")
    block = qkv_ref.shape[2]
    rim = taps_ref.shape[2] - 1
    moves = [
        pltpu.make_async_copy(flat_ref, flat, sems.at[0]),
        pltpu.make_async_copy(qkv_ref.at[0], query_ref, sems.at[1]),
        pltpu.make_async_copy(filter_ref, filters, sems.at[2]),
    ]
    shares = [
        pl.ds(pl.multiple_of((place ^ mask) * chans, chans), chans)
        for mask in reversed(range(nodes))
    ]
    arrivals = [
        pltpu.make_async_copy(
            qkv_ref.at[pl.ds(1, 2), rows, :], streams.at[:, rows, :], sems.at[3 + index]
        )
        for index, rows in enumerate(shares)
    ]
    for move in moves[:1] + arrivals + moves[1:]:
        move.start()
    lane = lax.broadcasted_iota(jnp.int32, (chans, LANES), 1)

    def place_at(tile, source, target, size, under):
        moved = pltpu.roll(tile, (target - source) % LANES, 1)
        return jnp.where((lane >= target) & (lane < target + size), moved, under)

    moves[0].wait()
    for stream in range(3):
        taps_ref[stream] = flat[stream].T
    for index, rows in enumerate(shares):
        mask = nodes - 1 - index
        arrivals[index].wait()
        edge = jnp.zeros((chans, LANES), jnp.float32)
        product = None
        for stream in range(2):
            values = streams[stream, rows, :].astype(jnp.float32)
            at = stream * LANE_V
            edge = place_at(values[:, block - LANES :], LANES - rim, at, rim, edge)
            edge = place_at(values[:, :LANES], 0, at + rim, rim, edge)
            featured = rolled_taps(values, taps_ref[1 + stream, rows, :])
            product = featured if product is None else product * featured
        outs[mask][:, :block] = product.astype(jnp.bfloat16)
        outs[mask][:, 2 * block :] = edge.astype(jnp.bfloat16)
    moves[1].wait()
    queries = jnp.zeros((chans, LANES), jnp.float32)
    for share in range(nodes):
        tile = query_ref[share * chans : (share + 1) * chans, block - LANES :]
        queries = place_at(
            tile.astype(jnp.float32), LANES - rim, LANE_Q + share * rim, rim, queries
        )
    for mask in range(nodes):
        edge = outs[mask][:, 2 * block :].astype(jnp.float32)
        outs[mask][:, 2 * block :] = jnp.where(lane >= LANE_Q, queries, edge).astype(jnp.bfloat16)
    moves[2].wait()
    for index, rows in enumerate(shares):
        mask = nodes - 1 - index
        outs[mask][:, block : 2 * block] = filters[rows, :].astype(jnp.bfloat16)


def pack(qkv, long_filter, short_taps, nodes, chans):
    _, every, block = qkv.shape
    far = pl.BlockSpec(memory_space=pltpu.HBM)
    near = pl.BlockSpec(memory_space=pltpu.VMEM)
    flat = jnp.swapaxes(short_taps, 1, 2)
    *pieces, query, taps = pl.pallas_call(
        lambda *refs: pack_kernel(nodes, chans, *refs),
        out_shape=[jax.ShapeDtypeStruct((chans, 2 * block + LANES), jnp.bfloat16)] * nodes
        + [
            jax.ShapeDtypeStruct((every, block), jnp.bfloat16),
            jax.ShapeDtypeStruct(short_taps.shape, jnp.float32),
        ],
        in_specs=[far] * 3,
        out_specs=[near] * (nodes + 2),
        scratch_shapes=[
            pltpu.VMEM((every, block), jnp.float32),
            pltpu.VMEM((2, every, block), jnp.bfloat16),
            pltpu.VMEM(flat.shape, jnp.float32),
            pltpu.SemaphoreType.DMA((3 + nodes,)),
        ],
        compiler_params=pltpu.CompilerParams(vmem_limit_bytes=16 << 20),
        name="pack",
    )(*in_hbm(qkv, long_filter, flat))
    return pieces, query, taps


def query_kernel(nodes, query_ref, taps_ref, *refs):
    pieces = refs[:nodes]
    out_ref = refs[nodes]
    place = lax.axis_index("ctx")
    _, chans, block = out_ref.shape
    rim = taps_ref.shape[2] - 1
    lane = lax.broadcasted_iota(jnp.int32, (chans, LANES), 1)
    edge = jnp.zeros((chans, LANES), jnp.float32)
    for mask in range(1, nodes):
        before = (place ^ mask) == place - 1
        found = pieces[mask][:, pieces[mask].shape[1] - LANES :].astype(jnp.float32)
        edge = jnp.where(before, found, edge)
    for mask in range(nodes):
        share = place ^ mask
        rows = pl.ds(pl.multiple_of(share * chans, chans), chans)
        taps = taps_ref[0, rows, :]
        values = query_ref[rows, :].astype(jnp.float32)
        history = pltpu.roll(edge, LANES - LANE_Q - (share + 1) * rim, 1)
        first = taps[:, :1] * values[:, :LANES]
        for shift in range(1, rim + 1):
            joined = jnp.where(lane >= LANES - shift, history, values[:, :LANES])
            first = first + taps[:, shift : shift + 1] * pltpu.roll(joined, shift, 1)
        out_ref[mask] = rolled_taps(values, taps)
        out_ref[mask, :, :LANES] = first


def query_features(query, short_taps, pieces, nodes, chans):
    near = pl.BlockSpec(memory_space=pltpu.VMEM)
    return pl.pallas_call(
        lambda *refs: query_kernel(nodes, *refs),
        out_shape=jax.ShapeDtypeStruct((nodes, chans, query.shape[1]), jnp.float32),
        in_specs=[near] * (2 + nodes),
        out_specs=near,
        compiler_params=pltpu.CompilerParams(vmem_limit_bytes=16 << 20),
        name="query_features",
    )(query, short_taps, *pieces)


def long_kernel(
    nodes, chans, per_node, repair, taps_ref, first_ref, twist_ref, second_ref, last_ref, skip_ref, *refs
):
    pieces = refs[:nodes]
    outs = refs[nodes : 2 * nodes]
    raw, edges, mid, spec, unturned, final = refs[2 * nodes :]
    rows = nodes * per_node
    pitch = rows + PAD
    place = lax.axis_index("ctx")
    base = place * chans
    block = per_node * LANES

    for mask in range(nodes):
        start = (place ^ mask) * per_node
        for part in range(2):
            for tile in range(per_node):
                at = part * block + tile * LANES
                raw[part, pl.ds(start + tile, chans, stride=pitch), :] = pieces[mask][
                    :, at : at + LANES
                ].astype(jnp.float32)
        if repair:
            edges[(place ^ mask) + 1] = pieces[mask][:, 2 * block :].astype(jnp.float32)
    if repair:
        rim = taps_ref.shape[2] - 1
        lane = lax.broadcasted_iota(jnp.int32, (chans, LANES), 1)
        own = pl.ds(pl.multiple_of(base, chans), chans)
        edges[0] = jnp.zeros((chans, LANES), jnp.float32)
        for node in range(nodes):
            before, now = edges[node], edges[node + 1]
            product = None
            for stream in range(2):
                back = (LANES - stream * LANE_V) % LANES
                joined = jnp.where(lane < stream * LANE_V + rim, before, now)
                if back:
                    joined = pltpu.roll(joined, back, 1)
                featured = rolled_taps(joined, taps_ref[1 + stream, own, :])
                product = featured if product is None else product * featured
            product = pltpu.roll(product, LANES - rim, 1).astype(jnp.bfloat16).astype(jnp.float32)
            spot = pl.ds(node * per_node, chans, stride=pitch)
            raw[0, spot, :] = jnp.where(lane < rim, product, raw[0, spot, :])

    cos_twist = twist_ref[:, :LANES]
    sin_twist = twist_ref[:, LANES:]
    for chan in range(chans):
        span = slice(chan * pitch, chan * pitch + rows)
        both = jnp.concatenate([raw[0, span, :], raw[1, span, :]], axis=1).astype(jnp.bfloat16)
        section = dot(first_ref[...], jnp.concatenate([both, both], axis=0))
        for part in range(2):
            real = section[:rows, part * LANES : (part + 1) * LANES]
            imag = section[rows:, part * LANES : (part + 1) * LANES]
            turned = jnp.concatenate(
                [
                    real * cos_twist + imag * sin_twist,
                    imag * cos_twist - real * sin_twist,
                ],
                axis=1,
            )
            high, low = halves(turned)
            at = (part * chans + chan) * rows
            mid[0, at : at + rows, :] = high
            mid[1, at : at + rows, :] = low

    def inner(high, low):
        return dot(jnp.concatenate([high, low, high], axis=1), second_ref[...])

    spec[...] = inner(mid[0], mid[1])
    for chan in range(chans):
        sig = spec[chan * rows : (chan + 1) * rows, :]
        fil = spec[(chans + chan) * rows : (chans + chan + 1) * rows, :]
        sig_real, sig_imag = sig[:, :LANES], sig[:, LANES:]
        fil_real, fil_imag = fil[:, :LANES], fil[:, LANES:]
        joined = jnp.concatenate(
            [
                sig_real * fil_real - sig_imag * fil_imag,
                -(sig_real * fil_imag + sig_imag * fil_real),
            ],
            axis=1,
        )
        high, low = halves(joined)
        mid[0, chan * rows : (chan + 1) * rows, :] = high
        mid[1, chan * rows : (chan + 1) * rows, :] = low
    skips = skip_ref[pl.ds(pl.multiple_of(base, chans), chans), :]
    half = chans * rows
    unturned[...] = inner(mid[0, :half, :], mid[1, :half, :])
    for chan in range(chans):
        back = unturned[chan * rows : (chan + 1) * rows, :]
        real, imag = back[:, :LANES], back[:, LANES:]
        turned = jnp.concatenate(
            [real * cos_twist + imag * sin_twist, imag * cos_twist - real * sin_twist], axis=0
        )
        high, low = halves(turned)
        convolved = dot(last_ref[...], jnp.concatenate([high, low, high], axis=0))
        product = raw[0, chan * pitch : chan * pitch + rows, :]
        final[chan * pitch : chan * pitch + rows, :] = convolved + skips[chan : chan + 1, :1] * product
    for mask in range(nodes):
        start = (place ^ mask) * per_node
        for tile in range(per_node):
            outs[mask][:, tile * LANES : (tile + 1) * LANES] = final[
                pl.ds(start + tile, chans, stride=pitch), :
            ].astype(jnp.bfloat16)


def long_mix(pieces, taps, tables, block):
    nodes = len(pieces)
    chans, width = pieces[0].shape
    per_node = block // LANES
    rows = nodes * per_node
    near = pl.BlockSpec(memory_space=pltpu.VMEM)
    return pl.pallas_call(
        lambda *refs: long_kernel(nodes, chans, per_node, width > 2 * block, *refs),
        out_shape=[jax.ShapeDtypeStruct((chans, block), jnp.bfloat16)] * nodes,
        in_specs=[near] * (1 + len(tables) + nodes),
        out_specs=[near] * nodes,
        scratch_shapes=[
            pltpu.VMEM((2, chans * (rows + PAD), LANES), jnp.float32),
            pltpu.VMEM((nodes + 1, chans, LANES), jnp.float32),
            pltpu.VMEM((2, 2 * chans * rows, 2 * LANES), jnp.bfloat16),
            pltpu.VMEM((2 * chans * rows, 2 * LANES), jnp.float32),
            pltpu.VMEM((chans * rows, 2 * LANES), jnp.float32),
            pltpu.VMEM((chans * (rows + PAD), LANES), jnp.float32),
        ],
        compiler_params=pltpu.CompilerParams(vmem_limit_bytes=24 << 20),
        name="long_mix",
    )(taps, *tables, *pieces)


def gather_blocks(depths, blocks, gathered):
    place = lax.axis_index("ctx")
    spot = lax.axis_index("ch")
    level, core = spot // 2, spot % 2
    for index, block in enumerate(blocks):
        nodes, chans, _ = block.shape
        side = core ^ (index % 2)
        for mask in range(nodes):
            row = ((2 * (index // 2) + side) * nodes + (place ^ mask)) * chans
            gathered[pl.ds(pl.multiple_of(row, chans), chans), :] = block[mask]
    width = 2 * nodes * chans
    return [pl.ds(pl.multiple_of((level ^ depth) * width, width), width) for depth in depths]


def partial_kernel(depths, rows, weight_ref, *refs):
    blocks = refs[: 2 * len(depths)]
    out_ref, gathered = refs[2 * len(depths) :]
    columns = gather_blocks(depths, blocks, gathered)
    for begin in range(0, out_ref.shape[0], rows):
        weight = jnp.concatenate([weight_ref[begin : begin + rows, at] for at in columns], axis=1)
        out_ref[begin : begin + rows, :] = dot(weight, gathered[...])


def final_kernel(depths, cuts, weight_ref, partial_ref, *refs):
    blocks = refs[: 2 * len(depths)]
    out_ref, gathered, held, sems = refs[2 * len(depths) :]
    columns = gather_blocks(depths, blocks, gathered)
    copies = []
    for part, (begin, end) in enumerate(zip(cuts, cuts[1:])):
        weight = jnp.concatenate([weight_ref[begin:end, at] for at in columns], axis=1)
        total = partial_ref[begin:end, :] + dot(weight, gathered[...])
        held[begin:end, :] = total.astype(jnp.bfloat16)
        rows = pl.ds(begin, end - begin)
        copies.append(
            pltpu.make_async_copy(held.at[rows, :], out_ref.at[rows, :], sems.at[part])
        )
        copies[-1].start()
    for copy in copies:
        copy.wait()


def project_early(early, out_weight):
    features, _ = out_weight.shape
    near = pl.BlockSpec(memory_space=pltpu.VMEM)
    blocks = [block for pair in early.values() for block in pair]
    nodes, chans, block = blocks[0].shape
    depth = nodes * chans * len(blocks)
    cost = pl.CostEstimate(
        flops=0, bytes_accessed=0, transcendentals=0
    )
    return pl.pallas_call(
        lambda *refs: partial_kernel(tuple(early), features // 4, *refs),
        out_shape=jax.ShapeDtypeStruct((features, block), jnp.float32),
        in_specs=[near] * (1 + len(blocks)),
        out_specs=near,
        scratch_shapes=[pltpu.VMEM((depth, block), jnp.bfloat16)],
        compiler_params=pltpu.CompilerParams(vmem_limit_bytes=16 << 20),
        cost_estimate=cost,
        name="project_early",
    )(out_weight, *blocks)


def project_late(partial, late, out_weight):
    features, _ = out_weight.shape
    near = pl.BlockSpec(memory_space=pltpu.VMEM)
    blocks = [block for pair in late.values() for block in pair]
    nodes, chans, block = blocks[0].shape
    depth = nodes * chans * len(blocks)
    cuts = tuple(range(0, features + 1, features // 8))
    return pl.pallas_call(
        lambda *refs: final_kernel(tuple(late), cuts, *refs),
        out_shape=jax.ShapeDtypeStruct((features, block), jnp.bfloat16),
        in_specs=[near] * (2 + len(blocks)),
        out_specs=pl.BlockSpec(memory_space=pl.ANY),
        scratch_shapes=[
            pltpu.VMEM((depth, block), jnp.bfloat16),
            pltpu.VMEM((features, block), jnp.bfloat16),
            pltpu.SemaphoreType.DMA((len(cuts) - 1,)),
        ],
        compiler_params=pltpu.CompilerParams(vmem_limit_bytes=16 << 20),
        name="project_late",
    )(out_weight, partial, *blocks)


def project_plain(blocks, out_weight):
    nodes, chans, block = blocks[0].shape
    stacks = len(blocks) // 2
    place = lax.axis_index("ctx")
    spot = lax.axis_index("ch")
    found = jnp.stack(blocks).reshape(2, stacks, nodes, chans, block)
    index = jnp.arange(2 * stacks, dtype=jnp.int32) ^ spot
    found = found[index % 2, index // 2]
    found = found[:, jnp.arange(nodes, dtype=jnp.int32) ^ place]
    summed = jnp.dot(
        out_weight, found.reshape(-1, block), preferred_element_type=jnp.float32
    )
    return summed.astype(jnp.bfloat16)


def features_plain(qkv, short_taps):
    block = qkv.shape[2]
    tap_count = short_taps.shape[2]
    devices = lax.axis_size("ctx")
    route = [(i, i + 1) for i in range(devices - 1)]
    history = lax.ppermute(qkv[:, :, block - (tap_count - 1) :], "ctx", route)
    extended = jnp.concatenate([history, qkv], axis=2).astype(jnp.float32)
    result = jnp.zeros(qkv.shape, jnp.float32)
    for offset in range(tap_count):
        begin = tap_count - 1 - offset
        result = (
            result
            + short_taps[:, :, offset : offset + 1] * extended[:, :, begin : begin + block]
        )
    return result


def swapped(block, mask, axis):
    if mask == 0:
        return block
    return lax.ppermute(block, axis, [(i, i ^ mask) for i in range(lax.axis_size(axis))])


def local(qkv, short_taps, long_filter, skip_gain, out_weight):
    nodes = lax.axis_size("ctx")
    spread = lax.axis_size("ch")
    stacks = spread // 2
    place = lax.axis_index("ctx")
    _, every, block = qkv.shape
    chans = every // nodes
    fits = chans % 16 == 0

    if fits:
        pieces, query, taps = pack(qkv, long_filter, short_taps, nodes, chans)
    else:
        taps = short_taps
        query, key, value = features_plain(qkv, short_taps)
        both = jnp.concatenate([key * value, long_filter], axis=1).astype(jnp.bfloat16)
        both = both.reshape(nodes, chans, 2 * block)
        pieces = [lax.dynamic_index_in_dim(both, place ^ mask, 0, False) for mask in range(nodes)]
    pieces = [swapped(pieces[mask], mask, "ctx") for mask in range(nodes)]
    out_weight, *tables = near_tables(
        nodes * block // LANES, skip_gain, out_weight, pieces[0]
    )
    mixed = long_mix(pieces, taps, tables, block)

    if fits:
        tied = lax.optimization_barrier((pieces, mixed[0]))[0]
        featured = query_features(query, taps, tied, nodes, chans)
    else:
        featured = query.reshape(nodes, chans, block)[jnp.arange(nodes, dtype=jnp.int32) ^ place]
    mixed = jnp.stack([swapped(mixed[mask], mask, "ctx") for mask in range(nodes)])
    gated = (featured * mixed.astype(jnp.float32)).astype(jnp.bfloat16)

    column = [swapped(gated, 2 * depth, "ch") for depth in range(stacks)]
    if not fits:
        return project_plain(column + [swapped(part, 1, "ch") for part in column], out_weight)
    early = {depth: (column[depth], swapped(column[depth], 1, "ch")) for depth in (0, stacks - 1)}
    partial = project_early(early, out_weight)
    late = {depth: (column[depth], swapped(column[depth], 1, "ch")) for depth in range(1, stacks - 1)}
    return project_late(partial, late, out_weight)


def solution(mesh):
    placed = (P(None, "ch", "ctx"), P(None, "ch", None), P("ch", "ctx"), P("ch"), P("ch", None))
    return jax.shard_map(
        local, mesh=mesh, in_specs=placed, out_specs=P("ch", "ctx"), check_vma=False
    )
```

```python
import math

import numpy as np

import jax
import jax.numpy as jnp
from jax import lax
from jax.experimental import pallas as pl
from jax.experimental.pallas import tpu as pltpu
from jax.sharding import PartitionSpec as P

LANES = 128
PAD = 8
LANE_V = 16
LANE_Q = 32


def split_table(table):
    high = table.astype(jnp.bfloat16)
    low = (table - high.astype(np.float64)).astype(jnp.bfloat16)
    return high, low


def dft_tables(rows):
    total = 2 * rows * LANES
    block = np.arange(rows, dtype=np.float64)
    freq = np.arange(rows, dtype=np.float64) + 0.5
    lane = np.arange(LANES, dtype=np.float64)
    head = 2.0 * math.pi * np.outer(freq, block) / (2 * rows)
    first = np.concatenate(
        split_table(np.concatenate([np.cos(head), -np.sin(head)], axis=0)), axis=1
    )
    turn = 2.0 * math.pi * np.outer(freq, lane) / total
    twist = np.concatenate([np.cos(turn), np.sin(turn)], axis=1).astype(np.float32)
    inner = 2.0 * math.pi * np.outer(lane, lane) / LANES
    square = np.block([[np.cos(inner), -np.sin(inner)], [np.sin(inner), np.cos(inner)]])
    square_high, square_low = split_table(square)
    second = np.concatenate([square_high, square_high, square_low], axis=0)
    tail = head.T
    tail_high, tail_low = split_table(
        (2.0 / total) * np.concatenate([np.cos(tail), np.sin(tail)], axis=1)
    )
    last = np.concatenate([tail_high, tail_high, tail_low], axis=1)
    return first, twist, second, last


def halves(value):
    high = value.astype(jnp.bfloat16)
    low = (value - high.astype(jnp.float32)).astype(jnp.bfloat16)
    return high, low


def dot(left, right):
    return jnp.dot(left, right, preferred_element_type=jnp.float32)


def rolled_taps(values, taps):
    total = taps[:, :1] * values
    for shift in range(1, taps.shape[1]):
        total = total + taps[:, shift : shift + 1] * pltpu.roll(values, shift, 1)
    return total


def in_hbm(*arrays):
    return [pltpu.with_memory_space_constraint(array, pltpu.HBM) for array in arrays]


def tables_kernel(count, *refs):
    sources, skip_ref = refs[:count], refs[count]
    outs, column_ref = refs[count + 2 : 2 * count + 2], refs[2 * count + 2]
    skips, sems = refs[2 * count + 3 :]
    moves = [
        pltpu.make_async_copy(source, out, sems.at[index])
        for index, (source, out) in enumerate(zip(sources, outs))
    ]
    moves.append(pltpu.make_async_copy(skip_ref, skips, sems.at[count]))
    for move in moves:
        move.start()
    moves[count].wait()
    column_ref[...] = jnp.broadcast_to(skips[...].reshape(1, -1), (8, skips.shape[0])).T
    for move in moves[:count]:
        move.wait()


def near_tables(rows, skip_gain, out_weight, after):
    tables = [out_weight] + [jnp.asarray(table) for table in dft_tables(rows)]
    count = len(tables)
    far = pl.BlockSpec(memory_space=pltpu.HBM)
    near = pl.BlockSpec(memory_space=pltpu.VMEM)
    return pl.pallas_call(
        lambda *refs: tables_kernel(count, *refs),
        out_shape=[jax.ShapeDtypeStruct(table.shape, table.dtype) for table in tables]
        + [jax.ShapeDtypeStruct((skip_gain.shape[0], 8), jnp.float32)],
        in_specs=[far] * (count + 1) + [near],
        out_specs=[near] * (count + 1),
        scratch_shapes=[
            pltpu.VMEM(skip_gain.shape, jnp.float32),
            pltpu.SemaphoreType.DMA((count + 1,)),
        ],
        compiler_params=pltpu.CompilerParams(vmem_limit_bytes=16 << 20),
        name="near_tables",
    )(*in_hbm(*tables, skip_gain), after)


def pack_kernel(nodes, chans, qkv_ref, filter_ref, flat_ref, *refs):
    outs = refs[:nodes]
    query_ref, taps_ref = refs[nodes : nodes + 2]
    filters, streams, flat, sems = refs[nodes + 2 :]
    place = lax.axis_index("ctx")
    block = qkv_ref.shape[2]
    rim = taps_ref.shape[2] - 1
    moves = [
        pltpu.make_async_copy(flat_ref, flat, sems.at[0]),
        pltpu.make_async_copy(qkv_ref.at[0], query_ref, sems.at[1]),
        pltpu.make_async_copy(filter_ref, filters, sems.at[2]),
    ]
    shares = [
        pl.ds(pl.multiple_of((place ^ mask) * chans, chans), chans)
        for mask in reversed(range(nodes))
    ]
    arrivals = [
        pltpu.make_async_copy(
            qkv_ref.at[pl.ds(1, 2), rows, :], streams.at[:, rows, :], sems.at[3 + index]
        )
        for index, rows in enumerate(shares)
    ]
    for move in moves[:1] + arrivals + moves[1:]:
        move.start()
    lane = lax.broadcasted_iota(jnp.int32, (chans, LANES), 1)

    def place_at(tile, source, target, size, under):
        moved = pltpu.roll(tile, (target - source) % LANES, 1)
        return jnp.where((lane >= target) & (lane < target + size), moved, under)

    moves[0].wait()
    for stream in range(3):
        taps_ref[stream] = flat[stream].T
    for index, rows in enumerate(shares):
        mask = nodes - 1 - index
        arrivals[index].wait()
        edge = jnp.zeros((chans, LANES), jnp.float32)
        product = None
        for stream in range(2):
            values = streams[stream, rows, :].astype(jnp.float32)
            at = stream * LANE_V
            edge = place_at(values[:, block - LANES :], LANES - rim, at, rim, edge)
            edge = place_at(values[:, :LANES], 0, at + rim, rim, edge)
            featured = rolled_taps(values, taps_ref[1 + stream, rows, :])
            product = featured if product is None else product * featured
        outs[mask][:, :block] = product.astype(jnp.bfloat16)
        outs[mask][:, 2 * block :] = edge.astype(jnp.bfloat16)
    moves[1].wait()
    queries = jnp.zeros((chans, LANES), jnp.float32)
    for share in range(nodes):
        tile = query_ref[share * chans : (share + 1) * chans, block - LANES :]
        queries = place_at(
            tile.astype(jnp.float32), LANES - rim, LANE_Q + share * rim, rim, queries
        )
    for mask in range(nodes):
        edge = outs[mask][:, 2 * block :].astype(jnp.float32)
        outs[mask][:, 2 * block :] = jnp.where(lane >= LANE_Q, queries, edge).astype(jnp.bfloat16)
    moves[2].wait()
    for index, rows in enumerate(shares):
        mask = nodes - 1 - index
        outs[mask][:, block : 2 * block] = filters[rows, :].astype(jnp.bfloat16)


def pack(qkv, long_filter, short_taps, nodes, chans):
    _, every, block = qkv.shape
    far = pl.BlockSpec(memory_space=pltpu.HBM)
    near = pl.BlockSpec(memory_space=pltpu.VMEM)
    flat = jnp.swapaxes(short_taps, 1, 2)
    *pieces, query, taps = pl.pallas_call(
        lambda *refs: pack_kernel(nodes, chans, *refs),
        out_shape=[jax.ShapeDtypeStruct((chans, 2 * block + LANES), jnp.bfloat16)] * nodes
        + [
            jax.ShapeDtypeStruct((every, block), jnp.bfloat16),
            jax.ShapeDtypeStruct(short_taps.shape, jnp.float32),
        ],
        in_specs=[far] * 3,
        out_specs=[near] * (nodes + 2),
        scratch_shapes=[
            pltpu.VMEM((every, block), jnp.float32),
            pltpu.VMEM((2, every, block), jnp.bfloat16),
            pltpu.VMEM(flat.shape, jnp.float32),
            pltpu.SemaphoreType.DMA((3 + nodes,)),
        ],
        compiler_params=pltpu.CompilerParams(vmem_limit_bytes=16 << 20),
        name="pack",
    )(*in_hbm(qkv, long_filter, flat))
    return pieces, query, taps


def query_kernel(nodes, query_ref, taps_ref, *refs):
    pieces = refs[:nodes]
    out_ref = refs[nodes]
    place = lax.axis_index("ctx")
    _, chans, block = out_ref.shape
    rim = taps_ref.shape[2] - 1
    lane = lax.broadcasted_iota(jnp.int32, (chans, LANES), 1)
    edge = jnp.zeros((chans, LANES), jnp.float32)
    for mask in range(1, nodes):
        before = (place ^ mask) == place - 1
        found = pieces[mask][:, pieces[mask].shape[1] - LANES :].astype(jnp.float32)
        edge = jnp.where(before, found, edge)
    for mask in range(nodes):
        share = place ^ mask
        rows = pl.ds(pl.multiple_of(share * chans, chans), chans)
        taps = taps_ref[0, rows, :]
        values = query_ref[rows, :].astype(jnp.float32)
        history = pltpu.roll(edge, LANES - LANE_Q - (share + 1) * rim, 1)
        first = taps[:, :1] * values[:, :LANES]
        for shift in range(1, rim + 1):
            joined = jnp.where(lane >= LANES - shift, history, values[:, :LANES])
            first = first + taps[:, shift : shift + 1] * pltpu.roll(joined, shift, 1)
        out_ref[nodes - 1 - mask] = rolled_taps(values, taps)
        out_ref[nodes - 1 - mask, :, :LANES] = first


def query_features(query, short_taps, pieces, nodes, chans):
    near = pl.BlockSpec(memory_space=pltpu.VMEM)
    return pl.pallas_call(
        lambda *refs: query_kernel(nodes, *refs),
        out_shape=jax.ShapeDtypeStruct((nodes, chans, query.shape[1]), jnp.float32),
        in_specs=[near] * (2 + nodes),
        out_specs=near,
        compiler_params=pltpu.CompilerParams(vmem_limit_bytes=16 << 20),
        name="query_features",
    )(query, short_taps, *pieces)


def long_kernel(
    nodes, chans, per_node, rim, taps_ref, first_ref, twist_ref, second_ref, last_ref, skip_ref, *refs
):
    pieces = refs[:nodes][::-1]
    outs = refs[nodes : 2 * nodes]
    raw, edges, final = refs[2 * nodes :]
    rows = nodes * per_node
    pitch = rows + PAD
    place = lax.axis_index("ctx")
    base = place * chans
    block = per_node * LANES

    if rim:
        lane = lax.broadcasted_iota(jnp.int32, (chans, LANES), 1)
        own = pl.ds(pl.multiple_of(base, chans), chans)
        edges[0] = jnp.zeros((chans, LANES), jnp.float32)
        for mask in range(nodes):
            edges[(place ^ mask) + 1] = pieces[mask][:, 2 * block :].astype(jnp.float32)

    def repaired(mask, tile):
        before, now = edges[place ^ mask], pieces[mask][:, 2 * block :].astype(jnp.float32)
        product = None
        for stream in range(2):
            back = (LANES - stream * LANE_V) % LANES
            joined = jnp.where(lane < stream * LANE_V + rim, before, now)
            if back:
                joined = pltpu.roll(joined, back, 1)
            featured = rolled_taps(joined, taps_ref[1 + stream, own, :])
            product = featured if product is None else product * featured
        product = pltpu.roll(product, LANES - rim, 1).astype(jnp.bfloat16).astype(jnp.float32)
        return jnp.where(lane < rim, product, tile)

    for part in reversed(range(2)):
        for mask in range(nodes):
            start = (place ^ mask) * per_node
            for tile in range(per_node):
                at = part * block + tile * LANES
                values = pieces[mask][:, at : at + LANES].astype(jnp.float32)
                if rim and at == 0:
                    values = repaired(mask, values)
                raw[part, pl.ds(start + tile, chans, stride=pitch), :] = values

    cos_twist = twist_ref[:, :LANES]
    sin_twist = twist_ref[:, LANES:]
    skips = skip_ref[pl.ds(pl.multiple_of(base, chans), chans), :]

    def inner(parts):
        high, low = halves(jnp.concatenate(parts, axis=0))
        return dot(jnp.concatenate([high, low, high], axis=1), second_ref[...])

    def turn(real, imag, axis):
        return jnp.concatenate(
            [real * cos_twist + imag * sin_twist, imag * cos_twist - real * sin_twist], axis=axis
        )

    spectra = [[], []]
    for chan in range(chans):
        span = slice(chan * pitch, chan * pitch + rows)
        both = jnp.concatenate([raw[0, span, :], raw[1, span, :]], axis=1).astype(jnp.bfloat16)
        section = dot(first_ref[...], jnp.concatenate([both, both], axis=0))
        for part in range(2):
            cols = slice(part * LANES, (part + 1) * LANES)
            spectra[part].append(turn(section[:rows, cols], section[rows:, cols], 1))
    spectra = spectra[0] + spectra[1]
    spec = inner(spectra)
    joined = []
    for chan in range(chans):
        sig = spec[chan * rows : (chan + 1) * rows, :]
        fil = spec[(chans + chan) * rows : (chans + chan + 1) * rows, :]
        sig_real, sig_imag = sig[:, :LANES], sig[:, LANES:]
        fil_real, fil_imag = fil[:, :LANES], fil[:, LANES:]
        joined.append(
            jnp.concatenate(
                [
                    sig_real * fil_real - sig_imag * fil_imag,
                    -(sig_real * fil_imag + sig_imag * fil_real),
                ],
                axis=1,
            )
        )
    back = inner(joined)
    turned = []
    for chan in range(chans):
        real = back[chan * rows : (chan + 1) * rows, :LANES]
        imag = back[chan * rows : (chan + 1) * rows, LANES:]
        turned.append(turn(real, imag, 0))
    high, low = halves(jnp.concatenate(turned, axis=1))
    convolved = dot(last_ref[...], jnp.concatenate([high, low, high], axis=0))
    for chan in range(chans):
        span = slice(chan * pitch, chan * pitch + rows)
        final[span, :] = (
            convolved[:, chan * LANES : (chan + 1) * LANES]
            + skips[chan : chan + 1, :1] * raw[0, span, :]
        )
    for mask in range(nodes):
        start = (place ^ mask) * per_node
        for tile in range(per_node):
            outs[mask][:, tile * LANES : (tile + 1) * LANES] = final[
                pl.ds(start + tile, chans, stride=pitch), :
            ].astype(jnp.bfloat16)


def long_mix(pieces, taps, tables, block):
    nodes = len(pieces)
    chans, width = pieces[0].shape
    per_node = block // LANES
    rows = nodes * per_node
    rim = taps.shape[2] - 1 if width > 2 * block else 0
    near = pl.BlockSpec(memory_space=pltpu.VMEM)
    return pl.pallas_call(
        lambda *refs: long_kernel(nodes, chans, per_node, rim, *refs),
        out_shape=[jax.ShapeDtypeStruct((chans, block), jnp.bfloat16)] * nodes,
        in_specs=[near] * (1 + len(tables) + nodes),
        out_specs=[near] * nodes,
        scratch_shapes=[
            pltpu.VMEM((2, chans * (rows + PAD), LANES), jnp.float32),
            pltpu.VMEM((nodes + 1, chans, LANES), jnp.float32),
            pltpu.VMEM((chans * (rows + PAD), LANES), jnp.float32),
        ],
        compiler_params=pltpu.CompilerParams(vmem_limit_bytes=24 << 20),
        name="long_mix",
    )(taps, *tables, *pieces[::-1])


def gather_blocks(depths, blocks, gathered):
    place = lax.axis_index("ctx")
    spot = lax.axis_index("ch")
    level, core = spot // 2, spot % 2
    for index, block in enumerate(blocks):
        nodes, chans, _ = block.shape
        side = core ^ (index % 2)
        for mask in range(nodes):
            row = ((2 * (index // 2) + side) * nodes + (place ^ mask)) * chans
            gathered[pl.ds(pl.multiple_of(row, chans), chans), :] = block[nodes - 1 - mask]
    width = 2 * nodes * chans
    return [pl.ds(pl.multiple_of((level ^ depth) * width, width), width) for depth in depths]


def partial_kernel(depths, rows, weight_ref, *refs):
    blocks = refs[: 2 * len(depths)]
    out_ref, gathered = refs[2 * len(depths) :]
    columns = gather_blocks(depths, blocks, gathered)
    for begin in range(0, out_ref.shape[0], rows):
        weight = jnp.concatenate([weight_ref[begin : begin + rows, at] for at in columns], axis=1)
        out_ref[begin : begin + rows, :] = dot(weight, gathered[...])


def final_kernel(depths, cuts, weight_ref, partial_ref, *refs):
    blocks = refs[: 2 * len(depths)]
    out_ref, gathered, held, sems = refs[2 * len(depths) :]
    columns = gather_blocks(depths, blocks, gathered)
    copies = []
    for part, (begin, end) in enumerate(zip(cuts, cuts[1:])):
        weight = jnp.concatenate([weight_ref[begin:end, at] for at in columns], axis=1)
        total = partial_ref[begin:end, :] + dot(weight, gathered[...])
        held[begin:end, :] = total.astype(jnp.bfloat16)
        rows = pl.ds(begin, end - begin)
        copies.append(
            pltpu.make_async_copy(held.at[rows, :], out_ref.at[rows, :], sems.at[part])
        )
        copies[-1].start()
    for copy in copies:
        copy.wait()


def project_early(early, out_weight):
    features, _ = out_weight.shape
    near = pl.BlockSpec(memory_space=pltpu.VMEM)
    blocks = [block for pair in early.values() for block in pair]
    nodes, chans, block = blocks[0].shape
    depth = nodes * chans * len(blocks)
    cost = pl.CostEstimate(
        flops=0, bytes_accessed=0, transcendentals=0
    )
    return pl.pallas_call(
        lambda *refs: partial_kernel(tuple(early), features // 4, *refs),
        out_shape=jax.ShapeDtypeStruct((features, block), jnp.float32),
        in_specs=[near] * (1 + len(blocks)),
        out_specs=near,
        scratch_shapes=[pltpu.VMEM((depth, block), jnp.bfloat16)],
        compiler_params=pltpu.CompilerParams(vmem_limit_bytes=16 << 20),
        cost_estimate=cost,
        name="project_early",
    )(out_weight, *blocks)


def project_late(partial, late, out_weight):
    features, _ = out_weight.shape
    near = pl.BlockSpec(memory_space=pltpu.VMEM)
    blocks = [block for pair in late.values() for block in pair]
    nodes, chans, block = blocks[0].shape
    depth = nodes * chans * len(blocks)
    cuts = tuple(range(0, features + 1, features // 8))
    return pl.pallas_call(
        lambda *refs: final_kernel(tuple(late), cuts, *refs),
        out_shape=jax.ShapeDtypeStruct((features, block), jnp.bfloat16),
        in_specs=[near] * (2 + len(blocks)),
        out_specs=pl.BlockSpec(memory_space=pl.ANY),
        scratch_shapes=[
            pltpu.VMEM((depth, block), jnp.bfloat16),
            pltpu.VMEM((features, block), jnp.bfloat16),
            pltpu.SemaphoreType.DMA((len(cuts) - 1,)),
        ],
        compiler_params=pltpu.CompilerParams(vmem_limit_bytes=16 << 20),
        name="project_late",
    )(out_weight, partial, *blocks)


def project_plain(blocks, out_weight):
    nodes, chans, block = blocks[0].shape
    stacks = len(blocks) // 2
    place = lax.axis_index("ctx")
    spot = lax.axis_index("ch")
    found = jnp.stack(blocks).reshape(2, stacks, nodes, chans, block)
    index = jnp.arange(2 * stacks, dtype=jnp.int32) ^ spot
    found = found[index % 2, index // 2]
    found = found[:, nodes - 1 - (jnp.arange(nodes, dtype=jnp.int32) ^ place)]
    summed = jnp.dot(
        out_weight, found.reshape(-1, block), preferred_element_type=jnp.float32
    )
    return summed.astype(jnp.bfloat16)


def features_plain(qkv, short_taps):
    block = qkv.shape[2]
    tap_count = short_taps.shape[2]
    devices = lax.axis_size("ctx")
    route = [(i, i + 1) for i in range(devices - 1)]
    history = lax.ppermute(qkv[:, :, block - (tap_count - 1) :], "ctx", route)
    extended = jnp.concatenate([history, qkv], axis=2).astype(jnp.float32)
    result = jnp.zeros(qkv.shape, jnp.float32)
    for offset in range(tap_count):
        begin = tap_count - 1 - offset
        result = (
            result
            + short_taps[:, :, offset : offset + 1] * extended[:, :, begin : begin + block]
        )
    return result


def swapped(block, mask, axis):
    if mask == 0:
        return block
    return lax.ppermute(block, axis, [(i, i ^ mask) for i in range(lax.axis_size(axis))])


def local(qkv, short_taps, long_filter, skip_gain, out_weight):
    nodes = lax.axis_size("ctx")
    spread = lax.axis_size("ch")
    stacks = spread // 2
    place = lax.axis_index("ctx")
    _, every, block = qkv.shape
    chans = every // nodes
    fits = chans % 16 == 0

    if fits:
        pieces, query, taps = pack(qkv, long_filter, short_taps, nodes, chans)
    else:
        taps = short_taps
        query, key, value = features_plain(qkv, short_taps)
        both = jnp.concatenate([key * value, long_filter], axis=1).astype(jnp.bfloat16)
        both = both.reshape(nodes, chans, 2 * block)
        pieces = [lax.dynamic_index_in_dim(both, place ^ mask, 0, False) for mask in range(nodes)]
    pieces = [swapped(pieces[mask], mask, "ctx") for mask in range(nodes)]
    out_weight, *tables = near_tables(
        nodes * block // LANES, skip_gain, out_weight, pieces[0]
    )
    mixed = long_mix(pieces, taps, tables, block)

    if fits:
        tied = lax.optimization_barrier((mixed[0], *pieces[::-1]))[:0:-1]
        featured = query_features(query, taps, tied, nodes, chans)
    else:
        featured = query.reshape(nodes, chans, block)[jnp.arange(nodes, dtype=jnp.int32) ^ place][::-1]
    mixed = [swapped(mixed[mask], mask, "ctx") for mask in range(nodes)]
    mixed = jnp.stack(mixed[::-1])
    gated = (featured * mixed.astype(jnp.float32)).astype(jnp.bfloat16)

    column = [swapped(gated, 2 * depth, "ch") for depth in range(stacks)]
    if not fits:
        return project_plain(column + [swapped(part, 1, "ch") for part in column], out_weight)
    pairs = {depth: (part, swapped(part, 1, "ch")) for depth, part in enumerate(column)}
    late = {depth: pairs.pop(depth) for depth in (3, 1)}
    return project_late(project_early(pairs, out_weight), late, out_weight)


def solution(mesh):
    placed = (P(None, "ch", "ctx"), P(None, "ch", None), P("ch", "ctx"), P("ch"), P("ch", None))
    return jax.shard_map(
        local, mesh=mesh, in_specs=placed, out_specs=P("ch", "ctx"), check_vma=False
    )
```

```python
import math

import numpy as np

import jax
import jax.numpy as jnp
from jax import lax
from jax.experimental import pallas as pl
from jax.experimental.pallas import tpu as pltpu
from jax.sharding import PartitionSpec as P

LANES = 128
PAD = 8
LANE_V = 16
LANE_Q = 32


def split_table(table):
    high = table.astype(jnp.bfloat16)
    low = (table - high.astype(np.float64)).astype(jnp.bfloat16)
    return high, low


def dft_tables(rows):
    total = 2 * rows * LANES
    block = np.arange(rows, dtype=np.float64)
    freq = np.arange(rows, dtype=np.float64) + 0.5
    lane = np.arange(LANES, dtype=np.float64)
    head = 2.0 * math.pi * np.outer(freq, block) / (2 * rows)
    first = np.concatenate(
        split_table(np.concatenate([np.cos(head), -np.sin(head)], axis=0)), axis=1
    )
    turn = 2.0 * math.pi * np.outer(freq, lane) / total
    twist = np.concatenate([np.cos(turn), np.sin(turn)], axis=1).astype(np.float32)
    inner = 2.0 * math.pi * np.outer(lane, lane) / LANES
    square = np.block([[np.cos(inner), -np.sin(inner)], [np.sin(inner), np.cos(inner)]])
    square_high, square_low = split_table(square)
    second = np.concatenate([square_high, square_high, square_low], axis=0)
    tail = head.T
    tail_high, tail_low = split_table(
        (2.0 / total) * np.concatenate([np.cos(tail), np.sin(tail)], axis=1)
    )
    last = np.concatenate([tail_high, tail_high, tail_low], axis=1)
    return first, twist, second, last


def halves(value):
    high = value.astype(jnp.bfloat16)
    low = (value - high.astype(jnp.float32)).astype(jnp.bfloat16)
    return high, low


def dot(left, right):
    return jnp.dot(left, right, preferred_element_type=jnp.float32)


def rolled_taps(values, taps):
    total = taps[:, :1] * values
    for shift in range(1, taps.shape[1]):
        total = total + taps[:, shift : shift + 1] * pltpu.roll(values, shift, 1)
    return total


def in_hbm(*arrays):
    return [pltpu.with_memory_space_constraint(array, pltpu.HBM) for array in arrays]


def tables_kernel(count, *refs):
    sources, skip_ref = refs[:count], refs[count]
    outs, column_ref = refs[count + 2 : 2 * count + 2], refs[2 * count + 2]
    skips, sems = refs[2 * count + 3 :]
    moves = [
        pltpu.make_async_copy(source, out, sems.at[index])
        for index, (source, out) in enumerate(zip(sources, outs))
    ]
    moves.append(pltpu.make_async_copy(skip_ref, skips, sems.at[count]))
    for move in moves:
        move.start()
    moves[count].wait()
    column_ref[...] = jnp.broadcast_to(skips[...].reshape(1, -1), (8, skips.shape[0])).T
    for move in moves[:count]:
        move.wait()


def near_tables(rows, skip_gain, out_weight, after):
    tables = [out_weight] + [jnp.asarray(table) for table in dft_tables(rows)]
    count = len(tables)
    far = pl.BlockSpec(memory_space=pltpu.HBM)
    near = pl.BlockSpec(memory_space=pltpu.VMEM)
    return pl.pallas_call(
        lambda *refs: tables_kernel(count, *refs),
        out_shape=[jax.ShapeDtypeStruct(table.shape, table.dtype) for table in tables]
        + [jax.ShapeDtypeStruct((skip_gain.shape[0], 8), jnp.float32)],
        in_specs=[far] * (count + 1) + [near],
        out_specs=[near] * (count + 1),
        scratch_shapes=[
            pltpu.VMEM(skip_gain.shape, jnp.float32),
            pltpu.SemaphoreType.DMA((count + 1,)),
        ],
        compiler_params=pltpu.CompilerParams(vmem_limit_bytes=16 << 20),
        name="near_tables",
    )(*in_hbm(*tables, skip_gain), after)


def pack_kernel(nodes, chans, qkv_ref, filter_ref, flat_ref, *refs):
    outs = refs[:nodes]
    query_ref, taps_ref = refs[nodes : nodes + 2]
    filters, streams, flat, sems = refs[nodes + 2 :]
    place = lax.axis_index("ctx")
    block = qkv_ref.shape[2]
    rim = taps_ref.shape[2] - 1
    shares = [
        pl.ds(pl.multiple_of((place ^ mask) * chans, chans), chans) for mask in range(nodes)
    ]
    flat_move = pltpu.make_async_copy(flat_ref, flat, sems.at[0])
    query_move = pltpu.make_async_copy(qkv_ref.at[0], query_ref, sems.at[1])
    filter_move = pltpu.make_async_copy(filter_ref, filters, sems.at[2])
    stream_move = pltpu.make_async_copy(qkv_ref.at[pl.ds(1, 2)], streams, sems.at[3])
    for move in (flat_move, stream_move, query_move, filter_move):
        move.start()
    lane = lax.broadcasted_iota(jnp.int32, (chans, LANES), 1)

    flat_move.wait()
    for stream in range(3):
        taps_ref[stream] = flat[stream].T
    query_move.wait()
    edges = jnp.zeros((chans, LANES), jnp.float32)
    for share in range(nodes):
        tile = query_ref[share * chans : (share + 1) * chans, block - LANES :]
        moved = pltpu.roll(tile.astype(jnp.float32), LANE_Q + (share + 1) * rim, 1)
        edges = jnp.where(lane >= LANE_Q + share * rim, moved, edges)
    stream_move.wait()
    for mask, rows in reversed(list(enumerate(shares))):
        edge = edges
        features = []
        for stream in reversed(range(2)):
            values = streams[stream, rows, :].astype(jnp.float32)
            ends = jnp.where(lane < rim, values[:, :LANES], values[:, block - LANES :])
            at = stream * LANE_V
            edge = jnp.where(lane < at + LANE_V, pltpu.roll(ends, at + rim, 1), edge)
            taps = taps_ref[1 + stream, rows, :]
            wide = [jnp.broadcast_to(taps[:, tap : tap + 1], (chans, LANES)) for tap in range(rim + 1)]
            raw = streams[stream, rows, :]
            totals = []
            for index in range(block // LANES):
                tile = raw[:, index * LANES : (index + 1) * LANES]
                total = wide[0] * tile.astype(jnp.float32)
                moved = [pltpu.roll(tile, shift, 1) for shift in range(1, rim + 1)]
                if index == 0:
                    before = moved
                for shift in range(1, rim + 1):
                    joined = jnp.where(lane < shift, before[shift - 1].astype(jnp.float32), moved[shift - 1].astype(jnp.float32))
                    total = total + wide[shift] * joined
                before = moved
                totals.append(total)
            features.append(totals)
        for index, (left, right) in enumerate(zip(*features)):
            outs[mask][:, index * LANES : (index + 1) * LANES] = (left * right).astype(jnp.bfloat16)
        outs[mask][:, 2 * block :] = edge.astype(jnp.bfloat16)
    filter_move.wait()
    for mask, rows in enumerate(shares):
        outs[mask][:, block : 2 * block] = filters[rows, :].astype(jnp.bfloat16)


def pack(qkv, long_filter, short_taps, nodes, chans):
    _, every, block = qkv.shape
    far = pl.BlockSpec(memory_space=pltpu.HBM)
    near = pl.BlockSpec(memory_space=pltpu.VMEM)
    flat = jnp.swapaxes(short_taps, 1, 2)
    *pieces, query, taps = pl.pallas_call(
        lambda *refs: pack_kernel(nodes, chans, *refs),
        out_shape=[jax.ShapeDtypeStruct((chans, 2 * block + LANES), jnp.bfloat16)] * nodes
        + [
            jax.ShapeDtypeStruct((every, block), jnp.bfloat16),
            jax.ShapeDtypeStruct(short_taps.shape, jnp.float32),
        ],
        in_specs=[far] * 3,
        out_specs=[near] * (nodes + 2),
        scratch_shapes=[
            pltpu.VMEM((every, block), jnp.float32),
            pltpu.VMEM((2, every, block), jnp.bfloat16),
            pltpu.VMEM(flat.shape, jnp.float32),
            pltpu.SemaphoreType.DMA((4,)),
        ],
        compiler_params=pltpu.CompilerParams(vmem_limit_bytes=16 << 20),
        name="pack",
    )(*in_hbm(qkv, long_filter, flat))
    return pieces, query, taps


def query_kernel(nodes, query_ref, taps_ref, *refs):
    pieces = refs[:nodes]
    out_ref = refs[nodes]
    place = lax.axis_index("ctx")
    _, chans, block = out_ref.shape
    rim = taps_ref.shape[2] - 1
    lane = lax.broadcasted_iota(jnp.int32, (chans, LANES), 1)
    edge = jnp.zeros((chans, LANES), jnp.float32)
    for mask in range(1, nodes):
        before = (place ^ mask) == place - 1
        found = pieces[mask][:, pieces[mask].shape[1] - LANES :].astype(jnp.float32)
        edge = jnp.where(before, found, edge)
    for mask in range(nodes):
        share = place ^ mask
        rows = pl.ds(pl.multiple_of(share * chans, chans), chans)
        taps = taps_ref[0, rows, :]
        values = query_ref[rows, :].astype(jnp.float32)
        history = pltpu.roll(edge, LANES - LANE_Q - (share + 1) * rim, 1)
        first = taps[:, :1] * values[:, :LANES]
        for shift in range(1, rim + 1):
            joined = jnp.where(lane >= LANES - shift, history, values[:, :LANES])
            first = first + taps[:, shift : shift + 1] * pltpu.roll(joined, shift, 1)
        out_ref[nodes - 1 - mask] = rolled_taps(values, taps)
        out_ref[nodes - 1 - mask, :, :LANES] = first


def query_features(query, short_taps, pieces, nodes, chans):
    near = pl.BlockSpec(memory_space=pltpu.VMEM)
    return pl.pallas_call(
        lambda *refs: query_kernel(nodes, *refs),
        out_shape=jax.ShapeDtypeStruct((nodes, chans, query.shape[1]), jnp.float32),
        in_specs=[near] * (2 + nodes),
        out_specs=near,
        compiler_params=pltpu.CompilerParams(vmem_limit_bytes=16 << 20),
        name="query_features",
    )(query, short_taps, *pieces)


def long_kernel(
    nodes, chans, per_node, rim, taps_ref, first_ref, twist_ref, second_ref, last_ref, skip_ref, *refs
):
    pieces = refs[:nodes][::-1]
    outs = refs[nodes : 2 * nodes]
    raw, edges, final = refs[2 * nodes :]
    rows = nodes * per_node
    pitch = rows + PAD
    place = lax.axis_index("ctx")
    base = place * chans
    block = per_node * LANES

    if rim:
        lane = lax.broadcasted_iota(jnp.int32, (chans, LANES), 1)
        own = pl.ds(pl.multiple_of(base, chans), chans)
        edges[0] = jnp.zeros((chans, LANES), jnp.float32)
        for mask in range(nodes):
            edges[(place ^ mask) + 1] = pieces[mask][:, 2 * block :].astype(jnp.float32)

    def repaired(mask, tile):
        before, now = edges[place ^ mask], pieces[mask][:, 2 * block :].astype(jnp.float32)
        product = None
        for stream in range(2):
            back = (LANES - stream * LANE_V) % LANES
            joined = jnp.where(lane < stream * LANE_V + rim, before, now)
            if back:
                joined = pltpu.roll(joined, back, 1)
            featured = rolled_taps(joined, taps_ref[1 + stream, own, :])
            product = featured if product is None else product * featured
        product = pltpu.roll(product, LANES - rim, 1).astype(jnp.bfloat16).astype(jnp.float32)
        return jnp.where(lane < rim, product, tile)

    for part in reversed(range(2)):
        for mask in range(nodes):
            start = (place ^ mask) * per_node
            for tile in range(per_node):
                at = part * block + tile * LANES
                values = pieces[mask][:, at : at + LANES].astype(jnp.float32)
                if rim and at == 0:
                    values = repaired(mask, values)
                raw[part, pl.ds(start + tile, chans, stride=pitch), :] = values

    cos_twist = twist_ref[:, :LANES]
    sin_twist = twist_ref[:, LANES:]
    skips = skip_ref[pl.ds(pl.multiple_of(base, chans), chans), :]

    def inner(parts):
        high, low = halves(jnp.concatenate(parts, axis=0))
        return dot(jnp.concatenate([high, low, high], axis=1), second_ref[...])

    def turn(real, imag, axis):
        return jnp.concatenate(
            [real * cos_twist + imag * sin_twist, imag * cos_twist - real * sin_twist], axis=axis
        )

    spectra = [[], []]
    for chan in range(chans):
        span = slice(chan * pitch, chan * pitch + rows)
        both = jnp.concatenate([raw[0, span, :], raw[1, span, :]], axis=1).astype(jnp.bfloat16)
        section = dot(first_ref[...], jnp.concatenate([both, both], axis=0))
        for part in range(2):
            cols = slice(part * LANES, (part + 1) * LANES)
            spectra[part].append(turn(section[:rows, cols], section[rows:, cols], 1))
    spectra = spectra[0] + spectra[1]
    fil_spec = inner(spectra[chans:])
    sig_spec = inner(spectra[:chans])
    def product(chan):
        sig = sig_spec[chan * rows : (chan + 1) * rows, :]
        fil = fil_spec[chan * rows : (chan + 1) * rows, :]
        sig_real, sig_imag = sig[:, :LANES], sig[:, LANES:]
        fil_real, fil_imag = fil[:, :LANES], fil[:, LANES:]
        return jnp.concatenate(
            [
                sig_real * fil_real - sig_imag * fil_imag,
                -(sig_real * fil_imag + sig_imag * fil_real),
            ],
            axis=1,
        )

    group = max(chans // 2, 1)
    groups = [range(begin, begin + group) for begin in range(0, chans, group)]
    turned = []
    for members in groups:
        back = inner([product(chan) for chan in members])
        for index in range(group):
            at = slice(index * rows, (index + 1) * rows)
            turned.append(turn(back[at, :LANES], back[at, LANES:], 0))
    for members in groups:
        high, low = halves(jnp.concatenate([turned[chan] for chan in members], axis=1))
        convolved = dot(last_ref[...], jnp.concatenate([high, low, high], axis=0))
        for index, chan in enumerate(members):
            span = slice(chan * pitch, chan * pitch + rows)
            final[span, :] = (
                convolved[:, index * LANES : (index + 1) * LANES]
                + skips[chan : chan + 1, :1] * raw[0, span, :]
            )
    for mask in range(nodes):
        start = (place ^ mask) * per_node
        for tile in range(per_node):
            outs[mask][:, tile * LANES : (tile + 1) * LANES] = final[
                pl.ds(start + tile, chans, stride=pitch), :
            ].astype(jnp.bfloat16)


def long_mix(pieces, taps, tables, block):
    nodes = len(pieces)
    chans, width = pieces[0].shape
    per_node = block // LANES
    rows = nodes * per_node
    rim = taps.shape[2] - 1 if width > 2 * block else 0
    near = pl.BlockSpec(memory_space=pltpu.VMEM)
    return pl.pallas_call(
        lambda *refs: long_kernel(nodes, chans, per_node, rim, *refs),
        out_shape=[jax.ShapeDtypeStruct((chans, block), jnp.bfloat16)] * nodes,
        in_specs=[near] * (1 + len(tables) + nodes),
        out_specs=[near] * nodes,
        scratch_shapes=[
            pltpu.VMEM((2, chans * (rows + PAD), LANES), jnp.float32),
            pltpu.VMEM((nodes + 1, chans, LANES), jnp.float32),
            pltpu.VMEM((chans * (rows + PAD), LANES), jnp.float32),
        ],
        compiler_params=pltpu.CompilerParams(vmem_limit_bytes=24 << 20),
        name="long_mix",
    )(taps, *tables, *pieces[::-1])


def gather_blocks(depths, blocks, gathered):
    place = lax.axis_index("ctx")
    spot = lax.axis_index("ch")
    level, core = spot // 2, spot % 2
    for index, block in enumerate(blocks):
        nodes, chans, _ = block.shape
        side = core ^ (index % 2)
        for mask in range(nodes):
            row = ((2 * (index // 2) + side) * nodes + (place ^ mask)) * chans
            gathered[pl.ds(pl.multiple_of(row, chans), chans), :] = block[nodes - 1 - mask]
    width = 2 * nodes * chans
    return [pl.ds(pl.multiple_of((level ^ depth) * width, width), width) for depth in depths]


def partial_kernel(depths, rows, weight_ref, *refs):
    blocks = refs[: 2 * len(depths)]
    out_ref, gathered = refs[2 * len(depths) :]
    columns = gather_blocks(depths, blocks, gathered)
    for begin in range(0, out_ref.shape[0], rows):
        weight = jnp.concatenate([weight_ref[begin : begin + rows, at] for at in columns], axis=1)
        out_ref[begin : begin + rows, :] = dot(weight, gathered[...])


def final_kernel(depths, cuts, weight_ref, partial_ref, *refs):
    blocks = refs[: 2 * len(depths)]
    out_ref, gathered, held, sems = refs[2 * len(depths) :]
    columns = gather_blocks(depths, blocks, gathered)
    copies = []
    for part, (begin, end) in enumerate(zip(cuts, cuts[1:])):
        weight = jnp.concatenate([weight_ref[begin:end, at] for at in columns], axis=1)
        total = partial_ref[begin:end, :] + dot(weight, gathered[...])
        held[begin:end, :] = total.astype(jnp.bfloat16)
        rows = pl.ds(begin, end - begin)
        copies.append(
            pltpu.make_async_copy(held.at[rows, :], out_ref.at[rows, :], sems.at[part])
        )
        copies[-1].start()
    for copy in copies:
        copy.wait()


def project_early(early, out_weight):
    features, _ = out_weight.shape
    near = pl.BlockSpec(memory_space=pltpu.VMEM)
    blocks = [block for pair in early.values() for block in pair]
    nodes, chans, block = blocks[0].shape
    depth = nodes * chans * len(blocks)
    cost = pl.CostEstimate(
        flops=0, bytes_accessed=0, transcendentals=0
    )
    return pl.pallas_call(
        lambda *refs: partial_kernel(tuple(early), features // 4, *refs),
        out_shape=jax.ShapeDtypeStruct((features, block), jnp.float32),
        in_specs=[near] * (1 + len(blocks)),
        out_specs=near,
        scratch_shapes=[pltpu.VMEM((depth, block), jnp.bfloat16)],
        compiler_params=pltpu.CompilerParams(vmem_limit_bytes=16 << 20),
        cost_estimate=cost,
        name="project_early",
    )(out_weight, *blocks)


def project_late(partial, late, out_weight):
    features, _ = out_weight.shape
    near = pl.BlockSpec(memory_space=pltpu.VMEM)
    blocks = [block for pair in late.values() for block in pair]
    nodes, chans, block = blocks[0].shape
    depth = nodes * chans * len(blocks)
    cuts = tuple(range(0, features + 1, features // 8))
    return pl.pallas_call(
        lambda *refs: final_kernel(tuple(late), cuts, *refs),
        out_shape=jax.ShapeDtypeStruct((features, block), jnp.bfloat16),
        in_specs=[near] * (2 + len(blocks)),
        out_specs=pl.BlockSpec(memory_space=pl.ANY),
        scratch_shapes=[
            pltpu.VMEM((depth, block), jnp.bfloat16),
            pltpu.VMEM((features, block), jnp.bfloat16),
            pltpu.SemaphoreType.DMA((len(cuts) - 1,)),
        ],
        compiler_params=pltpu.CompilerParams(vmem_limit_bytes=16 << 20),
        name="project_late",
    )(out_weight, partial, *blocks)


def project_plain(blocks, out_weight):
    nodes, chans, block = blocks[0].shape
    stacks = len(blocks) // 2
    place = lax.axis_index("ctx")
    spot = lax.axis_index("ch")
    found = jnp.stack(blocks).reshape(2, stacks, nodes, chans, block)
    index = jnp.arange(2 * stacks, dtype=jnp.int32) ^ spot
    found = found[index % 2, index // 2]
    found = found[:, nodes - 1 - (jnp.arange(nodes, dtype=jnp.int32) ^ place)]
    summed = jnp.dot(
        out_weight, found.reshape(-1, block), preferred_element_type=jnp.float32
    )
    return summed.astype(jnp.bfloat16)


def features_plain(qkv, short_taps):
    block = qkv.shape[2]
    tap_count = short_taps.shape[2]
    devices = lax.axis_size("ctx")
    route = [(i, i + 1) for i in range(devices - 1)]
    history = lax.ppermute(qkv[:, :, block - (tap_count - 1) :], "ctx", route)
    extended = jnp.concatenate([history, qkv], axis=2).astype(jnp.float32)
    result = jnp.zeros(qkv.shape, jnp.float32)
    for offset in range(tap_count):
        begin = tap_count - 1 - offset
        result = (
            result
            + short_taps[:, :, offset : offset + 1] * extended[:, :, begin : begin + block]
        )
    return result


def swapped(block, mask, axis):
    if mask == 0:
        return block
    return lax.ppermute(block, axis, [(i, i ^ mask) for i in range(lax.axis_size(axis))])


def local(qkv, short_taps, long_filter, skip_gain, out_weight):
    nodes = lax.axis_size("ctx")
    spread = lax.axis_size("ch")
    stacks = spread // 2
    place = lax.axis_index("ctx")
    _, every, block = qkv.shape
    chans = every // nodes
    fits = chans % 16 == 0

    if fits:
        pieces, query, taps = pack(qkv, long_filter, short_taps, nodes, chans)
    else:
        taps = short_taps
        query, key, value = features_plain(qkv, short_taps)
        both = jnp.concatenate([key * value, long_filter], axis=1).astype(jnp.bfloat16)
        both = both.reshape(nodes, chans, 2 * block)
        pieces = [lax.dynamic_index_in_dim(both, place ^ mask, 0, False) for mask in range(nodes)]
    pieces = [swapped(pieces[mask], mask, "ctx") for mask in range(nodes)]
    out_weight, *tables = near_tables(
        nodes * block // LANES, skip_gain, out_weight, pieces[0]
    )
    mixed = long_mix(pieces, taps, tables, block)

    if fits:
        tied = lax.optimization_barrier((mixed[0], *pieces[::-1]))[:0:-1]
        featured = query_features(query, taps, tied, nodes, chans)
    else:
        featured = query.reshape(nodes, chans, block)[jnp.arange(nodes, dtype=jnp.int32) ^ place][::-1]
    mixed = [swapped(mixed[mask], mask, "ctx") for mask in range(nodes)]
    mixed = jnp.stack(mixed[::-1])
    gated = (featured * mixed.astype(jnp.float32)).astype(jnp.bfloat16)

    column = [swapped(gated, 2 * depth, "ch") for depth in range(stacks)]
    if not fits:
        return project_plain(column + [swapped(part, 1, "ch") for part in column], out_weight)
    pairs = {depth: (part, swapped(part, 1, "ch")) for depth, part in enumerate(column)}
    late = {depth: pairs.pop(depth) for depth in (3, 1)}
    return project_late(project_early(pairs, out_weight), late, out_weight)


def solution(mesh):
    placed = (P(None, "ch", "ctx"), P(None, "ch", None), P("ch", "ctx"), P("ch"), P("ch", None))
    return jax.shard_map(
        local, mesh=mesh, in_specs=placed, out_specs=P("ch", "ctx"), check_vma=False
    )
```

```python
import math

import numpy as np

import jax
import jax.numpy as jnp
from jax import lax
from jax.experimental import pallas as pl
from jax.experimental.pallas import tpu as pltpu
from jax.sharding import PartitionSpec as P

LANES = 128
PAD = 8
LANE_V = 16
LANE_Q = 32


def split_table(table):
    high = table.astype(jnp.bfloat16)
    low = (table - high.astype(np.float64)).astype(jnp.bfloat16)
    return high, low


def dft_tables(rows):
    total = 2 * rows * LANES
    block = np.arange(rows, dtype=np.float64)
    freq = np.arange(rows, dtype=np.float64) + 0.5
    lane = np.arange(LANES, dtype=np.float64)
    head = 2.0 * math.pi * np.outer(freq, block) / (2 * rows)
    first = np.concatenate(
        split_table(np.concatenate([np.cos(head), -np.sin(head)], axis=0)), axis=1
    )
    turn = 2.0 * math.pi * np.outer(freq, lane) / total
    twist = np.concatenate([np.cos(turn), np.sin(turn)], axis=1).astype(np.float32)
    inner = 2.0 * math.pi * np.outer(lane, lane) / LANES
    square = np.block([[np.cos(inner), -np.sin(inner)], [np.sin(inner), np.cos(inner)]])
    square_high, square_low = split_table(square)
    second = np.concatenate([square_high, square_high, square_low], axis=0)
    tail = head.T
    tail_high, tail_low = split_table(
        (2.0 / total) * np.concatenate([np.cos(tail), np.sin(tail)], axis=1)
    )
    last = np.concatenate([tail_high, tail_high, tail_low], axis=1)
    return first, twist, second, last


def halves(value):
    high = value.astype(jnp.bfloat16)
    low = (value - high.astype(jnp.float32)).astype(jnp.bfloat16)
    return high, low


def dot(left, right):
    return jnp.dot(left, right, preferred_element_type=jnp.float32)


def rolled_taps(values, taps):
    total = taps[:, :1] * values
    for shift in range(1, taps.shape[1]):
        total = total + taps[:, shift : shift + 1] * pltpu.roll(values, shift, 1)
    return total


def in_hbm(*arrays):
    return [pltpu.with_memory_space_constraint(array, pltpu.HBM) for array in arrays]


def tables_kernel(count, *refs):
    sources, skip_ref = refs[:count], refs[count]
    outs, column_ref = refs[count + 2 : 2 * count + 2], refs[2 * count + 2]
    skips, sems = refs[2 * count + 3 :]
    moves = [
        pltpu.make_async_copy(source, out, sems.at[index])
        for index, (source, out) in enumerate(zip(sources, outs))
    ]
    moves.append(pltpu.make_async_copy(skip_ref, skips, sems.at[count]))
    for move in moves:
        move.start()
    moves[count].wait()
    column_ref[...] = jnp.broadcast_to(skips[...].reshape(1, -1), (8, skips.shape[0])).T
    for move in moves[:count]:
        move.wait()


def near_tables(rows, skip_gain, out_weight, after):
    tables = [out_weight] + [jnp.asarray(table) for table in dft_tables(rows)]
    count = len(tables)
    far = pl.BlockSpec(memory_space=pltpu.HBM)
    near = pl.BlockSpec(memory_space=pltpu.VMEM)
    return pl.pallas_call(
        lambda *refs: tables_kernel(count, *refs),
        out_shape=[jax.ShapeDtypeStruct(table.shape, table.dtype) for table in tables]
        + [jax.ShapeDtypeStruct((skip_gain.shape[0], 8), jnp.float32)],
        in_specs=[far] * (count + 1) + [near],
        out_specs=[near] * (count + 1),
        scratch_shapes=[
            pltpu.VMEM(skip_gain.shape, jnp.float32),
            pltpu.SemaphoreType.DMA((count + 1,)),
        ],
        compiler_params=pltpu.CompilerParams(vmem_limit_bytes=16 << 20),
        name="near_tables",
    )(*in_hbm(*tables, skip_gain), after)


def pack_kernel(nodes, chans, qkv_ref, filter_ref, flat_ref, *refs):
    outs = refs[:nodes]
    query_ref, taps_ref = refs[nodes : nodes + 2]
    filters, streams, flat, sems = refs[nodes + 2 :]
    place = lax.axis_index("ctx")
    block = qkv_ref.shape[2]
    rim = taps_ref.shape[2] - 1
    shares = [
        pl.ds(pl.multiple_of((place ^ mask) * chans, chans), chans) for mask in range(nodes)
    ]
    flat_move = pltpu.make_async_copy(flat_ref, flat, sems.at[0])
    query_move = pltpu.make_async_copy(qkv_ref.at[0], query_ref, sems.at[1])
    filter_move = pltpu.make_async_copy(filter_ref, filters, sems.at[2])
    stream_move = pltpu.make_async_copy(qkv_ref.at[pl.ds(1, 2)], streams, sems.at[3])
    for move in (flat_move, stream_move, query_move, filter_move):
        move.start()
    lane = lax.broadcasted_iota(jnp.int32, (chans, LANES), 1)

    flat_move.wait()
    for stream in range(3):
        taps_ref[stream] = flat[stream].T
    query_move.wait()
    edges = jnp.zeros((chans, LANES), jnp.float32)
    for share in range(nodes):
        tile = query_ref[share * chans : (share + 1) * chans, block - LANES :]
        moved = pltpu.roll(tile.astype(jnp.float32), LANE_Q + (share + 1) * rim, 1)
        edges = jnp.where(lane >= LANE_Q + share * rim, moved, edges)
    stream_move.wait()
    for mask, rows in reversed(list(enumerate(shares))):
        edge = edges
        features = []
        for stream in reversed(range(2)):
            values = streams[stream, rows, :].astype(jnp.float32)
            ends = jnp.where(lane < rim, values[:, :LANES], values[:, block - LANES :])
            at = stream * LANE_V
            edge = jnp.where(lane < at + LANE_V, pltpu.roll(ends, at + rim, 1), edge)
            taps = taps_ref[1 + stream, rows, :]
            wide = [
                jnp.broadcast_to(taps[:, tap : tap + 1], (chans, LANES)) for tap in range(rim + 1)
            ]
            raw = streams[stream, rows, :]
            totals = []
            for index in range(block // LANES):
                tile = raw[:, index * LANES : (index + 1) * LANES]
                total = wide[0] * tile.astype(jnp.float32)
                moved = [pltpu.roll(tile, shift, 1) for shift in range(1, rim + 1)]
                if index == 0:
                    before = moved
                for shift in range(1, rim + 1):
                    joined = jnp.where(lane < shift, before[shift - 1], moved[shift - 1])
                    total = total + wide[shift] * joined.astype(jnp.float32)
                before = moved
                totals.append(total)
            features.append(totals)
        for index, (left, right) in enumerate(zip(*features)):
            outs[mask][:, index * LANES : (index + 1) * LANES] = (left * right).astype(jnp.bfloat16)
        outs[mask][:, 2 * block :] = edge.astype(jnp.bfloat16)
    filter_move.wait()
    for mask, rows in enumerate(shares):
        outs[mask][:, block : 2 * block] = filters[rows, :].astype(jnp.bfloat16)


def pack(qkv, long_filter, short_taps, nodes, chans):
    _, every, block = qkv.shape
    far = pl.BlockSpec(memory_space=pltpu.HBM)
    near = pl.BlockSpec(memory_space=pltpu.VMEM)
    flat = jnp.swapaxes(short_taps, 1, 2)
    *pieces, query, taps = pl.pallas_call(
        lambda *refs: pack_kernel(nodes, chans, *refs),
        out_shape=[jax.ShapeDtypeStruct((chans, 2 * block + LANES), jnp.bfloat16)] * nodes
        + [
            jax.ShapeDtypeStruct((every, block), jnp.bfloat16),
            jax.ShapeDtypeStruct(short_taps.shape, jnp.float32),
        ],
        in_specs=[far] * 3,
        out_specs=[near] * (nodes + 2),
        scratch_shapes=[
            pltpu.VMEM((every, block), jnp.float32),
            pltpu.VMEM((2, every, block), jnp.bfloat16),
            pltpu.VMEM(flat.shape, jnp.float32),
            pltpu.SemaphoreType.DMA((4,)),
        ],
        compiler_params=pltpu.CompilerParams(vmem_limit_bytes=16 << 20),
        name="pack",
    )(*in_hbm(qkv, long_filter, flat))
    return pieces, query, taps


def query_kernel(nodes, query_ref, taps_ref, *refs):
    pieces = refs[:nodes]
    out_ref = refs[nodes]
    place = lax.axis_index("ctx")
    _, chans, block = out_ref.shape
    rim = taps_ref.shape[2] - 1
    lane = lax.broadcasted_iota(jnp.int32, (chans, LANES), 1)
    edge = jnp.zeros((chans, LANES), jnp.float32)
    for mask in range(1, nodes):
        before = (place ^ mask) == place - 1
        found = pieces[mask][:, pieces[mask].shape[1] - LANES :].astype(jnp.float32)
        edge = jnp.where(before, found, edge)
    for mask in range(nodes):
        share = place ^ mask
        rows = pl.ds(pl.multiple_of(share * chans, chans), chans)
        taps = taps_ref[0, rows, :]
        values = query_ref[rows, :].astype(jnp.float32)
        history = pltpu.roll(edge, LANES - LANE_Q - (share + 1) * rim, 1)
        first = taps[:, :1] * values[:, :LANES]
        for shift in range(1, rim + 1):
            joined = jnp.where(lane >= LANES - shift, history, values[:, :LANES])
            first = first + taps[:, shift : shift + 1] * pltpu.roll(joined, shift, 1)
        out_ref[nodes - 1 - mask] = rolled_taps(values, taps)
        out_ref[nodes - 1 - mask, :, :LANES] = first


def query_features(query, short_taps, pieces, nodes, chans):
    near = pl.BlockSpec(memory_space=pltpu.VMEM)
    return pl.pallas_call(
        lambda *refs: query_kernel(nodes, *refs),
        out_shape=jax.ShapeDtypeStruct((nodes, chans, query.shape[1]), jnp.float32),
        in_specs=[near] * (2 + nodes),
        out_specs=near,
        compiler_params=pltpu.CompilerParams(vmem_limit_bytes=16 << 20),
        name="query_features",
    )(query, short_taps, *pieces)


def long_kernel(
    nodes, chans, per_node, rim, taps_ref, first_ref, twist_ref, second_ref, last_ref, skip_ref, *refs
):
    pieces = refs[:nodes][::-1]
    outs = refs[nodes : 2 * nodes]
    raw, edges, final = refs[2 * nodes :]
    rows = nodes * per_node
    pitch = rows + PAD
    place = lax.axis_index("ctx")
    base = place * chans
    block = per_node * LANES

    if rim:
        lane = lax.broadcasted_iota(jnp.int32, (chans, LANES), 1)
        own = pl.ds(pl.multiple_of(base, chans), chans)
        edges[0] = jnp.zeros((chans, LANES), jnp.float32)
        for mask in range(nodes):
            edges[(place ^ mask) + 1] = pieces[mask][:, 2 * block :].astype(jnp.float32)

    def repaired(mask, tile):
        before, now = edges[place ^ mask], pieces[mask][:, 2 * block :].astype(jnp.float32)
        product = None
        for stream in range(2):
            back = (LANES - stream * LANE_V) % LANES
            joined = jnp.where(lane < stream * LANE_V + rim, before, now)
            if back:
                joined = pltpu.roll(joined, back, 1)
            featured = rolled_taps(joined, taps_ref[1 + stream, own, :])
            product = featured if product is None else product * featured
        product = pltpu.roll(product, LANES - rim, 1).astype(jnp.bfloat16).astype(jnp.float32)
        return jnp.where(lane < rim, product, tile)

    for part in reversed(range(2)):
        for mask in range(nodes):
            start = (place ^ mask) * per_node
            for tile in range(per_node):
                at = part * block + tile * LANES
                values = pieces[mask][:, at : at + LANES].astype(jnp.float32)
                if rim and at == 0:
                    values = repaired(mask, values)
                raw[part, pl.ds(start + tile, chans, stride=pitch), :] = values

    cos_twist = twist_ref[:, :LANES]
    sin_twist = twist_ref[:, LANES:]
    skips = skip_ref[pl.ds(pl.multiple_of(base, chans), chans), :]

    def inner(parts):
        high, low = halves(jnp.concatenate(parts, axis=0))
        return dot(jnp.concatenate([high, low, high], axis=1), second_ref[...])

    def turn(real, imag, axis):
        return jnp.concatenate(
            [real * cos_twist + imag * sin_twist, imag * cos_twist - real * sin_twist], axis=axis
        )

    spectra = [[], []]
    for chan in range(chans):
        span = slice(chan * pitch, chan * pitch + rows)
        both = jnp.concatenate([raw[0, span, :], raw[1, span, :]], axis=1).astype(jnp.bfloat16)
        section = dot(first_ref[...], jnp.concatenate([both, both], axis=0))
        for part in range(2):
            cols = slice(part * LANES, (part + 1) * LANES)
            spectra[part].append(turn(section[:rows, cols], section[rows:, cols], 1))
    spectra = spectra[0] + spectra[1]
    fil_spec = inner(spectra[chans:])
    sig_spec = inner(spectra[:chans])
    def product(chan):
        sig = sig_spec[chan * rows : (chan + 1) * rows, :]
        fil = fil_spec[chan * rows : (chan + 1) * rows, :]
        sig_real, sig_imag = sig[:, :LANES], sig[:, LANES:]
        fil_real, fil_imag = fil[:, :LANES], fil[:, LANES:]
        return jnp.concatenate(
            [
                sig_real * fil_real - sig_imag * fil_imag,
                -(sig_real * fil_imag + sig_imag * fil_real),
            ],
            axis=1,
        )

    group = max(chans // 2, 1)
    groups = [range(begin, begin + group) for begin in range(0, chans, group)]
    turned = []
    for members in groups:
        back = inner([product(chan) for chan in members])
        for index in range(group):
            at = slice(index * rows, (index + 1) * rows)
            turned.append(turn(back[at, :LANES], back[at, LANES:], 0))
    for members in groups:
        high, low = halves(jnp.concatenate([turned[chan] for chan in members], axis=1))
        convolved = dot(last_ref[...], jnp.concatenate([high, low, high], axis=0))
        for index, chan in enumerate(members):
            span = slice(chan * pitch, chan * pitch + rows)
            final[span, :] = (
                convolved[:, index * LANES : (index + 1) * LANES]
                + skips[chan : chan + 1, :1] * raw[0, span, :]
            )
    for mask in range(nodes):
        start = (place ^ mask) * per_node
        for tile in range(per_node):
            outs[mask][:, tile * LANES : (tile + 1) * LANES] = final[
                pl.ds(start + tile, chans, stride=pitch), :
            ].astype(jnp.bfloat16)


def long_mix(pieces, taps, tables, block):
    nodes = len(pieces)
    chans, width = pieces[0].shape
    per_node = block // LANES
    rows = nodes * per_node
    rim = taps.shape[2] - 1 if width > 2 * block else 0
    near = pl.BlockSpec(memory_space=pltpu.VMEM)
    return pl.pallas_call(
        lambda *refs: long_kernel(nodes, chans, per_node, rim, *refs),
        out_shape=[jax.ShapeDtypeStruct((chans, block), jnp.bfloat16)] * nodes,
        in_specs=[near] * (1 + len(tables) + nodes),
        out_specs=[near] * nodes,
        scratch_shapes=[
            pltpu.VMEM((2, (chans + 1) * (rows + PAD), LANES), jnp.float32),
            pltpu.VMEM((nodes + 1, chans, LANES), jnp.float32),
            pltpu.VMEM(((chans + 1) * (rows + PAD), LANES), jnp.float32),
        ],
        compiler_params=pltpu.CompilerParams(vmem_limit_bytes=24 << 20),
        name="long_mix",
    )(taps, *tables, *pieces[::-1])


def gather_blocks(depths, blocks, gathered):
    place = lax.axis_index("ctx")
    spot = lax.axis_index("ch")
    level, core = spot // 2, spot % 2
    for index, block in enumerate(blocks):
        nodes, chans, _ = block.shape
        side = core ^ (index % 2)
        for mask in range(nodes):
            row = ((2 * (index // 2) + side) * nodes + (place ^ mask)) * chans
            gathered[pl.ds(pl.multiple_of(row, chans), chans), :] = block[nodes - 1 - mask]
    width = 2 * nodes * chans
    return [pl.ds(pl.multiple_of((level ^ depth) * width, width), width) for depth in depths]


def partial_kernel(depths, rows, weight_ref, *refs):
    blocks = refs[: 2 * len(depths)]
    out_ref, gathered = refs[2 * len(depths) :]
    columns = gather_blocks(depths, blocks, gathered)
    for begin in range(0, out_ref.shape[0], rows):
        weight = jnp.concatenate([weight_ref[begin : begin + rows, at] for at in columns], axis=1)
        out_ref[begin : begin + rows, :] = dot(weight, gathered[...])


def final_kernel(depths, cuts, weight_ref, partial_ref, *refs):
    blocks = refs[: 2 * len(depths)]
    out_ref, gathered, held, sems = refs[2 * len(depths) :]
    columns = gather_blocks(depths, blocks, gathered)
    copies = []
    for part, (begin, end) in enumerate(zip(cuts, cuts[1:])):
        weight = jnp.concatenate([weight_ref[begin:end, at] for at in columns], axis=1)
        total = partial_ref[begin:end, :] + dot(weight, gathered[...])
        held[begin:end, :] = total.astype(jnp.bfloat16)
        rows = pl.ds(begin, end - begin)
        copies.append(
            pltpu.make_async_copy(held.at[rows, :], out_ref.at[rows, :], sems.at[part])
        )
        copies[-1].start()
    for copy in copies:
        copy.wait()


def project_early(early, out_weight):
    features, _ = out_weight.shape
    near = pl.BlockSpec(memory_space=pltpu.VMEM)
    blocks = [block for pair in early.values() for block in pair]
    nodes, chans, block = blocks[0].shape
    depth = nodes * chans * len(blocks)
    cost = pl.CostEstimate(
        flops=0, bytes_accessed=0, transcendentals=0
    )
    return pl.pallas_call(
        lambda *refs: partial_kernel(tuple(early), features // 4, *refs),
        out_shape=jax.ShapeDtypeStruct((features, block), jnp.float32),
        in_specs=[near] * (1 + len(blocks)),
        out_specs=near,
        scratch_shapes=[pltpu.VMEM((depth, block), jnp.bfloat16)],
        compiler_params=pltpu.CompilerParams(vmem_limit_bytes=16 << 20),
        cost_estimate=cost,
        name="project_early",
    )(out_weight, *blocks)


def project_late(partial, late, out_weight):
    features, _ = out_weight.shape
    near = pl.BlockSpec(memory_space=pltpu.VMEM)
    blocks = [block for pair in late.values() for block in pair]
    nodes, chans, block = blocks[0].shape
    depth = nodes * chans * len(blocks)
    cuts = tuple(range(0, features + 1, features // 8))
    return pl.pallas_call(
        lambda *refs: final_kernel(tuple(late), cuts, *refs),
        out_shape=jax.ShapeDtypeStruct((features, block), jnp.bfloat16),
        in_specs=[near] * (2 + len(blocks)),
        out_specs=pl.BlockSpec(memory_space=pl.ANY),
        scratch_shapes=[
            pltpu.VMEM((depth, block), jnp.bfloat16),
            pltpu.VMEM((features, block), jnp.bfloat16),
            pltpu.SemaphoreType.DMA((len(cuts) - 1,)),
        ],
        compiler_params=pltpu.CompilerParams(vmem_limit_bytes=16 << 20),
        name="project_late",
    )(out_weight, partial, *blocks)


def project_plain(blocks, out_weight):
    nodes, chans, block = blocks[0].shape
    stacks = len(blocks) // 2
    place = lax.axis_index("ctx")
    spot = lax.axis_index("ch")
    found = jnp.stack(blocks).reshape(2, stacks, nodes, chans, block)
    index = jnp.arange(2 * stacks, dtype=jnp.int32) ^ spot
    found = found[index % 2, index // 2]
    found = found[:, nodes - 1 - (jnp.arange(nodes, dtype=jnp.int32) ^ place)]
    summed = jnp.dot(
        out_weight, found.reshape(-1, block), preferred_element_type=jnp.float32
    )
    return summed.astype(jnp.bfloat16)


def features_plain(qkv, short_taps):
    block = qkv.shape[2]
    tap_count = short_taps.shape[2]
    devices = lax.axis_size("ctx")
    route = [(i, i + 1) for i in range(devices - 1)]
    history = lax.ppermute(qkv[:, :, block - (tap_count - 1) :], "ctx", route)
    extended = jnp.concatenate([history, qkv], axis=2).astype(jnp.float32)
    result = jnp.zeros(qkv.shape, jnp.float32)
    for offset in range(tap_count):
        begin = tap_count - 1 - offset
        result = (
            result
            + short_taps[:, :, offset : offset + 1] * extended[:, :, begin : begin + block]
        )
    return result


def swapped(block, mask, axis):
    if mask == 0:
        return block
    return lax.ppermute(block, axis, [(i, i ^ mask) for i in range(lax.axis_size(axis))])


def local(qkv, short_taps, long_filter, skip_gain, out_weight):
    nodes = lax.axis_size("ctx")
    spread = lax.axis_size("ch")
    stacks = spread // 2
    place = lax.axis_index("ctx")
    _, every, block = qkv.shape
    chans = every // nodes
    fits = chans % 16 == 0

    if fits:
        pieces, query, taps = pack(qkv, long_filter, short_taps, nodes, chans)
    else:
        taps = short_taps
        query, key, value = features_plain(qkv, short_taps)
        both = jnp.concatenate([key * value, long_filter], axis=1).astype(jnp.bfloat16)
        both = both.reshape(nodes, chans, 2 * block)
        pieces = [lax.dynamic_index_in_dim(both, place ^ mask, 0, False) for mask in range(nodes)]
    pieces = [swapped(pieces[mask], mask, "ctx") for mask in range(nodes)]
    out_weight, *tables = near_tables(
        nodes * block // LANES, skip_gain, out_weight, pieces[0]
    )
    mixed = long_mix(pieces, taps, tables, block)

    if fits:
        tied = lax.optimization_barrier((mixed[0], *pieces[::-1]))[:0:-1]
        featured = query_features(query, taps, tied, nodes, chans)
    else:
        featured = query.reshape(nodes, chans, block)[jnp.arange(nodes, dtype=jnp.int32) ^ place][::-1]
    mixed = [swapped(mixed[mask], mask, "ctx") for mask in range(nodes)]
    mixed = jnp.stack(mixed[::-1])
    gated = (featured * mixed.astype(jnp.float32)).astype(jnp.bfloat16)

    column = [swapped(gated, 2 * depth, "ch") for depth in range(stacks)]
    if not fits:
        return project_plain(column + [swapped(part, 1, "ch") for part in column], out_weight)
    pairs = {depth: (part, swapped(part, 1, "ch")) for depth, part in enumerate(column)}
    late = {depth: pairs.pop(depth) for depth in (3, 1)}
    return project_late(project_early(pairs, out_weight), late, out_weight)


def solution(mesh):
    placed = (P(None, "ch", "ctx"), P(None, "ch", None), P("ch", "ctx"), P("ch"), P("ch", None))
    return jax.shard_map(
        local, mesh=mesh, in_specs=placed, out_specs=P("ch", "ctx"), check_vma=False
    )
```

```python
import math

import numpy as np

import jax
import jax.numpy as jnp
from jax import lax
from jax.experimental import pallas as pl
from jax.experimental.pallas import tpu as pltpu
from jax.sharding import PartitionSpec as P

LANES = 128
PAD = 8
LANE_V = 16
LANE_Q = 32


def split_table(table):
    high = table.astype(jnp.bfloat16)
    low = (table - high.astype(np.float64)).astype(jnp.bfloat16)
    return high, low


def dft_tables(rows):
    total = 2 * rows * LANES
    block = np.arange(rows, dtype=np.float64)
    freq = np.arange(rows, dtype=np.float64) + 0.5
    lane = np.arange(LANES, dtype=np.float64)
    head = 2.0 * math.pi * np.outer(freq, block) / (2 * rows)
    first = np.concatenate(
        split_table(np.concatenate([np.cos(head), -np.sin(head)], axis=0)), axis=1
    )
    turn = 2.0 * math.pi * np.outer(freq, lane) / total
    twist = np.concatenate([np.cos(turn), np.sin(turn)], axis=1).astype(np.float32)
    inner = 2.0 * math.pi * np.outer(lane, lane) / LANES
    square = np.block([[np.cos(inner), -np.sin(inner)], [np.sin(inner), np.cos(inner)]])
    square_high, square_low = split_table(square)
    second = np.concatenate([square_high, square_high, square_low], axis=0)
    tail = head.T
    tail_high, tail_low = split_table(
        (2.0 / total) * np.concatenate([np.cos(tail), np.sin(tail)], axis=1)
    )
    last = np.concatenate([tail_high, tail_high, tail_low], axis=1)
    return first, twist, second, last


def halves(value):
    high = value.astype(jnp.bfloat16)
    low = (value - high.astype(jnp.float32)).astype(jnp.bfloat16)
    return high, low


def dot(left, right):
    return jnp.dot(left, right, preferred_element_type=jnp.float32)


def rolled_taps(values, taps):
    total = taps[:, :1] * values
    for shift in range(1, taps.shape[1]):
        total = total + taps[:, shift : shift + 1] * pltpu.roll(values, shift, 1)
    return total


def in_hbm(*arrays):
    return [pltpu.with_memory_space_constraint(array, pltpu.HBM) for array in arrays]


def tables_kernel(count, *refs):
    sources, skip_ref = refs[:count], refs[count]
    outs, column_ref = refs[count + 2 : 2 * count + 2], refs[2 * count + 2]
    skips, sems = refs[2 * count + 3 :]
    moves = [
        pltpu.make_async_copy(source, out, sems.at[index])
        for index, (source, out) in enumerate(zip(sources, outs))
    ]
    moves.append(pltpu.make_async_copy(skip_ref, skips, sems.at[count]))
    for move in moves:
        move.start()
    moves[count].wait()
    column_ref[...] = jnp.broadcast_to(skips[...].reshape(1, -1), (8, skips.shape[0])).T
    for move in moves[:count]:
        move.wait()


def near_tables(rows, skip_gain, out_weight, after):
    tables = [out_weight] + [jnp.asarray(table) for table in dft_tables(rows)]
    count = len(tables)
    far = pl.BlockSpec(memory_space=pltpu.HBM)
    near = pl.BlockSpec(memory_space=pltpu.VMEM)
    return pl.pallas_call(
        lambda *refs: tables_kernel(count, *refs),
        out_shape=[jax.ShapeDtypeStruct(table.shape, table.dtype) for table in tables]
        + [jax.ShapeDtypeStruct((skip_gain.shape[0], 8), jnp.float32)],
        in_specs=[far] * (count + 1) + [near],
        out_specs=[near] * (count + 1),
        scratch_shapes=[
            pltpu.VMEM(skip_gain.shape, jnp.float32),
            pltpu.SemaphoreType.DMA((count + 1,)),
        ],
        compiler_params=pltpu.CompilerParams(vmem_limit_bytes=16 << 20),
        name="near_tables",
    )(*in_hbm(*tables, skip_gain), after)


def pack_kernel(nodes, chans, qkv_ref, filter_ref, flat_ref, *refs):
    outs = refs[:nodes]
    query_ref, taps_ref = refs[nodes : nodes + 2]
    filters, streams, flat, sems = refs[nodes + 2 :]
    place = lax.axis_index("ctx")
    block = qkv_ref.shape[2]
    rim = taps_ref.shape[2] - 1
    shares = [
        pl.ds(pl.multiple_of((place ^ mask) * chans, chans), chans) for mask in range(nodes)
    ]
    flat_move = pltpu.make_async_copy(flat_ref, flat, sems.at[0])
    query_move = pltpu.make_async_copy(qkv_ref.at[0], query_ref, sems.at[1])
    filter_move = pltpu.make_async_copy(filter_ref, filters, sems.at[2])
    stream_move = pltpu.make_async_copy(qkv_ref.at[pl.ds(1, 2)], streams, sems.at[3])
    for move in (flat_move, stream_move, query_move, filter_move):
        move.start()
    lane = lax.broadcasted_iota(jnp.int32, (chans, LANES), 1)

    flat_move.wait()
    for stream in range(3):
        taps_ref[stream] = flat[stream].T
    query_move.wait()
    edges = jnp.zeros((chans, LANES), jnp.float32)
    for share in range(nodes):
        tile = query_ref[share * chans : (share + 1) * chans, block - LANES :]
        moved = pltpu.roll(tile.astype(jnp.float32), LANE_Q + (share + 1) * rim, 1)
        edges = jnp.where(lane >= LANE_Q + share * rim, moved, edges)
    stream_move.wait()
    for mask, rows in reversed(list(enumerate(shares))):
        edge = edges
        features = []
        for stream in reversed(range(2)):
            values = streams[stream, rows, :].astype(jnp.float32)
            ends = jnp.where(lane < rim, values[:, :LANES], values[:, block - LANES :])
            at = stream * LANE_V
            edge = jnp.where(lane < at + LANE_V, pltpu.roll(ends, at + rim, 1), edge)
            taps = taps_ref[1 + stream, rows, :]
            wide = [
                jnp.broadcast_to(taps[:, tap : tap + 1], (chans, LANES)) for tap in range(rim + 1)
            ]
            raw = streams[stream, rows, :]
            totals = []
            for index in range(block // LANES):
                tile = raw[:, index * LANES : (index + 1) * LANES]
                total = wide[0] * tile.astype(jnp.float32)
                moved = [pltpu.roll(tile, shift, 1) for shift in range(1, rim + 1)]
                if index == 0:
                    before = moved
                for shift in range(1, rim + 1):
                    joined = jnp.where(lane < shift, before[shift - 1], moved[shift - 1])
                    total = total + wide[shift] * joined.astype(jnp.float32)
                before = moved
                totals.append(total)
            features.append(totals)
        for index, (left, right) in enumerate(zip(*features)):
            outs[mask][:, index * LANES : (index + 1) * LANES] = (left * right).astype(jnp.bfloat16)
        outs[mask][:, 2 * block :] = edge.astype(jnp.bfloat16)
    filter_move.wait()
    for mask, rows in enumerate(shares):
        outs[mask][:, block : 2 * block] = filters[rows, :].astype(jnp.bfloat16)


def pack(qkv, long_filter, short_taps, nodes, chans):
    _, every, block = qkv.shape
    far = pl.BlockSpec(memory_space=pltpu.HBM)
    near = pl.BlockSpec(memory_space=pltpu.VMEM)
    flat = jnp.swapaxes(short_taps, 1, 2)
    *pieces, query, taps = pl.pallas_call(
        lambda *refs: pack_kernel(nodes, chans, *refs),
        out_shape=[jax.ShapeDtypeStruct((chans, 2 * block + LANES), jnp.bfloat16)] * nodes
        + [
            jax.ShapeDtypeStruct((every, block), jnp.bfloat16),
            jax.ShapeDtypeStruct(short_taps.shape, jnp.float32),
        ],
        in_specs=[far] * 3,
        out_specs=[near] * (nodes + 2),
        scratch_shapes=[
            pltpu.VMEM((every, block), jnp.float32),
            pltpu.VMEM((2, every, block), jnp.bfloat16),
            pltpu.VMEM(flat.shape, jnp.float32),
            pltpu.SemaphoreType.DMA((4,)),
        ],
        compiler_params=pltpu.CompilerParams(vmem_limit_bytes=16 << 20),
        name="pack",
    )(*in_hbm(qkv, long_filter, flat))
    return pieces, query, taps


def query_kernel(nodes, query_ref, taps_ref, *refs):
    pieces = refs[:nodes]
    out_ref = refs[nodes]
    place = lax.axis_index("ctx")
    _, chans, block = out_ref.shape
    rim = taps_ref.shape[2] - 1
    lane = lax.broadcasted_iota(jnp.int32, (chans, LANES), 1)
    edge = jnp.zeros((chans, LANES), jnp.float32)
    for mask in range(1, nodes):
        before = (place ^ mask) == place - 1
        found = pieces[mask][:, pieces[mask].shape[1] - LANES :].astype(jnp.float32)
        edge = jnp.where(before, found, edge)
    for mask in range(nodes):
        share = place ^ mask
        rows = pl.ds(pl.multiple_of(share * chans, chans), chans)
        taps = taps_ref[0, rows, :]
        values = query_ref[rows, :].astype(jnp.float32)
        history = pltpu.roll(edge, LANES - LANE_Q - (share + 1) * rim, 1)
        first = taps[:, :1] * values[:, :LANES]
        for shift in range(1, rim + 1):
            joined = jnp.where(lane >= LANES - shift, history, values[:, :LANES])
            first = first + taps[:, shift : shift + 1] * pltpu.roll(joined, shift, 1)
        out_ref[nodes - 1 - mask] = rolled_taps(values, taps)
        out_ref[nodes - 1 - mask, :, :LANES] = first


def query_features(query, short_taps, pieces, nodes, chans):
    near = pl.BlockSpec(memory_space=pltpu.VMEM)
    return pl.pallas_call(
        lambda *refs: query_kernel(nodes, *refs),
        out_shape=jax.ShapeDtypeStruct((nodes, chans, query.shape[1]), jnp.float32),
        in_specs=[near] * (2 + nodes),
        out_specs=near,
        compiler_params=pltpu.CompilerParams(vmem_limit_bytes=16 << 20),
        name="query_features",
    )(query, short_taps, *pieces)


def long_kernel(
    nodes, chans, per_node, rim, taps_ref, first_ref, twist_ref, second_ref, last_ref, skip_ref, *refs
):
    pieces = refs[:nodes][::-1]
    outs = refs[nodes : 2 * nodes]
    raw, edges, final = refs[2 * nodes :]
    rows = nodes * per_node
    pitch = rows + PAD
    place = lax.axis_index("ctx")
    base = place * chans
    block = per_node * LANES

    if rim:
        lane = lax.broadcasted_iota(jnp.int32, (chans, LANES), 1)
        own = pl.ds(pl.multiple_of(base, chans), chans)
        edges[0] = jnp.zeros((chans, LANES), jnp.bfloat16)
        for mask in range(nodes):
            edges[(place ^ mask) + 1] = pieces[mask][:, 2 * block :]
        wide = []
        for stream in range(2):
            taps = taps_ref[1 + stream, own, :]
            wide.append(
                [jnp.broadcast_to(taps[:, tap : tap + 1], (chans, LANES)) for tap in range(rim + 1)]
            )

    def repaired(mask, tile):
        before, now = edges[place ^ mask], pieces[mask][:, 2 * block :]
        product = None
        for stream in range(2):
            back = (LANES - stream * LANE_V) % LANES
            joined = jnp.where(lane < stream * LANE_V + rim, before, now)
            if back:
                joined = pltpu.roll(joined, back, 1)
            featured = wide[stream][0] * joined.astype(jnp.float32)
            for shift in range(1, rim + 1):
                moved = pltpu.roll(joined, shift, 1).astype(jnp.float32)
                featured = featured + wide[stream][shift] * moved
            product = featured if product is None else product * featured
        product = pltpu.roll(product, LANES - rim, 1).astype(jnp.bfloat16).astype(jnp.float32)
        return jnp.where(lane < rim, product, tile)

    for part in reversed(range(2)):
        for mask in range(nodes):
            start = (place ^ mask) * per_node
            for tile in range(per_node):
                at = part * block + tile * LANES
                values = pieces[mask][:, at : at + LANES].astype(jnp.float32)
                if rim and at == 0:
                    values = repaired(mask, values)
                raw[part, pl.ds(start + tile, chans, stride=pitch), :] = values

    cos_twist = twist_ref[:, :LANES]
    sin_twist = twist_ref[:, LANES:]
    skips = skip_ref[pl.ds(pl.multiple_of(base, chans), chans), :]

    def inner(parts):
        high, low = halves(jnp.concatenate(parts, axis=0))
        return dot(jnp.concatenate([high, low, high], axis=1), second_ref[...])

    def turn(real, imag, axis):
        return jnp.concatenate(
            [real * cos_twist + imag * sin_twist, imag * cos_twist - real * sin_twist], axis=axis
        )

    spectra = [[], []]
    for chan in range(chans):
        span = slice(chan * pitch, chan * pitch + rows)
        both = jnp.concatenate([raw[0, span, :], raw[1, span, :]], axis=1).astype(jnp.bfloat16)
        section = dot(first_ref[...], jnp.concatenate([both, both], axis=0))
        for part in range(2):
            cols = slice(part * LANES, (part + 1) * LANES)
            spectra[part].append(turn(section[:rows, cols], section[rows:, cols], 1))
    spectra = spectra[0] + spectra[1]
    fil_spec = inner(spectra[chans:])
    sig_spec = inner(spectra[:chans])
    def product(chan):
        sig = sig_spec[chan * rows : (chan + 1) * rows, :]
        fil = fil_spec[chan * rows : (chan + 1) * rows, :]
        sig_real, sig_imag = sig[:, :LANES], sig[:, LANES:]
        fil_real, fil_imag = fil[:, :LANES], fil[:, LANES:]
        return jnp.concatenate(
            [
                sig_real * fil_real - sig_imag * fil_imag,
                -(sig_real * fil_imag + sig_imag * fil_real),
            ],
            axis=1,
        )

    group = max(chans // 2, 1)
    groups = [range(begin, begin + group) for begin in range(0, chans, group)]
    turned = []
    for members in groups:
        back = inner([product(chan) for chan in members])
        for index in range(group):
            at = slice(index * rows, (index + 1) * rows)
            turned.append(turn(back[at, :LANES], back[at, LANES:], 0))
    for members in groups:
        high, low = halves(jnp.concatenate([turned[chan] for chan in members], axis=1))
        convolved = dot(last_ref[...], jnp.concatenate([high, low, high], axis=0))
        for index, chan in enumerate(members):
            span = slice(chan * pitch, chan * pitch + rows)
            final[span, :] = (
                convolved[:, index * LANES : (index + 1) * LANES]
                + skips[chan : chan + 1, :1] * raw[0, span, :]
            )
    for mask in range(nodes):
        start = (place ^ mask) * per_node
        for tile in range(per_node):
            outs[mask][:, tile * LANES : (tile + 1) * LANES] = final[
                pl.ds(start + tile, chans, stride=pitch), :
            ].astype(jnp.bfloat16)


def long_mix(pieces, taps, tables, block):
    nodes = len(pieces)
    chans, width = pieces[0].shape
    per_node = block // LANES
    rows = nodes * per_node
    rim = taps.shape[2] - 1 if width > 2 * block else 0
    near = pl.BlockSpec(memory_space=pltpu.VMEM)
    return pl.pallas_call(
        lambda *refs: long_kernel(nodes, chans, per_node, rim, *refs),
        out_shape=[jax.ShapeDtypeStruct((chans, block), jnp.bfloat16)] * nodes,
        in_specs=[near] * (1 + len(tables) + nodes),
        out_specs=[near] * nodes,
        scratch_shapes=[
            pltpu.VMEM((2, (chans + 1) * (rows + PAD), LANES), jnp.float32),
            pltpu.VMEM((nodes + 1, chans, LANES), jnp.bfloat16),
            pltpu.VMEM(((chans + 1) * (rows + PAD), LANES), jnp.float32),
        ],
        compiler_params=pltpu.CompilerParams(vmem_limit_bytes=24 << 20),
        name="long_mix",
    )(taps, *tables, *pieces[::-1])


def gather_blocks(depths, blocks, gathered):
    place = lax.axis_index("ctx")
    spot = lax.axis_index("ch")
    level, core = spot // 2, spot % 2
    for index, block in enumerate(blocks):
        nodes, chans, _ = block.shape
        side = core ^ (index % 2)
        for mask in range(nodes):
            row = ((2 * (index // 2) + side) * nodes + (place ^ mask)) * chans
            gathered[pl.ds(pl.multiple_of(row, chans), chans), :] = block[nodes - 1 - mask]
    width = 2 * nodes * chans
    return [pl.ds(pl.multiple_of((level ^ depth) * width, width), width) for depth in depths]


def partial_kernel(depths, rows, weight_ref, *refs):
    blocks = refs[: 2 * len(depths)]
    out_ref, gathered = refs[2 * len(depths) :]
    columns = gather_blocks(depths, blocks, gathered)
    for begin in range(0, out_ref.shape[0], rows):
        weight = jnp.concatenate([weight_ref[begin : begin + rows, at] for at in columns], axis=1)
        out_ref[begin : begin + rows, :] = dot(weight, gathered[...])


def final_kernel(depths, cuts, weight_ref, partial_ref, *refs):
    blocks = refs[: 2 * len(depths)]
    out_ref, gathered, held, sems = refs[2 * len(depths) :]
    columns = gather_blocks(depths, blocks, gathered)
    copies = []
    for part, (begin, end) in enumerate(zip(cuts, cuts[1:])):
        weight = jnp.concatenate([weight_ref[begin:end, at] for at in columns], axis=1)
        total = partial_ref[begin:end, :] + dot(weight, gathered[...])
        held[begin:end, :] = total.astype(jnp.bfloat16)
        rows = pl.ds(begin, end - begin)
        copies.append(
            pltpu.make_async_copy(held.at[rows, :], out_ref.at[rows, :], sems.at[part])
        )
        copies[-1].start()
    for copy in copies:
        copy.wait()


def project_early(early, out_weight):
    features, _ = out_weight.shape
    near = pl.BlockSpec(memory_space=pltpu.VMEM)
    blocks = [block for pair in early.values() for block in pair]
    nodes, chans, block = blocks[0].shape
    depth = nodes * chans * len(blocks)
    cost = pl.CostEstimate(
        flops=0, bytes_accessed=0, transcendentals=0
    )
    return pl.pallas_call(
        lambda *refs: partial_kernel(tuple(early), features // 4, *refs),
        out_shape=jax.ShapeDtypeStruct((features, block), jnp.float32),
        in_specs=[near] * (1 + len(blocks)),
        out_specs=near,
        scratch_shapes=[pltpu.VMEM((depth, block), jnp.bfloat16)],
        compiler_params=pltpu.CompilerParams(vmem_limit_bytes=16 << 20),
        cost_estimate=cost,
        name="project_early",
    )(out_weight, *blocks)


def project_late(partial, late, out_weight):
    features, _ = out_weight.shape
    near = pl.BlockSpec(memory_space=pltpu.VMEM)
    blocks = [block for pair in late.values() for block in pair]
    nodes, chans, block = blocks[0].shape
    depth = nodes * chans * len(blocks)
    cuts = tuple(range(0, features + 1, features // 8))
    return pl.pallas_call(
        lambda *refs: final_kernel(tuple(late), cuts, *refs),
        out_shape=jax.ShapeDtypeStruct((features, block), jnp.bfloat16),
        in_specs=[near] * (2 + len(blocks)),
        out_specs=pl.BlockSpec(memory_space=pl.ANY),
        scratch_shapes=[
            pltpu.VMEM((depth, block), jnp.bfloat16),
            pltpu.VMEM((features, block), jnp.bfloat16),
            pltpu.SemaphoreType.DMA((len(cuts) - 1,)),
        ],
        compiler_params=pltpu.CompilerParams(vmem_limit_bytes=16 << 20),
        name="project_late",
    )(out_weight, partial, *blocks)


def project_plain(blocks, out_weight):
    nodes, chans, block = blocks[0].shape
    stacks = len(blocks) // 2
    place = lax.axis_index("ctx")
    spot = lax.axis_index("ch")
    found = jnp.stack(blocks).reshape(2, stacks, nodes, chans, block)
    index = jnp.arange(2 * stacks, dtype=jnp.int32) ^ spot
    found = found[index % 2, index // 2]
    found = found[:, nodes - 1 - (jnp.arange(nodes, dtype=jnp.int32) ^ place)]
    summed = jnp.dot(
        out_weight, found.reshape(-1, block), preferred_element_type=jnp.float32
    )
    return summed.astype(jnp.bfloat16)


def features_plain(qkv, short_taps):
    block = qkv.shape[2]
    tap_count = short_taps.shape[2]
    devices = lax.axis_size("ctx")
    route = [(i, i + 1) for i in range(devices - 1)]
    history = lax.ppermute(qkv[:, :, block - (tap_count - 1) :], "ctx", route)
    extended = jnp.concatenate([history, qkv], axis=2).astype(jnp.float32)
    result = jnp.zeros(qkv.shape, jnp.float32)
    for offset in range(tap_count):
        begin = tap_count - 1 - offset
        result = (
            result
            + short_taps[:, :, offset : offset + 1] * extended[:, :, begin : begin + block]
        )
    return result


def swapped(block, mask, axis):
    if mask == 0:
        return block
    return lax.ppermute(block, axis, [(i, i ^ mask) for i in range(lax.axis_size(axis))])


def local(qkv, short_taps, long_filter, skip_gain, out_weight):
    nodes = lax.axis_size("ctx")
    spread = lax.axis_size("ch")
    stacks = spread // 2
    place = lax.axis_index("ctx")
    _, every, block = qkv.shape
    chans = every // nodes
    fits = chans % 16 == 0

    if fits:
        pieces, query, taps = pack(qkv, long_filter, short_taps, nodes, chans)
    else:
        taps = short_taps
        query, key, value = features_plain(qkv, short_taps)
        both = jnp.concatenate([key * value, long_filter], axis=1).astype(jnp.bfloat16)
        both = both.reshape(nodes, chans, 2 * block)
        pieces = [lax.dynamic_index_in_dim(both, place ^ mask, 0, False) for mask in range(nodes)]
    pieces = [swapped(pieces[mask], mask, "ctx") for mask in range(nodes)]
    out_weight, *tables = near_tables(
        nodes * block // LANES, skip_gain, out_weight, pieces[0]
    )
    mixed = long_mix(pieces, taps, tables, block)

    if fits:
        tied = lax.optimization_barrier((mixed[0], *pieces[::-1]))[:0:-1]
        featured = query_features(query, taps, tied, nodes, chans)
    else:
        featured = query.reshape(nodes, chans, block)[jnp.arange(nodes, dtype=jnp.int32) ^ place][::-1]
    mixed = [swapped(mixed[mask], mask, "ctx") for mask in range(nodes)]
    mixed = jnp.stack(mixed[::-1])
    gated = (featured * mixed.astype(jnp.float32)).astype(jnp.bfloat16)

    column = [swapped(gated, 2 * depth, "ch") for depth in range(stacks)]
    if not fits:
        return project_plain(column + [swapped(part, 1, "ch") for part in column], out_weight)
    pairs = {depth: (part, swapped(part, 1, "ch")) for depth, part in enumerate(column)}
    late = {depth: pairs.pop(depth) for depth in (3, 1)}
    return project_late(project_early(pairs, out_weight), late, out_weight)


def solution(mesh):
    placed = (P(None, "ch", "ctx"), P(None, "ch", None), P("ch", "ctx"), P("ch"), P("ch", None))
    return jax.shard_map(
        local, mesh=mesh, in_specs=placed, out_specs=P("ch", "ctx"), check_vma=False
    )
```

```python
import math

import numpy as np

import jax
import jax.numpy as jnp
from jax import lax
from jax.experimental import pallas as pl
from jax.experimental.pallas import tpu as pltpu
from jax.sharding import PartitionSpec as P

LANES = 128
PAD = 8
LANE_V = 16
LANE_Q = 32


def split_table(table):
    high = table.astype(jnp.bfloat16)
    low = (table - high.astype(np.float64)).astype(jnp.bfloat16)
    return high, low


def dft_tables(rows):
    total = 2 * rows * LANES
    block = np.arange(rows, dtype=np.float64)
    freq = np.arange(rows, dtype=np.float64) + 0.5
    lane = np.arange(LANES, dtype=np.float64)
    head = 2.0 * math.pi * np.outer(freq, block) / (2 * rows)
    first = np.concatenate(
        split_table(np.concatenate([np.cos(head), -np.sin(head)], axis=0)), axis=1
    )
    turn = 2.0 * math.pi * np.outer(freq, lane) / total
    twist = np.concatenate([np.cos(turn), np.sin(turn)], axis=1).astype(np.float32)
    inner = 2.0 * math.pi * np.outer(lane, lane) / LANES
    square = np.block([[np.cos(inner), -np.sin(inner)], [np.sin(inner), np.cos(inner)]])
    square_high, square_low = split_table(square)
    second = np.concatenate([square_high, square_high, square_low], axis=0)
    tail = head.T
    tail_high, tail_low = split_table(
        (2.0 / total) * np.concatenate([np.cos(tail), np.sin(tail)], axis=1)
    )
    last = np.concatenate([tail_high, tail_high, tail_low], axis=1)
    return first, twist, second, last


def halves(value):
    high = value.astype(jnp.bfloat16)
    low = (value - high.astype(jnp.float32)).astype(jnp.bfloat16)
    return high, low


def dot(left, right):
    return jnp.dot(left, right, preferred_element_type=jnp.float32)


def rolled_taps(values, weights):
    total = weights[0] * values
    for shift, weight in enumerate(weights[1:], 1):
        total = total + weight * pltpu.roll(values, shift, 1)
    return total


def widened(flat):
    count, every = flat.shape
    rest = jnp.concatenate([flat, jnp.zeros((8 - count, every), jnp.float32)], axis=0)
    parts = []
    for _ in range(3):
        part = rest.astype(jnp.bfloat16)
        rest = rest - part.astype(jnp.float32)
        parts.append(part.astype(jnp.float32))
    shape = (8, count * LANES)
    tap = lax.broadcasted_iota(jnp.int32, shape, 0) * LANES
    lane = lax.broadcasted_iota(jnp.int32, shape, 1)
    ones = jnp.where((lane >= tap) & (lane < tap + LANES), 1.0, 0.0)
    left = jnp.concatenate(parts, axis=0).T.astype(jnp.bfloat16)
    return dot(left, jnp.concatenate([ones] * 3, axis=0).astype(jnp.bfloat16))


def tap_tiles(wide_ref, stream, rows):
    return [wide_ref[stream, rows, at : at + LANES] for at in range(0, wide_ref.shape[2], LANES)]


def in_hbm(*arrays):
    return [pltpu.with_memory_space_constraint(array, pltpu.HBM) for array in arrays]


def tables_kernel(count, *refs):
    sources, skip_ref = refs[:count], refs[count]
    outs, column_ref = refs[count + 2 : 2 * count + 2], refs[2 * count + 2]
    skips, sems = refs[2 * count + 3 :]
    moves = [
        pltpu.make_async_copy(source, out, sems.at[index])
        for index, (source, out) in enumerate(zip(sources, outs))
    ]
    moves.append(pltpu.make_async_copy(skip_ref, skips, sems.at[count]))
    for move in moves:
        move.start()
    moves[count].wait()
    column_ref[...] = jnp.broadcast_to(skips[...].reshape(1, -1), (8, skips.shape[0])).T
    for move in moves[:count]:
        move.wait()


def near_tables(rows, skip_gain, out_weight, after):
    tables = [out_weight] + [jnp.asarray(table) for table in dft_tables(rows)]
    count = len(tables)
    far = pl.BlockSpec(memory_space=pltpu.HBM)
    near = pl.BlockSpec(memory_space=pltpu.VMEM)
    return pl.pallas_call(
        lambda *refs: tables_kernel(count, *refs),
        out_shape=[jax.ShapeDtypeStruct(table.shape, table.dtype) for table in tables]
        + [jax.ShapeDtypeStruct((skip_gain.shape[0], 8), jnp.float32)],
        in_specs=[far] * (count + 1) + [near],
        out_specs=[near] * (count + 1),
        scratch_shapes=[
            pltpu.VMEM(skip_gain.shape, jnp.float32),
            pltpu.SemaphoreType.DMA((count + 1,)),
        ],
        compiler_params=pltpu.CompilerParams(vmem_limit_bytes=16 << 20),
        name="near_tables",
    )(*in_hbm(*tables, skip_gain), after)


def pack_kernel(nodes, chans, qkv_ref, filter_ref, flat_ref, *refs):
    outs = refs[:nodes]
    query_ref, wide_ref = refs[nodes : nodes + 2]
    filters, streams, flat, sems = refs[nodes + 2 :]
    place = lax.axis_index("ctx")
    block = qkv_ref.shape[2]
    rim = flat_ref.shape[1] - 1
    shares = [
        pl.ds(pl.multiple_of((place ^ mask) * chans, chans), chans) for mask in range(nodes)
    ]
    flat_move = pltpu.make_async_copy(flat_ref, flat, sems.at[0])
    query_move = pltpu.make_async_copy(qkv_ref.at[0], query_ref, sems.at[1])
    filter_move = pltpu.make_async_copy(filter_ref, filters, sems.at[2])
    stream_move = pltpu.make_async_copy(qkv_ref.at[pl.ds(1, 2)], streams, sems.at[3])
    for move in (flat_move, stream_move, query_move, filter_move):
        move.start()
    lane = lax.broadcasted_iota(jnp.int32, (chans, LANES), 1)

    flat_move.wait()
    for stream in range(3):
        wide_ref[stream] = widened(flat[stream])
    query_move.wait()
    edges = jnp.zeros((chans, LANES), jnp.float32)
    for share in range(nodes):
        tile = query_ref[share * chans : (share + 1) * chans, block - LANES :]
        moved = pltpu.roll(tile.astype(jnp.float32), LANE_Q + (share + 1) * rim, 1)
        edges = jnp.where(lane >= LANE_Q + share * rim, moved, edges)
    stream_move.wait()
    for mask, rows in reversed(list(enumerate(shares))):
        edge = edges
        features = []
        for stream in reversed(range(2)):
            values = streams[stream, rows, :].astype(jnp.float32)
            ends = jnp.where(lane < rim, values[:, :LANES], values[:, block - LANES :])
            at = stream * LANE_V
            edge = jnp.where(lane < at + LANE_V, pltpu.roll(ends, at + rim, 1), edge)
            wide = tap_tiles(wide_ref, 1 + stream, rows)
            raw = streams[stream, rows, :]
            totals = []
            for index in range(block // LANES):
                tile = raw[:, index * LANES : (index + 1) * LANES]
                total = wide[0] * tile.astype(jnp.float32)
                moved = [pltpu.roll(tile, shift, 1) for shift in range(1, rim + 1)]
                if index == 0:
                    before = moved
                for shift in range(1, rim + 1):
                    joined = jnp.where(lane < shift, before[shift - 1], moved[shift - 1])
                    total = total + wide[shift] * joined.astype(jnp.float32)
                before = moved
                totals.append(total)
            features.append(totals)
        for index, (left, right) in enumerate(zip(*features)):
            outs[mask][:, index * LANES : (index + 1) * LANES] = (left * right).astype(jnp.bfloat16)
        outs[mask][:, 2 * block :] = edge.astype(jnp.bfloat16)
    filter_move.wait()
    for mask, rows in enumerate(shares):
        outs[mask][:, block : 2 * block] = filters[rows, :].astype(jnp.bfloat16)


def pack(qkv, long_filter, short_taps, nodes, chans):
    _, every, block = qkv.shape
    far = pl.BlockSpec(memory_space=pltpu.HBM)
    near = pl.BlockSpec(memory_space=pltpu.VMEM)
    flat = jnp.swapaxes(short_taps, 1, 2)
    *pieces, query, wide = pl.pallas_call(
        lambda *refs: pack_kernel(nodes, chans, *refs),
        out_shape=[jax.ShapeDtypeStruct((chans, 2 * block + LANES), jnp.bfloat16)] * nodes
        + [
            jax.ShapeDtypeStruct((every, block), jnp.bfloat16),
            jax.ShapeDtypeStruct((3, every, short_taps.shape[2] * LANES), jnp.float32),
        ],
        in_specs=[far] * 3,
        out_specs=[near] * (nodes + 2),
        scratch_shapes=[
            pltpu.VMEM((every, block), jnp.float32),
            pltpu.VMEM((2, every, block), jnp.bfloat16),
            pltpu.VMEM(flat.shape, jnp.float32),
            pltpu.SemaphoreType.DMA((4,)),
        ],
        compiler_params=pltpu.CompilerParams(vmem_limit_bytes=16 << 20),
        name="pack",
    )(*in_hbm(qkv, long_filter, flat))
    return pieces, query, wide


def query_kernel(nodes, query_ref, wide_ref, *refs):
    pieces = refs[:nodes]
    out_ref = refs[nodes]
    place = lax.axis_index("ctx")
    _, chans, block = out_ref.shape
    rim = wide_ref.shape[2] // LANES - 1
    lane = lax.broadcasted_iota(jnp.int32, (chans, LANES), 1)
    edge = jnp.zeros((chans, LANES), jnp.float32)
    for mask in range(1, nodes):
        before = (place ^ mask) == place - 1
        found = pieces[mask][:, pieces[mask].shape[1] - LANES :].astype(jnp.float32)
        edge = jnp.where(before, found, edge)
    for mask in range(nodes):
        share = place ^ mask
        rows = pl.ds(pl.multiple_of(share * chans, chans), chans)
        weights = [tile[:, :1] for tile in tap_tiles(wide_ref, 0, rows)]
        values = query_ref[rows, :].astype(jnp.float32)
        history = pltpu.roll(edge, LANES - LANE_Q - (share + 1) * rim, 1)
        first = weights[0] * values[:, :LANES]
        for shift in range(1, rim + 1):
            joined = jnp.where(lane >= LANES - shift, history, values[:, :LANES])
            first = first + weights[shift] * pltpu.roll(joined, shift, 1)
        out_ref[nodes - 1 - mask] = rolled_taps(values, weights)
        out_ref[nodes - 1 - mask, :, :LANES] = first


def query_features(query, wide, pieces, nodes, chans):
    near = pl.BlockSpec(memory_space=pltpu.VMEM)
    return pl.pallas_call(
        lambda *refs: query_kernel(nodes, *refs),
        out_shape=jax.ShapeDtypeStruct((nodes, chans, query.shape[1]), jnp.float32),
        in_specs=[near] * (2 + nodes),
        out_specs=near,
        compiler_params=pltpu.CompilerParams(vmem_limit_bytes=16 << 20),
        name="query_features",
    )(query, wide, *pieces)


def long_kernel(
    nodes, chans, per_node, rim, wide_ref, first_ref, twist_ref, second_ref, last_ref, skip_ref, *refs
):
    pieces = refs[:nodes][::-1]
    outs = refs[nodes : 2 * nodes]
    raw, edges, final = refs[2 * nodes :]
    rows = nodes * per_node
    pitch = rows + PAD
    place = lax.axis_index("ctx")
    base = place * chans
    block = per_node * LANES

    if rim:
        lane = lax.broadcasted_iota(jnp.int32, (chans, LANES), 1)
        own = pl.ds(pl.multiple_of(base, chans), chans)
        edges[0] = jnp.zeros((chans, LANES), jnp.bfloat16)
        for mask in range(nodes):
            edges[(place ^ mask) + 1] = pieces[mask][:, 2 * block :]
        wide = [tap_tiles(wide_ref, 1 + stream, own) for stream in range(2)]

    def repaired(mask, tile):
        before, now = edges[place ^ mask], pieces[mask][:, 2 * block :]
        product = None
        for stream in range(2):
            back = (LANES - stream * LANE_V) % LANES
            joined = jnp.where(lane < stream * LANE_V + rim, before, now)
            if back:
                joined = pltpu.roll(joined, back, 1)
            featured = wide[stream][0] * joined.astype(jnp.float32)
            for shift in range(1, rim + 1):
                moved = pltpu.roll(joined, shift, 1).astype(jnp.float32)
                featured = featured + wide[stream][shift] * moved
            product = featured if product is None else product * featured
        product = pltpu.roll(product, LANES - rim, 1).astype(jnp.bfloat16).astype(jnp.float32)
        return jnp.where(lane < rim, product, tile)

    for part in reversed(range(2)):
        for mask in range(nodes):
            start = (place ^ mask) * per_node
            for tile in range(per_node):
                at = part * block + tile * LANES
                values = pieces[mask][:, at : at + LANES].astype(jnp.float32)
                if rim and at == 0:
                    values = repaired(mask, values)
                raw[part, pl.ds(start + tile, chans, stride=pitch), :] = values

    cos_twist = twist_ref[:, :LANES]
    sin_twist = twist_ref[:, LANES:]
    skips = skip_ref[pl.ds(pl.multiple_of(base, chans), chans), :]

    def inner(parts):
        high, low = halves(jnp.concatenate(parts, axis=0))
        return dot(jnp.concatenate([high, low, high], axis=1), second_ref[...])

    def turn(real, imag, axis):
        return jnp.concatenate(
            [real * cos_twist + imag * sin_twist, imag * cos_twist - real * sin_twist], axis=axis
        )

    spectra = [[], []]
    for chan in range(chans):
        span = slice(chan * pitch, chan * pitch + rows)
        both = jnp.concatenate([raw[0, span, :], raw[1, span, :]], axis=1).astype(jnp.bfloat16)
        section = dot(first_ref[...], jnp.concatenate([both, both], axis=0))
        for part in range(2):
            cols = slice(part * LANES, (part + 1) * LANES)
            spectra[part].append(turn(section[:rows, cols], section[rows:, cols], 1))
    spectra = spectra[0] + spectra[1]
    fil_spec = inner(spectra[chans:])
    sig_spec = inner(spectra[:chans])
    def product(chan):
        sig = sig_spec[chan * rows : (chan + 1) * rows, :]
        fil = fil_spec[chan * rows : (chan + 1) * rows, :]
        sig_real, sig_imag = sig[:, :LANES], sig[:, LANES:]
        fil_real, fil_imag = fil[:, :LANES], fil[:, LANES:]
        return jnp.concatenate(
            [
                sig_real * fil_real - sig_imag * fil_imag,
                -(sig_real * fil_imag + sig_imag * fil_real),
            ],
            axis=1,
        )

    group = max(chans // 2, 1)
    groups = [range(begin, begin + group) for begin in range(0, chans, group)]
    turned = []
    for members in groups:
        back = inner([product(chan) for chan in members])
        for index in range(group):
            at = slice(index * rows, (index + 1) * rows)
            turned.append(turn(back[at, :LANES], back[at, LANES:], 0))
    for members in groups:
        high, low = halves(jnp.concatenate([turned[chan] for chan in members], axis=1))
        convolved = dot(last_ref[...], jnp.concatenate([high, low, high], axis=0))
        for index, chan in enumerate(members):
            span = slice(chan * pitch, chan * pitch + rows)
            final[span, :] = (
                convolved[:, index * LANES : (index + 1) * LANES]
                + skips[chan : chan + 1, :1] * raw[0, span, :]
            )
    for mask in range(nodes):
        start = (place ^ mask) * per_node
        for tile in range(per_node):
            outs[mask][:, tile * LANES : (tile + 1) * LANES] = final[
                pl.ds(start + tile, chans, stride=pitch), :
            ].astype(jnp.bfloat16)


def long_mix(pieces, wide, tables, block):
    nodes = len(pieces)
    chans, width = pieces[0].shape
    per_node = block // LANES
    rows = nodes * per_node
    rim = wide.shape[2] // LANES - 1 if width > 2 * block else 0
    near = pl.BlockSpec(memory_space=pltpu.VMEM)
    return pl.pallas_call(
        lambda *refs: long_kernel(nodes, chans, per_node, rim, *refs),
        out_shape=[jax.ShapeDtypeStruct((chans, block), jnp.bfloat16)] * nodes,
        in_specs=[near] * (1 + len(tables) + nodes),
        out_specs=[near] * nodes,
        scratch_shapes=[
            pltpu.VMEM((2, (chans + 1) * (rows + PAD), LANES), jnp.float32),
            pltpu.VMEM((nodes + 1, chans, LANES), jnp.bfloat16),
            pltpu.VMEM(((chans + 1) * (rows + PAD), LANES), jnp.float32),
        ],
        compiler_params=pltpu.CompilerParams(vmem_limit_bytes=24 << 20),
        name="long_mix",
    )(wide, *tables, *pieces[::-1])


def gather_blocks(depths, blocks, gathered):
    place = lax.axis_index("ctx")
    spot = lax.axis_index("ch")
    level, core = spot // 2, spot % 2
    for index, block in enumerate(blocks):
        nodes, chans, _ = block.shape
        side = core ^ (index % 2)
        for mask in range(nodes):
            row = ((2 * (index // 2) + side) * nodes + (place ^ mask)) * chans
            gathered[pl.ds(pl.multiple_of(row, chans), chans), :] = block[nodes - 1 - mask]
    width = 2 * nodes * chans
    return [pl.ds(pl.multiple_of((level ^ depth) * width, width), width) for depth in depths]


def partial_kernel(depths, rows, weight_ref, *refs):
    blocks = refs[: 2 * len(depths)]
    out_ref, gathered = refs[2 * len(depths) :]
    columns = gather_blocks(depths, blocks, gathered)
    for begin in range(0, out_ref.shape[0], rows):
        weight = jnp.concatenate([weight_ref[begin : begin + rows, at] for at in columns], axis=1)
        out_ref[begin : begin + rows, :] = dot(weight, gathered[...])


def final_kernel(depths, cuts, weight_ref, partial_ref, *refs):
    blocks = refs[: 2 * len(depths)]
    out_ref, gathered, held, sems = refs[2 * len(depths) :]
    columns = gather_blocks(depths, blocks, gathered)
    copies = []
    for part, (begin, end) in enumerate(zip(cuts, cuts[1:])):
        weight = jnp.concatenate([weight_ref[begin:end, at] for at in columns], axis=1)
        total = partial_ref[begin:end, :] + dot(weight, gathered[...])
        held[begin:end, :] = total.astype(jnp.bfloat16)
        rows = pl.ds(begin, end - begin)
        copies.append(
            pltpu.make_async_copy(held.at[rows, :], out_ref.at[rows, :], sems.at[part])
        )
        copies[-1].start()
    for copy in copies:
        copy.wait()


def project_early(early, out_weight):
    features, _ = out_weight.shape
    near = pl.BlockSpec(memory_space=pltpu.VMEM)
    blocks = [block for pair in early.values() for block in pair]
    nodes, chans, block = blocks[0].shape
    depth = nodes * chans * len(blocks)
    cost = pl.CostEstimate(
        flops=0, bytes_accessed=0, transcendentals=0
    )
    return pl.pallas_call(
        lambda *refs: partial_kernel(tuple(early), features // 4, *refs),
        out_shape=jax.ShapeDtypeStruct((features, block), jnp.float32),
        in_specs=[near] * (1 + len(blocks)),
        out_specs=near,
        scratch_shapes=[pltpu.VMEM((depth, block), jnp.bfloat16)],
        compiler_params=pltpu.CompilerParams(vmem_limit_bytes=16 << 20),
        cost_estimate=cost,
        name="project_early",
    )(out_weight, *blocks)


def project_late(partial, late, out_weight):
    features, _ = out_weight.shape
    near = pl.BlockSpec(memory_space=pltpu.VMEM)
    blocks = [block for pair in late.values() for block in pair]
    nodes, chans, block = blocks[0].shape
    depth = nodes * chans * len(blocks)
    cuts = tuple(range(0, features + 1, features // 8))
    return pl.pallas_call(
        lambda *refs: final_kernel(tuple(late), cuts, *refs),
        out_shape=jax.ShapeDtypeStruct((features, block), jnp.bfloat16),
        in_specs=[near] * (2 + len(blocks)),
        out_specs=pl.BlockSpec(memory_space=pl.ANY),
        scratch_shapes=[
            pltpu.VMEM((depth, block), jnp.bfloat16),
            pltpu.VMEM((features, block), jnp.bfloat16),
            pltpu.SemaphoreType.DMA((len(cuts) - 1,)),
        ],
        compiler_params=pltpu.CompilerParams(vmem_limit_bytes=16 << 20),
        name="project_late",
    )(out_weight, partial, *blocks)


def project_plain(blocks, out_weight):
    nodes, chans, block = blocks[0].shape
    stacks = len(blocks) // 2
    place = lax.axis_index("ctx")
    spot = lax.axis_index("ch")
    found = jnp.stack(blocks).reshape(2, stacks, nodes, chans, block)
    index = jnp.arange(2 * stacks, dtype=jnp.int32) ^ spot
    found = found[index % 2, index // 2]
    found = found[:, nodes - 1 - (jnp.arange(nodes, dtype=jnp.int32) ^ place)]
    summed = jnp.dot(
        out_weight, found.reshape(-1, block), preferred_element_type=jnp.float32
    )
    return summed.astype(jnp.bfloat16)


def features_plain(qkv, short_taps):
    block = qkv.shape[2]
    tap_count = short_taps.shape[2]
    devices = lax.axis_size("ctx")
    route = [(i, i + 1) for i in range(devices - 1)]
    history = lax.ppermute(qkv[:, :, block - (tap_count - 1) :], "ctx", route)
    extended = jnp.concatenate([history, qkv], axis=2).astype(jnp.float32)
    result = jnp.zeros(qkv.shape, jnp.float32)
    for offset in range(tap_count):
        begin = tap_count - 1 - offset
        result = (
            result
            + short_taps[:, :, offset : offset + 1] * extended[:, :, begin : begin + block]
        )
    return result


def swapped(block, mask, axis):
    if mask == 0:
        return block
    return lax.ppermute(block, axis, [(i, i ^ mask) for i in range(lax.axis_size(axis))])


def local(qkv, short_taps, long_filter, skip_gain, out_weight):
    nodes = lax.axis_size("ctx")
    spread = lax.axis_size("ch")
    stacks = spread // 2
    place = lax.axis_index("ctx")
    _, every, block = qkv.shape
    chans = every // nodes
    fits = chans % 16 == 0

    if fits:
        pieces, query, wide = pack(qkv, long_filter, short_taps, nodes, chans)
    else:
        wide = short_taps
        query, key, value = features_plain(qkv, short_taps)
        both = jnp.concatenate([key * value, long_filter], axis=1).astype(jnp.bfloat16)
        both = both.reshape(nodes, chans, 2 * block)
        pieces = [lax.dynamic_index_in_dim(both, place ^ mask, 0, False) for mask in range(nodes)]
    pieces = [swapped(pieces[mask], mask, "ctx") for mask in range(nodes)]
    out_weight, *tables = near_tables(
        nodes * block // LANES, skip_gain, out_weight, pieces[0]
    )
    mixed = long_mix(pieces, wide, tables, block)

    if fits:
        tied = lax.optimization_barrier((mixed[0], *pieces[::-1]))[:0:-1]
        featured = query_features(query, wide, tied, nodes, chans)
    else:
        featured = query.reshape(nodes, chans, block)[jnp.arange(nodes, dtype=jnp.int32) ^ place][::-1]
    mixed = [swapped(mixed[mask], mask, "ctx") for mask in range(nodes)]
    mixed = jnp.stack(mixed[::-1])
    gated = (featured * mixed.astype(jnp.float32)).astype(jnp.bfloat16)

    column = [swapped(gated, 2 * depth, "ch") for depth in range(stacks)]
    if not fits:
        return project_plain(column + [swapped(part, 1, "ch") for part in column], out_weight)
    pairs = {depth: (part, swapped(part, 1, "ch")) for depth, part in enumerate(column)}
    late = {depth: pairs.pop(depth) for depth in (3, 1)}
    return project_late(project_early(pairs, out_weight), late, out_weight)


def solution(mesh):
    placed = (P(None, "ch", "ctx"), P(None, "ch", None), P("ch", "ctx"), P("ch"), P("ch", None))
    return jax.shard_map(
        local, mesh=mesh, in_specs=placed, out_specs=P("ch", "ctx"), check_vma=False
    )
```

```python
import math

import numpy as np

import jax
import jax.numpy as jnp
from jax import lax
from jax.experimental import pallas as pl
from jax.experimental.pallas import tpu as pltpu
from jax.sharding import PartitionSpec as P

LANES = 128
PAD = 8
LANE_V = 16
LANE_Q = 32


def split_table(table):
    high = table.astype(jnp.bfloat16)
    low = (table - high.astype(np.float64)).astype(jnp.bfloat16)
    return high, low


def dft_tables(rows):
    total = 2 * rows * LANES
    block = np.arange(rows, dtype=np.float64)
    freq = np.arange(rows, dtype=np.float64) + 0.5
    lane = np.arange(LANES, dtype=np.float64)
    head = 2.0 * math.pi * np.outer(freq, block) / (2 * rows)
    first = np.concatenate(
        split_table(np.concatenate([np.cos(head), -np.sin(head)], axis=0)), axis=1
    )
    turn = 2.0 * math.pi * np.outer(freq, lane) / total
    twist = np.concatenate([np.cos(turn), np.sin(turn)], axis=1).astype(np.float32)
    inner = 2.0 * math.pi * np.outer(lane, lane) / LANES
    square = np.block([[np.cos(inner), -np.sin(inner)], [np.sin(inner), np.cos(inner)]])
    square_high, square_low = split_table(square)
    second = np.concatenate([square_high, square_high, square_low], axis=0)
    tail = head.T
    tail_high, tail_low = split_table(
        (2.0 / total) * np.concatenate([np.cos(tail), np.sin(tail)], axis=1)
    )
    last = np.concatenate([tail_high, tail_high, tail_low], axis=1)
    return first, twist, second, last


def halves(value):
    high = value.astype(jnp.bfloat16)
    low = (value - high.astype(jnp.float32)).astype(jnp.bfloat16)
    return high, low


def dot(left, right):
    return jnp.dot(left, right, preferred_element_type=jnp.float32)


def rolled_taps(values, weights):
    total = weights[0] * values
    for shift, weight in enumerate(weights[1:], 1):
        total = total + weight * pltpu.roll(values, shift, 1)
    return total


def widened(flat):
    count, every = flat.shape
    rest = jnp.concatenate([flat, jnp.zeros((8 - count, every), jnp.float32)], axis=0)
    parts = []
    for _ in range(3):
        part = rest.astype(jnp.bfloat16)
        rest = rest - part.astype(jnp.float32)
        parts.append(part.astype(jnp.float32))
    shape = (8, count * LANES)
    tap = lax.broadcasted_iota(jnp.int32, shape, 0) * LANES
    lane = lax.broadcasted_iota(jnp.int32, shape, 1)
    ones = jnp.where((lane >= tap) & (lane < tap + LANES), 1.0, 0.0)
    left = jnp.concatenate(parts, axis=0).T.astype(jnp.bfloat16)
    return dot(left, jnp.concatenate([ones] * 3, axis=0).astype(jnp.bfloat16))


def tap_tiles(wide_ref, stream, rows):
    return [wide_ref[stream, rows, at : at + LANES] for at in range(0, wide_ref.shape[2], LANES)]


def in_hbm(*arrays):
    return [pltpu.with_memory_space_constraint(array, pltpu.HBM) for array in arrays]


def tables_kernel(count, *refs):
    sources, skip_ref = refs[:count], refs[count]
    outs, column_ref = refs[count + 2 : 2 * count + 2], refs[2 * count + 2]
    skips, sems = refs[2 * count + 3 :]
    moves = [
        pltpu.make_async_copy(source, out, sems.at[index])
        for index, (source, out) in enumerate(zip(sources, outs))
    ]
    moves.append(pltpu.make_async_copy(skip_ref, skips, sems.at[count]))
    for move in moves:
        move.start()
    moves[count].wait()
    column_ref[...] = jnp.broadcast_to(skips[...].reshape(1, -1), (LANES, skips.shape[0])).T
    for move in moves[:count]:
        move.wait()


def near_tables(rows, skip_gain, out_weight, after):
    tables = [out_weight] + [jnp.asarray(table) for table in dft_tables(rows)]
    count = len(tables)
    far = pl.BlockSpec(memory_space=pltpu.HBM)
    near = pl.BlockSpec(memory_space=pltpu.VMEM)
    return pl.pallas_call(
        lambda *refs: tables_kernel(count, *refs),
        out_shape=[jax.ShapeDtypeStruct(table.shape, table.dtype) for table in tables]
        + [jax.ShapeDtypeStruct((skip_gain.shape[0], LANES), jnp.float32)],
        in_specs=[far] * (count + 1) + [near],
        out_specs=[near] * (count + 1),
        scratch_shapes=[
            pltpu.VMEM(skip_gain.shape, jnp.float32),
            pltpu.SemaphoreType.DMA((count + 1,)),
        ],
        compiler_params=pltpu.CompilerParams(vmem_limit_bytes=16 << 20),
        name="near_tables",
    )(*in_hbm(*tables, skip_gain), after)


def pack_kernel(nodes, chans, qkv_ref, filter_ref, flat_ref, *refs):
    outs = refs[:nodes]
    query_ref, wide_ref = refs[nodes : nodes + 2]
    filters, streams, flat, sems = refs[nodes + 2 :]
    place = lax.axis_index("ctx")
    block = qkv_ref.shape[2]
    rim = flat_ref.shape[1] - 1
    shares = [
        pl.ds(pl.multiple_of((place ^ mask) * chans, chans), chans) for mask in range(nodes)
    ]
    flat_move = pltpu.make_async_copy(flat_ref, flat, sems.at[0])
    query_move = pltpu.make_async_copy(qkv_ref.at[0], query_ref, sems.at[1])
    filter_move = pltpu.make_async_copy(filter_ref, filters, sems.at[2])
    stream_move = pltpu.make_async_copy(qkv_ref.at[pl.ds(1, 2)], streams, sems.at[3])
    for move in (flat_move, stream_move, query_move, filter_move):
        move.start()
    lane = lax.broadcasted_iota(jnp.int32, (chans, LANES), 1)

    flat_move.wait()
    for stream in range(3):
        wide_ref[stream] = widened(flat[stream])
    query_move.wait()
    edges = jnp.zeros((chans, LANES), jnp.float32)
    for share in range(nodes):
        tile = query_ref[share * chans : (share + 1) * chans, block - LANES :]
        moved = pltpu.roll(tile.astype(jnp.float32), LANE_Q + (share + 1) * rim, 1)
        edges = jnp.where(lane >= LANE_Q + share * rim, moved, edges)
    stream_move.wait()
    for mask, rows in reversed(list(enumerate(shares))):
        edge = edges
        raws = [streams[stream, rows, :] for stream in range(2)]
        wides = [tap_tiles(wide_ref, 1 + stream, rows) for stream in range(2)]
        for stream in reversed(range(2)):
            ends = jnp.where(lane < rim, raws[stream][:, :LANES], raws[stream][:, block - LANES :])
            at = stream * LANE_V
            moved = pltpu.roll(ends, at + rim, 1).astype(jnp.float32)
            edge = jnp.where(lane < at + LANE_V, moved, edge)
        outs[mask][:, 2 * block :] = edge.astype(jnp.bfloat16)
        before = [None, None]
        for index in range(block // LANES):
            product = None
            for stream in range(2):
                tile = raws[stream][:, index * LANES : (index + 1) * LANES]
                wide = wides[stream]
                moved = [pltpu.roll(tile, shift, 1) for shift in range(1, rim + 1)]
                behind = before[stream] or moved
                total = wide[0] * tile.astype(jnp.float32)
                for shift in range(1, rim + 1):
                    joined = jnp.where(lane < shift, behind[shift - 1], moved[shift - 1])
                    total = total + wide[shift] * joined.astype(jnp.float32)
                before[stream] = moved
                product = total if product is None else product * total
            outs[mask][:, index * LANES : (index + 1) * LANES] = product.astype(jnp.bfloat16)
    filter_move.wait()
    for mask, rows in enumerate(shares):
        outs[mask][:, block : 2 * block] = filters[rows, :].astype(jnp.bfloat16)


def pack(qkv, long_filter, short_taps, nodes, chans):
    _, every, block = qkv.shape
    far = pl.BlockSpec(memory_space=pltpu.HBM)
    near = pl.BlockSpec(memory_space=pltpu.VMEM)
    flat = jnp.swapaxes(short_taps, 1, 2)
    *pieces, query, wide = pl.pallas_call(
        lambda *refs: pack_kernel(nodes, chans, *refs),
        out_shape=[jax.ShapeDtypeStruct((chans, 2 * block + LANES), jnp.bfloat16)] * nodes
        + [
            jax.ShapeDtypeStruct((every, block), jnp.bfloat16),
            jax.ShapeDtypeStruct((3, every, short_taps.shape[2] * LANES), jnp.float32),
        ],
        in_specs=[far] * 3,
        out_specs=[near] * (nodes + 2),
        scratch_shapes=[
            pltpu.VMEM((every, block), jnp.float32),
            pltpu.VMEM((2, every, block), jnp.bfloat16),
            pltpu.VMEM(flat.shape, jnp.float32),
            pltpu.SemaphoreType.DMA((4,)),
        ],
        compiler_params=pltpu.CompilerParams(vmem_limit_bytes=16 << 20),
        name="pack",
    )(*in_hbm(qkv, long_filter, flat))
    return pieces, query, wide


def query_kernel(nodes, query_ref, wide_ref, *refs):
    pieces = refs[:nodes]
    out_ref = refs[nodes]
    place = lax.axis_index("ctx")
    _, chans, block = out_ref.shape
    rim = wide_ref.shape[2] // LANES - 1
    lane = lax.broadcasted_iota(jnp.int32, (chans, LANES), 1)
    edge = jnp.zeros((chans, LANES), jnp.float32)
    for mask in range(1, nodes):
        before = (place ^ mask) == place - 1
        found = pieces[mask][:, pieces[mask].shape[1] - LANES :].astype(jnp.float32)
        edge = jnp.where(before, found, edge)
    for mask in range(nodes):
        share = place ^ mask
        rows = pl.ds(pl.multiple_of(share * chans, chans), chans)
        weights = [tile[:, :1] for tile in tap_tiles(wide_ref, 0, rows)]
        values = query_ref[rows, :].astype(jnp.float32)
        history = pltpu.roll(edge, LANES - LANE_Q - (share + 1) * rim, 1)
        first = weights[0] * values[:, :LANES]
        for shift in range(1, rim + 1):
            joined = jnp.where(lane >= LANES - shift, history, values[:, :LANES])
            first = first + weights[shift] * pltpu.roll(joined, shift, 1)
        out_ref[nodes - 1 - mask] = rolled_taps(values, weights)
        out_ref[nodes - 1 - mask, :, :LANES] = first


def query_features(query, wide, pieces, nodes, chans):
    near = pl.BlockSpec(memory_space=pltpu.VMEM)
    return pl.pallas_call(
        lambda *refs: query_kernel(nodes, *refs),
        out_shape=jax.ShapeDtypeStruct((nodes, chans, query.shape[1]), jnp.float32),
        in_specs=[near] * (2 + nodes),
        out_specs=near,
        compiler_params=pltpu.CompilerParams(vmem_limit_bytes=16 << 20),
        name="query_features",
    )(query, wide, *pieces)


def long_kernel(
    nodes, chans, per_node, rim, wide_ref, first_ref, twist_ref, second_ref, last_ref, skip_ref, *refs
):
    pieces = refs[:nodes][::-1]
    outs = refs[nodes : 2 * nodes]
    raw, edges, final = refs[2 * nodes :]
    rows = nodes * per_node
    pitch = rows + PAD
    place = lax.axis_index("ctx")
    base = place * chans
    block = per_node * LANES

    if rim:
        lane = lax.broadcasted_iota(jnp.int32, (chans, LANES), 1)
        own = pl.ds(pl.multiple_of(base, chans), chans)
        edges[0] = jnp.zeros((chans, LANES), jnp.bfloat16)
        for mask in range(nodes):
            edges[(place ^ mask) + 1] = pieces[mask][:, 2 * block :]
        wide = [tap_tiles(wide_ref, 1 + stream, own) for stream in range(2)]

    def repaired(mask, tile):
        before, now = edges[place ^ mask], pieces[mask][:, 2 * block :]
        product = None
        for stream in range(2):
            back = (LANES - stream * LANE_V) % LANES
            joined = jnp.where(lane < stream * LANE_V + rim, before, now)
            if back:
                joined = pltpu.roll(joined, back, 1)
            featured = wide[stream][0] * joined.astype(jnp.float32)
            for shift in range(1, rim + 1):
                moved = pltpu.roll(joined, shift, 1).astype(jnp.float32)
                featured = featured + wide[stream][shift] * moved
            product = featured if product is None else product * featured
        product = pltpu.roll(product, LANES - rim, 1).astype(jnp.bfloat16).astype(jnp.float32)
        return jnp.where(lane < rim, product, tile)

    for part in reversed(range(2)):
        for mask in range(nodes):
            start = (place ^ mask) * per_node
            for tile in range(per_node):
                at = part * block + tile * LANES
                values = pieces[mask][:, at : at + LANES].astype(jnp.float32)
                if rim and at == 0:
                    values = repaired(mask, values)
                raw[part, pl.ds(start + tile, chans, stride=pitch), :] = values

    cos_twist = twist_ref[:, :LANES]
    sin_twist = twist_ref[:, LANES:]
    skips = skip_ref[pl.ds(pl.multiple_of(base, chans), chans), :]

    def inner(parts):
        high, low = halves(jnp.concatenate(parts, axis=0))
        return dot(jnp.concatenate([high, low, high], axis=1), second_ref[...])

    def turn(real, imag, axis):
        return jnp.concatenate(
            [real * cos_twist + imag * sin_twist, imag * cos_twist - real * sin_twist], axis=axis
        )

    spectra = [[], []]
    for chan in range(chans):
        span = slice(chan * pitch, chan * pitch + rows)
        both = jnp.concatenate([raw[0, span, :], raw[1, span, :]], axis=1).astype(jnp.bfloat16)
        section = dot(first_ref[...], jnp.concatenate([both, both], axis=0))
        for part in range(2):
            cols = slice(part * LANES, (part + 1) * LANES)
            spectra[part].append(turn(section[:rows, cols], section[rows:, cols], 1))
    spectra = spectra[0] + spectra[1]
    fil_spec = inner(spectra[chans:])
    sig_spec = inner(spectra[:chans])
    def product(chan):
        sig = sig_spec[chan * rows : (chan + 1) * rows, :]
        fil = fil_spec[chan * rows : (chan + 1) * rows, :]
        sig_real, sig_imag = sig[:, :LANES], sig[:, LANES:]
        fil_real, fil_imag = fil[:, :LANES], fil[:, LANES:]
        return jnp.concatenate(
            [
                sig_real * fil_real - sig_imag * fil_imag,
                -(sig_real * fil_imag + sig_imag * fil_real),
            ],
            axis=1,
        )

    group = max(chans // 4, 1)
    groups = [range(begin, begin + group) for begin in range(0, chans, group)]
    turned = []
    for members in groups:
        back = inner([product(chan) for chan in members])
        for index in range(group):
            at = slice(index * rows, (index + 1) * rows)
            turned.append(turn(back[at, :LANES], back[at, LANES:], 0))
    for members in groups:
        high, low = halves(jnp.concatenate([turned[chan] for chan in members], axis=1))
        convolved = dot(last_ref[...], jnp.concatenate([high, low, high], axis=0))
        for index, chan in enumerate(members):
            span = slice(chan * pitch, chan * pitch + rows)
            final[span, :] = (
                convolved[:, index * LANES : (index + 1) * LANES]
                + skips[chan : chan + 1, :] * raw[0, span, :]
            )
    for mask in range(nodes):
        start = (place ^ mask) * per_node
        for tile in range(per_node):
            outs[mask][:, tile * LANES : (tile + 1) * LANES] = final[
                pl.ds(start + tile, chans, stride=pitch), :
            ].astype(jnp.bfloat16)


def long_mix(pieces, wide, tables, block):
    nodes = len(pieces)
    chans, width = pieces[0].shape
    per_node = block // LANES
    rows = nodes * per_node
    rim = wide.shape[2] // LANES - 1 if width > 2 * block else 0
    near = pl.BlockSpec(memory_space=pltpu.VMEM)
    return pl.pallas_call(
        lambda *refs: long_kernel(nodes, chans, per_node, rim, *refs),
        out_shape=[jax.ShapeDtypeStruct((chans, block), jnp.bfloat16)] * nodes,
        in_specs=[near] * (1 + len(tables) + nodes),
        out_specs=[near] * nodes,
        scratch_shapes=[
            pltpu.VMEM((2, (chans + 1) * (rows + PAD), LANES), jnp.float32),
            pltpu.VMEM((nodes + 1, chans, LANES), jnp.bfloat16),
            pltpu.VMEM(((chans + 1) * (rows + PAD), LANES), jnp.float32),
        ],
        compiler_params=pltpu.CompilerParams(vmem_limit_bytes=24 << 20),
        name="long_mix",
    )(wide, *tables, *pieces[::-1])


def gather_blocks(depths, blocks, gathered):
    place = lax.axis_index("ctx")
    spot = lax.axis_index("ch")
    level, core = spot // 2, spot % 2
    for index, block in enumerate(blocks):
        nodes, chans, _ = block.shape
        side = core ^ (index % 2)
        for mask in range(nodes):
            row = ((2 * (index // 2) + side) * nodes + (place ^ mask)) * chans
            gathered[pl.ds(pl.multiple_of(row, chans), chans), :] = block[nodes - 1 - mask]
    width = 2 * nodes * chans
    return [pl.ds(pl.multiple_of((level ^ depth) * width, width), width) for depth in depths]


def partial_kernel(depths, rows, weight_ref, *refs):
    blocks = refs[: 2 * len(depths)]
    out_ref, gathered = refs[2 * len(depths) :]
    columns = gather_blocks(depths, blocks, gathered)
    for begin in range(0, out_ref.shape[0], rows):
        weight = jnp.concatenate([weight_ref[begin : begin + rows, at] for at in columns], axis=1)
        out_ref[begin : begin + rows, :] = dot(weight, gathered[...])


def final_kernel(depths, cuts, weight_ref, partial_ref, *refs):
    blocks = refs[: 2 * len(depths)]
    out_ref, gathered, held, sems = refs[2 * len(depths) :]
    columns = gather_blocks(depths, blocks, gathered)
    copies = []
    for part, (begin, end) in enumerate(zip(cuts, cuts[1:])):
        weight = jnp.concatenate([weight_ref[begin:end, at] for at in columns], axis=1)
        total = partial_ref[begin:end, :] + dot(weight, gathered[...])
        held[begin:end, :] = total.astype(jnp.bfloat16)
        rows = pl.ds(begin, end - begin)
        copies.append(
            pltpu.make_async_copy(held.at[rows, :], out_ref.at[rows, :], sems.at[part])
        )
        copies[-1].start()
    for copy in copies:
        copy.wait()


def project_early(early, out_weight):
    features, _ = out_weight.shape
    near = pl.BlockSpec(memory_space=pltpu.VMEM)
    blocks = [block for pair in early.values() for block in pair]
    nodes, chans, block = blocks[0].shape
    depth = nodes * chans * len(blocks)
    cost = pl.CostEstimate(
        flops=0, bytes_accessed=0, transcendentals=0
    )
    return pl.pallas_call(
        lambda *refs: partial_kernel(tuple(early), features // 4, *refs),
        out_shape=jax.ShapeDtypeStruct((features, block), jnp.float32),
        in_specs=[near] * (1 + len(blocks)),
        out_specs=near,
        scratch_shapes=[pltpu.VMEM((depth, block), jnp.bfloat16)],
        compiler_params=pltpu.CompilerParams(vmem_limit_bytes=16 << 20),
        cost_estimate=cost,
        name="project_early",
    )(out_weight, *blocks)


def project_late(partial, late, out_weight):
    features, _ = out_weight.shape
    near = pl.BlockSpec(memory_space=pltpu.VMEM)
    blocks = [block for pair in late.values() for block in pair]
    nodes, chans, block = blocks[0].shape
    depth = nodes * chans * len(blocks)
    cuts = tuple(range(0, features + 1, features // 8))
    return pl.pallas_call(
        lambda *refs: final_kernel(tuple(late), cuts, *refs),
        out_shape=jax.ShapeDtypeStruct((features, block), jnp.bfloat16),
        in_specs=[near] * (2 + len(blocks)),
        out_specs=pl.BlockSpec(memory_space=pl.ANY),
        scratch_shapes=[
            pltpu.VMEM((depth, block), jnp.bfloat16),
            pltpu.VMEM((features, block), jnp.bfloat16),
            pltpu.SemaphoreType.DMA((len(cuts) - 1,)),
        ],
        compiler_params=pltpu.CompilerParams(vmem_limit_bytes=16 << 20),
        name="project_late",
    )(out_weight, partial, *blocks)


def project_plain(blocks, out_weight):
    nodes, chans, block = blocks[0].shape
    stacks = len(blocks) // 2
    place = lax.axis_index("ctx")
    spot = lax.axis_index("ch")
    found = jnp.stack(blocks).reshape(2, stacks, nodes, chans, block)
    index = jnp.arange(2 * stacks, dtype=jnp.int32) ^ spot
    found = found[index % 2, index // 2]
    found = found[:, nodes - 1 - (jnp.arange(nodes, dtype=jnp.int32) ^ place)]
    summed = jnp.dot(
        out_weight, found.reshape(-1, block), preferred_element_type=jnp.float32
    )
    return summed.astype(jnp.bfloat16)


def features_plain(qkv, short_taps):
    block = qkv.shape[2]
    tap_count = short_taps.shape[2]
    devices = lax.axis_size("ctx")
    route = [(i, i + 1) for i in range(devices - 1)]
    history = lax.ppermute(qkv[:, :, block - (tap_count - 1) :], "ctx", route)
    extended = jnp.concatenate([history, qkv], axis=2).astype(jnp.float32)
    result = jnp.zeros(qkv.shape, jnp.float32)
    for offset in range(tap_count):
        begin = tap_count - 1 - offset
        result = (
            result
            + short_taps[:, :, offset : offset + 1] * extended[:, :, begin : begin + block]
        )
    return result


def swapped(block, mask, axis):
    if mask == 0:
        return block
    return lax.ppermute(block, axis, [(i, i ^ mask) for i in range(lax.axis_size(axis))])


def local(qkv, short_taps, long_filter, skip_gain, out_weight):
    nodes = lax.axis_size("ctx")
    spread = lax.axis_size("ch")
    stacks = spread // 2
    place = lax.axis_index("ctx")
    _, every, block = qkv.shape
    chans = every // nodes
    fits = chans % 16 == 0

    if fits:
        pieces, query, wide = pack(qkv, long_filter, short_taps, nodes, chans)
    else:
        wide = short_taps
        query, key, value = features_plain(qkv, short_taps)
        both = jnp.concatenate([key * value, long_filter], axis=1).astype(jnp.bfloat16)
        both = both.reshape(nodes, chans, 2 * block)
        pieces = [lax.dynamic_index_in_dim(both, place ^ mask, 0, False) for mask in range(nodes)]
    pieces = [swapped(pieces[mask], mask, "ctx") for mask in range(nodes)]
    out_weight, *tables = near_tables(
        nodes * block // LANES, skip_gain, out_weight, pieces[0]
    )
    mixed = long_mix(pieces, wide, tables, block)

    if fits:
        tied = lax.optimization_barrier((mixed[0], *pieces[::-1]))[:0:-1]
        featured = query_features(query, wide, tied, nodes, chans)
    else:
        featured = query.reshape(nodes, chans, block)[jnp.arange(nodes, dtype=jnp.int32) ^ place][::-1]
    mixed = [swapped(mixed[mask], mask, "ctx") for mask in range(nodes)]
    mixed = jnp.stack(mixed[::-1])
    gated = (featured * mixed.astype(jnp.float32)).astype(jnp.bfloat16)

    column = [swapped(gated, 2 * depth, "ch") for depth in range(stacks)]
    if not fits:
        return project_plain(column + [swapped(part, 1, "ch") for part in column], out_weight)
    pairs = {depth: (part, swapped(part, 1, "ch")) for depth, part in enumerate(column)}
    late = {depth: pairs.pop(depth) for depth in (3, 1)}
    return project_late(project_early(pairs, out_weight), late, out_weight)


def solution(mesh):
    placed = (P(None, "ch", "ctx"), P(None, "ch", None), P("ch", "ctx"), P("ch"), P("ch", None))
    return jax.shard_map(
        local, mesh=mesh, in_specs=placed, out_specs=P("ch", "ctx"), check_vma=False
    )
```

```python
import math

import numpy as np

import jax
import jax.numpy as jnp
from jax import lax
from jax.experimental import pallas as pl
from jax.experimental.pallas import tpu as pltpu
from jax.sharding import PartitionSpec as P

LANES = 128
PAD = 8
LANE_V = 16
LANE_Q = 32


def split_table(table):
    high = table.astype(jnp.bfloat16)
    low = (table - high.astype(np.float64)).astype(jnp.bfloat16)
    return high, low


def dft_tables(rows):
    total = 2 * rows * LANES
    block = np.arange(rows, dtype=np.float64)
    freq = np.arange(rows, dtype=np.float64) + 0.5
    lane = np.arange(LANES, dtype=np.float64)
    head = 2.0 * math.pi * np.outer(freq, block) / (2 * rows)
    first = np.concatenate(
        split_table(np.concatenate([np.cos(head), -np.sin(head)], axis=0)), axis=1
    )
    turn = 2.0 * math.pi * np.outer(freq, lane) / total
    twist = np.concatenate([np.cos(turn), np.sin(turn)], axis=1).astype(np.float32)
    inner = 2.0 * math.pi * np.outer(lane, lane) / LANES
    square = np.block([[np.cos(inner), -np.sin(inner)], [np.sin(inner), np.cos(inner)]])
    square_high, square_low = split_table(square)
    second = np.concatenate([square_high, square_high, square_low], axis=0)
    tail = head.T
    tail_high, tail_low = split_table(
        (2.0 / total) * np.concatenate([np.cos(tail), np.sin(tail)], axis=1)
    )
    last = np.concatenate([tail_high, tail_high, tail_low], axis=1)
    return first, twist, second, last


def halves(value):
    high = value.astype(jnp.bfloat16)
    low = (value - high.astype(jnp.float32)).astype(jnp.bfloat16)
    return high, low


def dot(left, right):
    return jnp.dot(left, right, preferred_element_type=jnp.float32)


def rolled_taps(values, weights):
    total = weights[0] * values
    for shift, weight in enumerate(weights[1:], 1):
        total = total + weight * pltpu.roll(values, shift, 1)
    return total


def widened(flat):
    count, every = flat.shape
    rest = jnp.concatenate([flat, jnp.zeros((8 - count, every), jnp.float32)], axis=0)
    parts = []
    for _ in range(3):
        part = rest.astype(jnp.bfloat16)
        rest = rest - part.astype(jnp.float32)
        parts.append(part.astype(jnp.float32))
    shape = (8, count * LANES)
    tap = lax.broadcasted_iota(jnp.int32, shape, 0) * LANES
    lane = lax.broadcasted_iota(jnp.int32, shape, 1)
    ones = jnp.where((lane >= tap) & (lane < tap + LANES), 1.0, 0.0)
    left = jnp.concatenate(parts, axis=0).T.astype(jnp.bfloat16)
    return dot(left, jnp.concatenate([ones] * 3, axis=0).astype(jnp.bfloat16))


def tap_tiles(wide_ref, stream, rows):
    return [wide_ref[stream, rows, at : at + LANES] for at in range(0, wide_ref.shape[2], LANES)]


def in_hbm(*arrays):
    return [pltpu.with_memory_space_constraint(array, pltpu.HBM) for array in arrays]


def tables_kernel(count, *refs):
    sources, skip_ref = refs[:count], refs[count]
    outs, column_ref = refs[count + 2 : 2 * count + 2], refs[2 * count + 2]
    skips, sems = refs[2 * count + 3 :]
    moves = [
        pltpu.make_async_copy(source, out, sems.at[index])
        for index, (source, out) in enumerate(zip(sources, outs))
    ]
    moves.append(pltpu.make_async_copy(skip_ref, skips, sems.at[count]))
    for move in moves:
        move.start()
    moves[count].wait()
    column_ref[...] = jnp.broadcast_to(skips[...].reshape(1, -1), (LANES, skips.shape[0])).T
    for move in moves[:count]:
        move.wait()


def near_tables(rows, skip_gain, out_weight, after):
    tables = [out_weight] + [jnp.asarray(table) for table in dft_tables(rows)]
    count = len(tables)
    far = pl.BlockSpec(memory_space=pltpu.HBM)
    near = pl.BlockSpec(memory_space=pltpu.VMEM)
    return pl.pallas_call(
        lambda *refs: tables_kernel(count, *refs),
        out_shape=[jax.ShapeDtypeStruct(table.shape, table.dtype) for table in tables]
        + [jax.ShapeDtypeStruct((skip_gain.shape[0], LANES), jnp.float32)],
        in_specs=[far] * (count + 1) + [near],
        out_specs=[near] * (count + 1),
        scratch_shapes=[
            pltpu.VMEM(skip_gain.shape, jnp.float32),
            pltpu.SemaphoreType.DMA((count + 1,)),
        ],
        compiler_params=pltpu.CompilerParams(vmem_limit_bytes=16 << 20),
        name="near_tables",
    )(*in_hbm(*tables, skip_gain), after)


def pack_kernel(nodes, chans, qkv_ref, filter_ref, flat_ref, *refs):
    outs = refs[:nodes]
    query_ref, first_ref, wide_ref = refs[nodes : nodes + 3]
    filters, streams, flat, sems = refs[nodes + 3 :]
    place = lax.axis_index("ctx")
    block = qkv_ref.shape[2]
    rim = flat_ref.shape[1] - 1
    shares = [
        pl.ds(pl.multiple_of((place ^ mask) * chans, chans), chans) for mask in range(nodes)
    ]
    flat_move = pltpu.make_async_copy(flat_ref, flat, sems.at[0])
    query_move = pltpu.make_async_copy(qkv_ref.at[0], query_ref, sems.at[1])
    filter_move = pltpu.make_async_copy(filter_ref, filters, sems.at[2])
    stream_move = pltpu.make_async_copy(qkv_ref.at[pl.ds(1, 2)], streams, sems.at[3])
    for move in (flat_move, stream_move, query_move, filter_move):
        move.start()
    lane = lax.broadcasted_iota(jnp.int32, (chans, LANES), 1)

    flat_move.wait()
    for stream in range(2):
        wide_ref[stream] = widened(flat[1 + stream])
    first_ref[...] = flat[0]
    query_move.wait()
    edges = jnp.zeros((chans, LANES), jnp.float32)
    for share in range(nodes):
        tile = query_ref[share * chans : (share + 1) * chans, block - LANES :]
        moved = pltpu.roll(tile.astype(jnp.float32), LANE_Q + (share + 1) * rim, 1)
        edges = jnp.where(lane >= LANE_Q + share * rim, moved, edges)
    stream_move.wait()
    for mask, rows in reversed(list(enumerate(shares))):
        edge = edges
        raws = [streams[stream, rows, :] for stream in range(2)]
        wides = [tap_tiles(wide_ref, stream, rows) for stream in range(2)]
        for stream in reversed(range(2)):
            ends = jnp.where(lane < rim, raws[stream][:, :LANES], raws[stream][:, block - LANES :])
            at = stream * LANE_V
            moved = pltpu.roll(ends, at + rim, 1).astype(jnp.float32)
            edge = jnp.where(lane < at + LANE_V, moved, edge)
        outs[mask][:, 2 * block :] = edge.astype(jnp.bfloat16)
        before = [None, None]
        for index in range(block // LANES):
            product = None
            for stream in range(2):
                tile = raws[stream][:, index * LANES : (index + 1) * LANES]
                wide = wides[stream]
                moved = [pltpu.roll(tile, shift, 1) for shift in range(1, rim + 1)]
                behind = before[stream] or moved
                total = wide[0] * tile.astype(jnp.float32)
                for shift in range(1, rim + 1):
                    joined = jnp.where(lane < shift, behind[shift - 1], moved[shift - 1])
                    total = total + wide[shift] * joined.astype(jnp.float32)
                before[stream] = moved
                product = total if product is None else product * total
            outs[mask][:, index * LANES : (index + 1) * LANES] = product.astype(jnp.bfloat16)
    filter_move.wait()
    for mask, rows in enumerate(shares):
        outs[mask][:, block : 2 * block] = filters[rows, :].astype(jnp.bfloat16)


def pack(qkv, long_filter, short_taps, nodes, chans):
    _, every, block = qkv.shape
    far = pl.BlockSpec(memory_space=pltpu.HBM)
    near = pl.BlockSpec(memory_space=pltpu.VMEM)
    flat = jnp.swapaxes(short_taps, 1, 2)
    *pieces, query, first, wide = pl.pallas_call(
        lambda *refs: pack_kernel(nodes, chans, *refs),
        out_shape=[jax.ShapeDtypeStruct((chans, 2 * block + LANES), jnp.bfloat16)] * nodes
        + [
            jax.ShapeDtypeStruct((every, block), jnp.bfloat16),
            jax.ShapeDtypeStruct(flat.shape[1:], jnp.float32),
            jax.ShapeDtypeStruct((2, every, short_taps.shape[2] * LANES), jnp.float32),
        ],
        in_specs=[far] * 3,
        out_specs=[near] * (nodes + 3),
        scratch_shapes=[
            pltpu.VMEM((every, block), jnp.float32),
            pltpu.VMEM((2, every, block), jnp.bfloat16),
            pltpu.VMEM(flat.shape, jnp.float32),
            pltpu.SemaphoreType.DMA((4,)),
        ],
        compiler_params=pltpu.CompilerParams(vmem_limit_bytes=16 << 20),
        name="pack",
    )(*in_hbm(qkv, long_filter, flat))
    return pieces, (query, first), wide


def query_kernel(nodes, query_ref, flat_ref, *refs):
    pieces = refs[:nodes]
    out_ref, wide_ref = refs[nodes:]
    wide_ref[0] = widened(flat_ref[...])
    place = lax.axis_index("ctx")
    _, chans, block = out_ref.shape
    rim = wide_ref.shape[2] // LANES - 1
    lane = lax.broadcasted_iota(jnp.int32, (chans, LANES), 1)
    edge = jnp.zeros((chans, LANES), jnp.float32)
    for mask in range(1, nodes):
        before = (place ^ mask) == place - 1
        found = pieces[mask][:, pieces[mask].shape[1] - LANES :].astype(jnp.float32)
        edge = jnp.where(before, found, edge)
    for mask in range(nodes):
        share = place ^ mask
        rows = pl.ds(pl.multiple_of(share * chans, chans), chans)
        weights = [tile[:, :1] for tile in tap_tiles(wide_ref, 0, rows)]
        values = query_ref[rows, :].astype(jnp.float32)
        history = pltpu.roll(edge, LANES - LANE_Q - (share + 1) * rim, 1)
        first = weights[0] * values[:, :LANES]
        for shift in range(1, rim + 1):
            joined = jnp.where(lane >= LANES - shift, history, values[:, :LANES])
            first = first + weights[shift] * pltpu.roll(joined, shift, 1)
        out_ref[nodes - 1 - mask] = rolled_taps(values, weights)
        out_ref[nodes - 1 - mask, :, :LANES] = first


def query_features(query, flat, pieces, nodes, chans):
    near = pl.BlockSpec(memory_space=pltpu.VMEM)
    return pl.pallas_call(
        lambda *refs: query_kernel(nodes, *refs),
        out_shape=jax.ShapeDtypeStruct((nodes, chans, query.shape[1]), jnp.float32),
        in_specs=[near] * (2 + nodes),
        out_specs=near,
        scratch_shapes=[pltpu.VMEM((1, flat.shape[1], flat.shape[0] * LANES), jnp.float32)],
        compiler_params=pltpu.CompilerParams(vmem_limit_bytes=16 << 20),
        name="query_features",
    )(query, flat, *pieces)


def long_kernel(
    nodes, chans, per_node, rim, wide_ref, first_ref, twist_ref, second_ref, last_ref, skip_ref, *refs
):
    pieces = refs[:nodes][::-1]
    outs = refs[nodes : 2 * nodes]
    raw, edges, final = refs[2 * nodes :]
    rows = nodes * per_node
    pitch = rows + PAD
    place = lax.axis_index("ctx")
    base = place * chans
    block = per_node * LANES

    if rim:
        lane = lax.broadcasted_iota(jnp.int32, (chans, LANES), 1)
        own = pl.ds(pl.multiple_of(base, chans), chans)
        edges[0] = jnp.zeros((chans, LANES), jnp.bfloat16)
        for mask in range(nodes):
            edges[(place ^ mask) + 1] = pieces[mask][:, 2 * block :]
        wide = [tap_tiles(wide_ref, stream, own) for stream in range(2)]

    def repaired(mask, tile):
        before, now = edges[place ^ mask], pieces[mask][:, 2 * block :]
        product = None
        for stream in range(2):
            back = (LANES - stream * LANE_V) % LANES
            joined = jnp.where(lane < stream * LANE_V + rim, before, now)
            if back:
                joined = pltpu.roll(joined, back, 1)
            featured = wide[stream][0] * joined.astype(jnp.float32)
            for shift in range(1, rim + 1):
                moved = pltpu.roll(joined, shift, 1).astype(jnp.float32)
                featured = featured + wide[stream][shift] * moved
            product = featured if product is None else product * featured
        product = pltpu.roll(product, LANES - rim, 1).astype(jnp.bfloat16).astype(jnp.float32)
        return jnp.where(lane < rim, product, tile)

    for part in reversed(range(2)):
        for mask in range(nodes):
            start = (place ^ mask) * per_node
            for tile in range(per_node):
                at = part * block + tile * LANES
                values = pieces[mask][:, at : at + LANES].astype(jnp.float32)
                if rim and at == 0:
                    values = repaired(mask, values)
                raw[part, pl.ds(start + tile, chans, stride=pitch), :] = values

    cos_twist = twist_ref[:, :LANES]
    sin_twist = twist_ref[:, LANES:]
    skips = skip_ref[pl.ds(pl.multiple_of(base, chans), chans), :]

    def inner(parts):
        high, low = halves(jnp.concatenate(parts, axis=0))
        return dot(jnp.concatenate([high, low, high], axis=1), second_ref[...])

    def turn(real, imag, axis):
        return jnp.concatenate(
            [real * cos_twist + imag * sin_twist, imag * cos_twist - real * sin_twist], axis=axis
        )

    spectra = [[], []]
    for chan in range(chans):
        span = slice(chan * pitch, chan * pitch + rows)
        both = jnp.concatenate([raw[0, span, :], raw[1, span, :]], axis=1).astype(jnp.bfloat16)
        section = dot(first_ref[...], jnp.concatenate([both, both], axis=0))
        for part in range(2):
            cols = slice(part * LANES, (part + 1) * LANES)
            spectra[part].append(turn(section[:rows, cols], section[rows:, cols], 1))
    spectra = spectra[0] + spectra[1]
    fil_spec = inner(spectra[chans:])
    sig_spec = inner(spectra[:chans])
    def product(chan):
        sig = sig_spec[chan * rows : (chan + 1) * rows, :]
        fil = fil_spec[chan * rows : (chan + 1) * rows, :]
        sig_real, sig_imag = sig[:, :LANES], sig[:, LANES:]
        fil_real, fil_imag = fil[:, :LANES], fil[:, LANES:]
        return jnp.concatenate(
            [
                sig_real * fil_real - sig_imag * fil_imag,
                -(sig_real * fil_imag + sig_imag * fil_real),
            ],
            axis=1,
        )

    group = max(chans // 4, 1)
    groups = [range(begin, begin + group) for begin in range(0, chans, group)]
    turned = []
    for members in groups:
        back = inner([product(chan) for chan in members])
        for index in range(group):
            at = slice(index * rows, (index + 1) * rows)
            turned.append(turn(back[at, :LANES], back[at, LANES:], 0))
    for members in groups:
        high, low = halves(jnp.concatenate([turned[chan] for chan in members], axis=1))
        convolved = dot(last_ref[...], jnp.concatenate([high, low, high], axis=0))
        for index, chan in enumerate(members):
            span = slice(chan * pitch, chan * pitch + rows)
            final[span, :] = (
                convolved[:, index * LANES : (index + 1) * LANES]
                + skips[chan : chan + 1, :] * raw[0, span, :]
            )
    for mask in range(nodes):
        start = (place ^ mask) * per_node
        for tile in range(per_node):
            outs[mask][:, tile * LANES : (tile + 1) * LANES] = final[
                pl.ds(start + tile, chans, stride=pitch), :
            ].astype(jnp.bfloat16)


def long_mix(pieces, wide, tables, block):
    nodes = len(pieces)
    chans, width = pieces[0].shape
    per_node = block // LANES
    rows = nodes * per_node
    rim = wide.shape[2] // LANES - 1 if width > 2 * block else 0
    near = pl.BlockSpec(memory_space=pltpu.VMEM)
    return pl.pallas_call(
        lambda *refs: long_kernel(nodes, chans, per_node, rim, *refs),
        out_shape=[jax.ShapeDtypeStruct((chans, block), jnp.bfloat16)] * nodes,
        in_specs=[near] * (1 + len(tables) + nodes),
        out_specs=[near] * nodes,
        scratch_shapes=[
            pltpu.VMEM((2, (chans + 1) * (rows + PAD), LANES), jnp.float32),
            pltpu.VMEM((nodes + 1, chans, LANES), jnp.bfloat16),
            pltpu.VMEM(((chans + 1) * (rows + PAD), LANES), jnp.float32),
        ],
        compiler_params=pltpu.CompilerParams(vmem_limit_bytes=24 << 20),
        name="long_mix",
    )(wide, *tables, *pieces[::-1])


def gather_blocks(depths, blocks, gathered):
    place = lax.axis_index("ctx")
    spot = lax.axis_index("ch")
    level, core = spot // 2, spot % 2
    for index, block in enumerate(blocks):
        nodes, chans, _ = block.shape
        side = core ^ (index % 2)
        for mask in range(nodes):
            row = ((2 * (index // 2) + side) * nodes + (place ^ mask)) * chans
            gathered[pl.ds(pl.multiple_of(row, chans), chans), :] = block[nodes - 1 - mask]
    width = 2 * nodes * chans
    return [pl.ds(pl.multiple_of((level ^ depth) * width, width), width) for depth in depths]


def partial_kernel(depths, rows, weight_ref, *refs):
    blocks = refs[: 2 * len(depths)]
    out_ref, gathered = refs[2 * len(depths) :]
    columns = gather_blocks(depths, blocks, gathered)
    for begin in range(0, out_ref.shape[0], rows):
        weight = jnp.concatenate([weight_ref[begin : begin + rows, at] for at in columns], axis=1)
        out_ref[begin : begin + rows, :] = dot(weight, gathered[...])


def final_kernel(depths, cuts, weight_ref, partial_ref, *refs):
    blocks = refs[: 2 * len(depths)]
    out_ref, gathered, held, sems = refs[2 * len(depths) :]
    columns = gather_blocks(depths, blocks, gathered)
    copies = []
    for part, (begin, end) in enumerate(zip(cuts, cuts[1:])):
        weight = jnp.concatenate([weight_ref[begin:end, at] for at in columns], axis=1)
        total = partial_ref[begin:end, :] + dot(weight, gathered[...])
        held[begin:end, :] = total.astype(jnp.bfloat16)
        rows = pl.ds(begin, end - begin)
        copies.append(
            pltpu.make_async_copy(held.at[rows, :], out_ref.at[rows, :], sems.at[part])
        )
        copies[-1].start()
    for copy in copies:
        copy.wait()


def project_early(early, out_weight):
    features, _ = out_weight.shape
    near = pl.BlockSpec(memory_space=pltpu.VMEM)
    blocks = [block for pair in early.values() for block in pair]
    nodes, chans, block = blocks[0].shape
    depth = nodes * chans * len(blocks)
    cost = pl.CostEstimate(
        flops=0, bytes_accessed=0, transcendentals=0
    )
    return pl.pallas_call(
        lambda *refs: partial_kernel(tuple(early), features // 4, *refs),
        out_shape=jax.ShapeDtypeStruct((features, block), jnp.float32),
        in_specs=[near] * (1 + len(blocks)),
        out_specs=near,
        scratch_shapes=[pltpu.VMEM((depth, block), jnp.bfloat16)],
        compiler_params=pltpu.CompilerParams(vmem_limit_bytes=16 << 20),
        cost_estimate=cost,
        name="project_early",
    )(out_weight, *blocks)


def project_late(partial, late, out_weight):
    features, _ = out_weight.shape
    near = pl.BlockSpec(memory_space=pltpu.VMEM)
    blocks = [block for pair in late.values() for block in pair]
    nodes, chans, block = blocks[0].shape
    depth = nodes * chans * len(blocks)
    cuts = tuple(range(0, features + 1, features // 8))
    return pl.pallas_call(
        lambda *refs: final_kernel(tuple(late), cuts, *refs),
        out_shape=jax.ShapeDtypeStruct((features, block), jnp.bfloat16),
        in_specs=[near] * (2 + len(blocks)),
        out_specs=pl.BlockSpec(memory_space=pl.ANY),
        scratch_shapes=[
            pltpu.VMEM((depth, block), jnp.bfloat16),
            pltpu.VMEM((features, block), jnp.bfloat16),
            pltpu.SemaphoreType.DMA((len(cuts) - 1,)),
        ],
        compiler_params=pltpu.CompilerParams(vmem_limit_bytes=16 << 20),
        name="project_late",
    )(out_weight, partial, *blocks)


def project_plain(blocks, out_weight):
    nodes, chans, block = blocks[0].shape
    stacks = len(blocks) // 2
    place = lax.axis_index("ctx")
    spot = lax.axis_index("ch")
    found = jnp.stack(blocks).reshape(2, stacks, nodes, chans, block)
    index = jnp.arange(2 * stacks, dtype=jnp.int32) ^ spot
    found = found[index % 2, index // 2]
    found = found[:, nodes - 1 - (jnp.arange(nodes, dtype=jnp.int32) ^ place)]
    summed = jnp.dot(
        out_weight, found.reshape(-1, block), preferred_element_type=jnp.float32
    )
    return summed.astype(jnp.bfloat16)


def features_plain(qkv, short_taps):
    block = qkv.shape[2]
    tap_count = short_taps.shape[2]
    devices = lax.axis_size("ctx")
    route = [(i, i + 1) for i in range(devices - 1)]
    history = lax.ppermute(qkv[:, :, block - (tap_count - 1) :], "ctx", route)
    extended = jnp.concatenate([history, qkv], axis=2).astype(jnp.float32)
    result = jnp.zeros(qkv.shape, jnp.float32)
    for offset in range(tap_count):
        begin = tap_count - 1 - offset
        result = (
            result
            + short_taps[:, :, offset : offset + 1] * extended[:, :, begin : begin + block]
        )
    return result


def swapped(block, mask, axis):
    if mask == 0:
        return block
    return lax.ppermute(block, axis, [(i, i ^ mask) for i in range(lax.axis_size(axis))])


def local(qkv, short_taps, long_filter, skip_gain, out_weight):
    nodes = lax.axis_size("ctx")
    spread = lax.axis_size("ch")
    stacks = spread // 2
    place = lax.axis_index("ctx")
    _, every, block = qkv.shape
    chans = every // nodes
    fits = chans % 16 == 0

    if fits:
        pieces, query, wide = pack(qkv, long_filter, short_taps, nodes, chans)
    else:
        wide = short_taps
        query, key, value = features_plain(qkv, short_taps)
        both = jnp.concatenate([key * value, long_filter], axis=1).astype(jnp.bfloat16)
        both = both.reshape(nodes, chans, 2 * block)
        pieces = [lax.dynamic_index_in_dim(both, place ^ mask, 0, False) for mask in range(nodes)]
    pieces = [swapped(pieces[mask], mask, "ctx") for mask in range(nodes)]
    out_weight, *tables = near_tables(
        nodes * block // LANES, skip_gain, out_weight, pieces[0]
    )
    mixed = long_mix(pieces, wide, tables, block)

    if fits:
        tied = lax.optimization_barrier((mixed[0], *pieces[::-1]))[:0:-1]
        featured = query_features(*query, tied, nodes, chans)
    else:
        featured = query.reshape(nodes, chans, block)[jnp.arange(nodes, dtype=jnp.int32) ^ place][::-1]
    mixed = [swapped(mixed[mask], mask, "ctx") for mask in range(nodes)]
    mixed = jnp.stack(mixed[::-1])
    gated = (featured * mixed.astype(jnp.float32)).astype(jnp.bfloat16)

    column = [swapped(gated, 2 * depth, "ch") for depth in range(stacks)]
    if not fits:
        return project_plain(column + [swapped(part, 1, "ch") for part in column], out_weight)
    pairs = {depth: (part, swapped(part, 1, "ch")) for depth, part in enumerate(column)}
    late = {depth: pairs.pop(depth) for depth in (3, 1)}
    return project_late(project_early(pairs, out_weight), late, out_weight)


def solution(mesh):
    placed = (P(None, "ch", "ctx"), P(None, "ch", None), P("ch", "ctx"), P("ch"), P("ch", None))
    return jax.shard_map(
        local, mesh=mesh, in_specs=placed, out_specs=P("ch", "ctx"), check_vma=False
    )
```

```python
import math

import numpy as np

import jax
import jax.numpy as jnp
from jax import lax
from jax.experimental import pallas as pl
from jax.experimental.pallas import tpu as pltpu
from jax.sharding import PartitionSpec as P

LANES = 128
PAD = 8
LANE_V = 16
LANE_Q = 32


def split_table(table):
    high = table.astype(jnp.bfloat16)
    low = (table - high.astype(np.float64)).astype(jnp.bfloat16)
    return high, low


def dft_tables(rows):
    total = 2 * rows * LANES
    block = np.arange(rows, dtype=np.float64)
    freq = np.arange(rows, dtype=np.float64) + 0.5
    lane = np.arange(LANES, dtype=np.float64)
    head = 2.0 * math.pi * np.outer(freq, block) / (2 * rows)
    first = np.concatenate(
        split_table(np.concatenate([np.cos(head), -np.sin(head)], axis=0)), axis=1
    )
    turn = 2.0 * math.pi * np.outer(freq, lane) / total
    twist = np.concatenate([np.cos(turn), np.sin(turn)], axis=1).astype(np.float32)
    inner = 2.0 * math.pi * np.outer(lane, lane) / LANES
    square = np.block([[np.cos(inner), -np.sin(inner)], [np.sin(inner), np.cos(inner)]])
    square_high, square_low = split_table(square)
    second = np.concatenate([square_high, square_high, square_low], axis=0)
    tail = head.T
    tail_high, tail_low = split_table(
        (2.0 / total) * np.concatenate([np.cos(tail), np.sin(tail)], axis=1)
    )
    last = np.concatenate([tail_high, tail_high, tail_low], axis=1)
    return first, twist, second, last


def halves(value):
    high = value.astype(jnp.bfloat16)
    low = (value - high.astype(jnp.float32)).astype(jnp.bfloat16)
    return high, low


def dot(left, right):
    return jnp.dot(left, right, preferred_element_type=jnp.float32)


def rolled_taps(values, weights):
    total = weights[0] * values
    for shift, weight in enumerate(weights[1:], 1):
        total = total + weight * pltpu.roll(values, shift, 1)
    return total


def widened(flat):
    count, every = flat.shape
    rest = jnp.concatenate([flat, jnp.zeros((8 - count, every), jnp.float32)], axis=0)
    parts = []
    for _ in range(3):
        part = rest.astype(jnp.bfloat16)
        rest = rest - part.astype(jnp.float32)
        parts.append(part.astype(jnp.float32))
    shape = (8, count * LANES)
    tap = lax.broadcasted_iota(jnp.int32, shape, 0) * LANES
    lane = lax.broadcasted_iota(jnp.int32, shape, 1)
    ones = jnp.where((lane >= tap) & (lane < tap + LANES), 1.0, 0.0)
    left = jnp.concatenate(parts, axis=0).T.astype(jnp.bfloat16)
    return dot(left, jnp.concatenate([ones] * 3, axis=0).astype(jnp.bfloat16))


def tap_tiles(wide_ref, stream, rows):
    return [wide_ref[stream, rows, at : at + LANES] for at in range(0, wide_ref.shape[2], LANES)]


def in_hbm(*arrays):
    return [pltpu.with_memory_space_constraint(array, pltpu.HBM) for array in arrays]


def tables_kernel(count, *refs):
    sources, skip_ref = refs[:count], refs[count]
    outs, column_ref = refs[count + 2 : 2 * count + 2], refs[2 * count + 2]
    skips, sems = refs[2 * count + 3 :]
    moves = [
        pltpu.make_async_copy(source, out, sems.at[index])
        for index, (source, out) in enumerate(zip(sources, outs))
    ]
    moves.append(pltpu.make_async_copy(skip_ref, skips, sems.at[count]))
    for move in moves:
        move.start()
    moves[count].wait()
    column_ref[...] = jnp.broadcast_to(skips[...].reshape(1, -1), (LANES, skips.shape[0])).T
    for move in moves[:count]:
        move.wait()


def near_tables(rows, skip_gain, out_weight, after):
    tables = [out_weight] + [jnp.asarray(table) for table in dft_tables(rows)]
    count = len(tables)
    far = pl.BlockSpec(memory_space=pltpu.HBM)
    near = pl.BlockSpec(memory_space=pltpu.VMEM)
    return pl.pallas_call(
        lambda *refs: tables_kernel(count, *refs),
        out_shape=[jax.ShapeDtypeStruct(table.shape, table.dtype) for table in tables]
        + [jax.ShapeDtypeStruct((skip_gain.shape[0], LANES), jnp.float32)],
        in_specs=[far] * (count + 1) + [near],
        out_specs=[near] * (count + 1),
        scratch_shapes=[
            pltpu.VMEM(skip_gain.shape, jnp.float32),
            pltpu.SemaphoreType.DMA((count + 1,)),
        ],
        compiler_params=pltpu.CompilerParams(vmem_limit_bytes=16 << 20),
        name="near_tables",
    )(*in_hbm(*tables, skip_gain), after)


def pack_kernel(nodes, chans, qkv_ref, filter_ref, flat_ref, *refs):
    outs = refs[:nodes]
    query_ref, first_ref, wide_ref = refs[nodes : nodes + 3]
    filters, streams, flat, sems = refs[nodes + 3 :]
    place = lax.axis_index("ctx")
    block = qkv_ref.shape[2]
    rim = flat_ref.shape[1] - 1
    shares = [
        pl.ds(pl.multiple_of((place ^ mask) * chans, chans), chans) for mask in range(nodes)
    ]
    flat_move = pltpu.make_async_copy(flat_ref, flat, sems.at[0])
    query_move = pltpu.make_async_copy(qkv_ref.at[0], query_ref, sems.at[1])
    filter_move = pltpu.make_async_copy(filter_ref, filters, sems.at[2])
    stream_move = pltpu.make_async_copy(qkv_ref.at[pl.ds(1, 2)], streams, sems.at[3])
    for move in (flat_move, stream_move, query_move, filter_move):
        move.start()
    lane = lax.broadcasted_iota(jnp.int32, (chans, LANES), 1)

    flat_move.wait()
    both = widened(jnp.concatenate([flat[1], flat[2]], axis=1))
    for stream in range(2):
        wide_ref[stream] = both[stream * flat.shape[2] : (stream + 1) * flat.shape[2]]
    first_ref[...] = flat[0]
    query_move.wait()
    edges = jnp.zeros((chans, LANES), jnp.float32)
    for share in range(nodes):
        tile = query_ref[share * chans : (share + 1) * chans, block - LANES :]
        moved = pltpu.roll(tile.astype(jnp.float32), LANE_Q + (share + 1) * rim, 1)
        edges = jnp.where(lane >= LANE_Q + share * rim, moved, edges)
    stream_move.wait()
    for mask, rows in reversed(list(enumerate(shares))):
        edge = edges
        raws = [streams[stream, rows, :] for stream in range(2)]
        wides = [tap_tiles(wide_ref, stream, rows) for stream in range(2)]
        for stream in reversed(range(2)):
            ends = jnp.where(lane < rim, raws[stream][:, :LANES], raws[stream][:, block - LANES :])
            at = stream * LANE_V
            moved = pltpu.roll(ends, at + rim, 1).astype(jnp.float32)
            edge = jnp.where(lane < at + LANE_V, moved, edge)
        outs[mask][:, 2 * block :] = edge.astype(jnp.bfloat16)
        before = [None, None]
        for index in range(block // LANES):
            product = None
            for stream in range(2):
                tile = raws[stream][:, index * LANES : (index + 1) * LANES]
                wide = wides[stream]
                moved = [pltpu.roll(tile, shift, 1) for shift in range(1, rim + 1)]
                behind = before[stream] or moved
                total = wide[0] * tile.astype(jnp.float32)
                for shift in range(1, rim + 1):
                    joined = jnp.where(lane < shift, behind[shift - 1], moved[shift - 1])
                    total = total + wide[shift] * joined.astype(jnp.float32)
                before[stream] = moved
                product = total if product is None else product * total
            outs[mask][:, index * LANES : (index + 1) * LANES] = product.astype(jnp.bfloat16)
    filter_move.wait()
    for mask, rows in enumerate(shares):
        outs[mask][:, block : 2 * block] = filters[rows, :].astype(jnp.bfloat16)


def pack(qkv, long_filter, short_taps, nodes, chans):
    _, every, block = qkv.shape
    far = pl.BlockSpec(memory_space=pltpu.HBM)
    near = pl.BlockSpec(memory_space=pltpu.VMEM)
    flat = jnp.swapaxes(short_taps, 1, 2)
    *pieces, query, first, wide = pl.pallas_call(
        lambda *refs: pack_kernel(nodes, chans, *refs),
        out_shape=[jax.ShapeDtypeStruct((chans, 2 * block + LANES), jnp.bfloat16)] * nodes
        + [
            jax.ShapeDtypeStruct((every, block), jnp.bfloat16),
            jax.ShapeDtypeStruct(flat.shape[1:], jnp.float32),
            jax.ShapeDtypeStruct((2, every, short_taps.shape[2] * LANES), jnp.float32),
        ],
        in_specs=[far] * 3,
        out_specs=[near] * (nodes + 3),
        scratch_shapes=[
            pltpu.VMEM((every, block), jnp.float32),
            pltpu.VMEM((2, every, block), jnp.bfloat16),
            pltpu.VMEM(flat.shape, jnp.float32),
            pltpu.SemaphoreType.DMA((4,)),
        ],
        compiler_params=pltpu.CompilerParams(vmem_limit_bytes=16 << 20),
        name="pack",
    )(*in_hbm(qkv, long_filter, flat))
    return pieces, (query, first), wide


def query_kernel(nodes, query_ref, flat_ref, *refs):
    pieces = refs[:nodes]
    out_ref, wide_ref = refs[nodes:]
    wide_ref[0] = widened(flat_ref[...])
    place = lax.axis_index("ctx")
    _, chans, block = out_ref.shape
    rim = wide_ref.shape[2] // LANES - 1
    lane = lax.broadcasted_iota(jnp.int32, (chans, LANES), 1)
    edge = jnp.zeros((chans, LANES), jnp.float32)
    for mask in range(1, nodes):
        before = (place ^ mask) == place - 1
        found = pieces[mask][:, pieces[mask].shape[1] - LANES :].astype(jnp.float32)
        edge = jnp.where(before, found, edge)
    for mask in range(nodes):
        share = place ^ mask
        rows = pl.ds(pl.multiple_of(share * chans, chans), chans)
        weights = [tile[:, :1] for tile in tap_tiles(wide_ref, 0, rows)]
        values = query_ref[rows, :].astype(jnp.float32)
        history = pltpu.roll(edge, LANES - LANE_Q - (share + 1) * rim, 1)
        first = weights[0] * values[:, :LANES]
        for shift in range(1, rim + 1):
            joined = jnp.where(lane >= LANES - shift, history, values[:, :LANES])
            first = first + weights[shift] * pltpu.roll(joined, shift, 1)
        out_ref[nodes - 1 - mask] = rolled_taps(values, weights)
        out_ref[nodes - 1 - mask, :, :LANES] = first


def query_features(query, flat, pieces, nodes, chans):
    near = pl.BlockSpec(memory_space=pltpu.VMEM)
    return pl.pallas_call(
        lambda *refs: query_kernel(nodes, *refs),
        out_shape=jax.ShapeDtypeStruct((nodes, chans, query.shape[1]), jnp.float32),
        in_specs=[near] * (2 + nodes),
        out_specs=near,
        scratch_shapes=[pltpu.VMEM((1, flat.shape[1], flat.shape[0] * LANES), jnp.float32)],
        compiler_params=pltpu.CompilerParams(vmem_limit_bytes=16 << 20),
        name="query_features",
    )(query, flat, *pieces)


def long_kernel(
    nodes, chans, per_node, rim, wide_ref, first_ref, twist_ref, second_ref, last_ref, skip_ref, *refs
):
    pieces = refs[:nodes][::-1]
    outs = refs[nodes : 2 * nodes]
    raw, edges, final = refs[2 * nodes :]
    rows = nodes * per_node
    pitch = rows + PAD
    place = lax.axis_index("ctx")
    base = place * chans
    block = per_node * LANES

    if rim:
        lane = lax.broadcasted_iota(jnp.int32, (chans, LANES), 1)
        own = pl.ds(pl.multiple_of(base, chans), chans)
        edges[0] = jnp.zeros((chans, LANES), jnp.bfloat16)
        for mask in range(nodes):
            edges[(place ^ mask) + 1] = pieces[mask][:, 2 * block :]
        wide = [tap_tiles(wide_ref, stream, own) for stream in range(2)]

    def repaired(mask, tile):
        before, now = edges[place ^ mask], pieces[mask][:, 2 * block :]
        product = None
        for stream in range(2):
            back = (LANES - stream * LANE_V) % LANES
            joined = jnp.where(lane < stream * LANE_V + rim, before, now)
            if back:
                joined = pltpu.roll(joined, back, 1)
            featured = wide[stream][0] * joined.astype(jnp.float32)
            for shift in range(1, rim + 1):
                moved = pltpu.roll(joined, shift, 1).astype(jnp.float32)
                featured = featured + wide[stream][shift] * moved
            product = featured if product is None else product * featured
        product = pltpu.roll(product, LANES - rim, 1).astype(jnp.bfloat16).astype(jnp.float32)
        return jnp.where(lane < rim, product, tile)

    for part in reversed(range(2)):
        for mask in range(nodes):
            start = (place ^ mask) * per_node
            for tile in range(per_node):
                at = part * block + tile * LANES
                values = pieces[mask][:, at : at + LANES].astype(jnp.float32)
                if rim and at == 0:
                    values = repaired(mask, values)
                raw[part, pl.ds(start + tile, chans, stride=pitch), :] = values

    cos_twist = twist_ref[:, :LANES]
    sin_twist = twist_ref[:, LANES:]
    skips = skip_ref[pl.ds(pl.multiple_of(base, chans), chans), :]

    def inner(parts):
        high, low = halves(jnp.concatenate(parts, axis=0))
        return dot(jnp.concatenate([high, low, high], axis=1), second_ref[...])

    def turn(real, imag, axis):
        return jnp.concatenate(
            [real * cos_twist + imag * sin_twist, imag * cos_twist - real * sin_twist], axis=axis
        )

    spectra = [[], []]
    for chan in range(chans):
        span = slice(chan * pitch, chan * pitch + rows)
        both = jnp.concatenate([raw[0, span, :], raw[1, span, :]], axis=1).astype(jnp.bfloat16)
        section = dot(first_ref[...], jnp.concatenate([both, both], axis=0))
        for part in range(2):
            cols = slice(part * LANES, (part + 1) * LANES)
            spectra[part].append(turn(section[:rows, cols], section[rows:, cols], 1))
    spectra = spectra[0] + spectra[1]
    fil_spec = inner(spectra[chans:])
    sig_spec = inner(spectra[:chans])
    def product(chan):
        sig = sig_spec[chan * rows : (chan + 1) * rows, :]
        fil = fil_spec[chan * rows : (chan + 1) * rows, :]
        sig_real, sig_imag = sig[:, :LANES], sig[:, LANES:]
        fil_real, fil_imag = fil[:, :LANES], fil[:, LANES:]
        return jnp.concatenate(
            [
                sig_real * fil_real - sig_imag * fil_imag,
                -(sig_real * fil_imag + sig_imag * fil_real),
            ],
            axis=1,
        )

    group = max(chans // 4, 1)
    groups = [range(begin, begin + group) for begin in range(0, chans, group)]
    turned = []
    for members in groups:
        back = inner([product(chan) for chan in members])
        for index in range(group):
            at = slice(index * rows, (index + 1) * rows)
            turned.append(turn(back[at, :LANES], back[at, LANES:], 0))
    for members in groups:
        high, low = halves(jnp.concatenate([turned[chan] for chan in members], axis=1))
        convolved = dot(last_ref[...], jnp.concatenate([high, low, high], axis=0))
        for index, chan in enumerate(members):
            span = slice(chan * pitch, chan * pitch + rows)
            final[span, :] = (
                convolved[:, index * LANES : (index + 1) * LANES]
                + skips[chan : chan + 1, :] * raw[0, span, :]
            )
    for mask in range(nodes):
        start = (place ^ mask) * per_node
        for tile in range(per_node):
            outs[mask][:, tile * LANES : (tile + 1) * LANES] = final[
                pl.ds(start + tile, chans, stride=pitch), :
            ].astype(jnp.bfloat16)


def long_mix(pieces, wide, tables, block):
    nodes = len(pieces)
    chans, width = pieces[0].shape
    per_node = block // LANES
    rows = nodes * per_node
    rim = wide.shape[2] // LANES - 1 if width > 2 * block else 0
    near = pl.BlockSpec(memory_space=pltpu.VMEM)
    return pl.pallas_call(
        lambda *refs: long_kernel(nodes, chans, per_node, rim, *refs),
        out_shape=[jax.ShapeDtypeStruct((chans, block), jnp.bfloat16)] * nodes,
        in_specs=[near] * (1 + len(tables) + nodes),
        out_specs=[near] * nodes,
        scratch_shapes=[
            pltpu.VMEM((2, (chans + 1) * (rows + PAD), LANES), jnp.float32),
            pltpu.VMEM((nodes + 1, chans, LANES), jnp.bfloat16),
            pltpu.VMEM(((chans + 1) * (rows + PAD), LANES), jnp.float32),
        ],
        compiler_params=pltpu.CompilerParams(vmem_limit_bytes=24 << 20),
        name="long_mix",
    )(wide, *tables, *pieces[::-1])


def gather_blocks(depths, blocks, gathered):
    place = lax.axis_index("ctx")
    spot = lax.axis_index("ch")
    level, core = spot // 2, spot % 2
    for index, block in enumerate(blocks):
        nodes, chans, _ = block.shape
        side = core ^ (index % 2)
        for mask in range(nodes):
            row = ((2 * (index // 2) + side) * nodes + (place ^ mask)) * chans
            gathered[pl.ds(pl.multiple_of(row, chans), chans), :] = block[nodes - 1 - mask]
    width = 2 * nodes * chans
    return [pl.ds(pl.multiple_of((level ^ depth) * width, width), width) for depth in depths]


def partial_kernel(depths, rows, weight_ref, *refs):
    blocks = refs[: 2 * len(depths)]
    out_ref, gathered = refs[2 * len(depths) :]
    columns = gather_blocks(depths, blocks, gathered)
    for begin in range(0, out_ref.shape[0], rows):
        weight = jnp.concatenate([weight_ref[begin : begin + rows, at] for at in columns], axis=1)
        out_ref[begin : begin + rows, :] = dot(weight, gathered[...])


def final_kernel(depths, cuts, weight_ref, partial_ref, *refs):
    blocks = refs[: 2 * len(depths)]
    out_ref, gathered, held, sems = refs[2 * len(depths) :]
    columns = gather_blocks(depths, blocks, gathered)
    copies = []
    for part, (begin, end) in enumerate(zip(cuts, cuts[1:])):
        weight = jnp.concatenate([weight_ref[begin:end, at] for at in columns], axis=1)
        total = partial_ref[begin:end, :] + dot(weight, gathered[...])
        held[begin:end, :] = total.astype(jnp.bfloat16)
        rows = pl.ds(begin, end - begin)
        copies.append(
            pltpu.make_async_copy(held.at[rows, :], out_ref.at[rows, :], sems.at[part])
        )
        copies[-1].start()
    for copy in copies:
        copy.wait()


def project_early(early, out_weight):
    features, _ = out_weight.shape
    near = pl.BlockSpec(memory_space=pltpu.VMEM)
    blocks = [block for pair in early.values() for block in pair]
    nodes, chans, block = blocks[0].shape
    depth = nodes * chans * len(blocks)
    cost = pl.CostEstimate(
        flops=0, bytes_accessed=0, transcendentals=0
    )
    return pl.pallas_call(
        lambda *refs: partial_kernel(tuple(early), features // 4, *refs),
        out_shape=jax.ShapeDtypeStruct((features, block), jnp.float32),
        in_specs=[near] * (1 + len(blocks)),
        out_specs=near,
        scratch_shapes=[pltpu.VMEM((depth, block), jnp.bfloat16)],
        compiler_params=pltpu.CompilerParams(vmem_limit_bytes=16 << 20),
        cost_estimate=cost,
        name="project_early",
    )(out_weight, *blocks)


def project_late(partial, late, out_weight):
    features, _ = out_weight.shape
    near = pl.BlockSpec(memory_space=pltpu.VMEM)
    blocks = [block for pair in late.values() for block in pair]
    nodes, chans, block = blocks[0].shape
    depth = nodes * chans * len(blocks)
    cuts = tuple(range(0, features + 1, features // 8))
    return pl.pallas_call(
        lambda *refs: final_kernel(tuple(late), cuts, *refs),
        out_shape=jax.ShapeDtypeStruct((features, block), jnp.bfloat16),
        in_specs=[near] * (2 + len(blocks)),
        out_specs=pl.BlockSpec(memory_space=pl.ANY),
        scratch_shapes=[
            pltpu.VMEM((depth, block), jnp.bfloat16),
            pltpu.VMEM((features, block), jnp.bfloat16),
            pltpu.SemaphoreType.DMA((len(cuts) - 1,)),
        ],
        compiler_params=pltpu.CompilerParams(vmem_limit_bytes=16 << 20),
        name="project_late",
    )(out_weight, partial, *blocks)


def project_plain(blocks, out_weight):
    nodes, chans, block = blocks[0].shape
    stacks = len(blocks) // 2
    place = lax.axis_index("ctx")
    spot = lax.axis_index("ch")
    found = jnp.stack(blocks).reshape(2, stacks, nodes, chans, block)
    index = jnp.arange(2 * stacks, dtype=jnp.int32) ^ spot
    found = found[index % 2, index // 2]
    found = found[:, nodes - 1 - (jnp.arange(nodes, dtype=jnp.int32) ^ place)]
    summed = jnp.dot(
        out_weight, found.reshape(-1, block), preferred_element_type=jnp.float32
    )
    return summed.astype(jnp.bfloat16)


def features_plain(qkv, short_taps):
    block = qkv.shape[2]
    tap_count = short_taps.shape[2]
    devices = lax.axis_size("ctx")
    route = [(i, i + 1) for i in range(devices - 1)]
    history = lax.ppermute(qkv[:, :, block - (tap_count - 1) :], "ctx", route)
    extended = jnp.concatenate([history, qkv], axis=2).astype(jnp.float32)
    result = jnp.zeros(qkv.shape, jnp.float32)
    for offset in range(tap_count):
        begin = tap_count - 1 - offset
        result = (
            result
            + short_taps[:, :, offset : offset + 1] * extended[:, :, begin : begin + block]
        )
    return result


def swapped(block, mask, axis):
    if mask == 0:
        return block
    return lax.ppermute(block, axis, [(i, i ^ mask) for i in range(lax.axis_size(axis))])


def local(qkv, short_taps, long_filter, skip_gain, out_weight):
    nodes = lax.axis_size("ctx")
    spread = lax.axis_size("ch")
    stacks = spread // 2
    place = lax.axis_index("ctx")
    _, every, block = qkv.shape
    chans = every // nodes
    fits = chans % 16 == 0

    if fits:
        pieces, query, wide = pack(qkv, long_filter, short_taps, nodes, chans)
    else:
        wide = short_taps
        query, key, value = features_plain(qkv, short_taps)
        both = jnp.concatenate([key * value, long_filter], axis=1).astype(jnp.bfloat16)
        both = both.reshape(nodes, chans, 2 * block)
        pieces = [lax.dynamic_index_in_dim(both, place ^ mask, 0, False) for mask in range(nodes)]
    pieces = [swapped(pieces[mask], mask, "ctx") for mask in range(nodes)]
    out_weight, *tables = near_tables(
        nodes * block // LANES, skip_gain, out_weight, pieces[0]
    )
    mixed = long_mix(pieces, wide, tables, block)

    if fits:
        tied = lax.optimization_barrier((mixed[0], *pieces[::-1]))[:0:-1]
        featured = query_features(*query, tied, nodes, chans)
    else:
        featured = query.reshape(nodes, chans, block)[jnp.arange(nodes, dtype=jnp.int32) ^ place][::-1]
    mixed = [swapped(mixed[mask], mask, "ctx") for mask in range(nodes)]
    mixed = jnp.stack(mixed[::-1])
    gated = (featured * mixed.astype(jnp.float32)).astype(jnp.bfloat16)

    column = [swapped(gated, 2 * depth, "ch") for depth in range(stacks)]
    if not fits:
        return project_plain(column + [swapped(part, 1, "ch") for part in column], out_weight)
    pairs = {depth: (part, swapped(part, 1, "ch")) for depth, part in enumerate(column)}
    late = {depth: pairs.pop(depth) for depth in (3, 1)}
    return project_late(project_early(pairs, out_weight), late, out_weight)


def solution(mesh):
    placed = (P(None, "ch", "ctx"), P(None, "ch", None), P("ch", "ctx"), P("ch"), P("ch", None))
    return jax.shard_map(
        local, mesh=mesh, in_specs=placed, out_specs=P("ch", "ctx"), check_vma=False
    )
```

```python
import math

import numpy as np

import jax
import jax.numpy as jnp
from jax import lax
from jax.experimental import pallas as pl
from jax.experimental.pallas import tpu as pltpu
from jax.sharding import PartitionSpec as P

LANES = 128
PAD = 8
LANE_V = 16
LANE_Q = 32


def split_table(table):
    high = table.astype(jnp.bfloat16)
    low = (table - high.astype(np.float64)).astype(jnp.bfloat16)
    return high, low


def dft_tables(rows):
    total = 2 * rows * LANES
    block = np.arange(rows, dtype=np.float64)
    freq = np.arange(rows, dtype=np.float64) + 0.5
    lane = np.arange(LANES, dtype=np.float64)
    head = 2.0 * math.pi * np.outer(freq, block) / (2 * rows)
    first = np.concatenate(
        split_table(np.concatenate([np.cos(head), -np.sin(head)], axis=0)), axis=1
    )
    turn = 2.0 * math.pi * np.outer(freq, lane) / total
    twist = np.concatenate([np.cos(turn), np.sin(turn)], axis=1).astype(np.float32)
    inner = 2.0 * math.pi * np.outer(lane, lane) / LANES
    square = np.block([[np.cos(inner), -np.sin(inner)], [np.sin(inner), np.cos(inner)]])
    square_high, square_low = split_table(square)
    second = np.concatenate([square_high, square_high, square_low], axis=0)
    tail = head.T
    tail_high, tail_low = split_table(
        (2.0 / total) * np.concatenate([np.cos(tail), np.sin(tail)], axis=1)
    )
    last = np.concatenate([tail_high, tail_high, tail_low], axis=1)
    return first, twist, second, last


def halves(value):
    high = value.astype(jnp.bfloat16)
    low = (value - high.astype(jnp.float32)).astype(jnp.bfloat16)
    return high, low


def dot(left, right):
    return jnp.dot(left, right, preferred_element_type=jnp.float32)


def rolled_taps(values, weights):
    total = weights[0] * values
    for shift, weight in enumerate(weights[1:], 1):
        total = total + weight * pltpu.roll(values, shift, 1)
    return total


def widened(flat):
    count, every = flat.shape
    rest = jnp.concatenate([flat, jnp.zeros((8 - count, every), jnp.float32)], axis=0)
    parts = []
    for _ in range(3):
        part = rest.astype(jnp.bfloat16)
        rest = rest - part.astype(jnp.float32)
        parts.append(part.astype(jnp.float32))
    shape = (8, count * LANES)
    tap = lax.broadcasted_iota(jnp.int32, shape, 0) * LANES
    lane = lax.broadcasted_iota(jnp.int32, shape, 1)
    ones = jnp.where((lane >= tap) & (lane < tap + LANES), 1.0, 0.0)
    left = jnp.concatenate(parts, axis=0).T.astype(jnp.bfloat16)
    return dot(left, jnp.concatenate([ones] * 3, axis=0).astype(jnp.bfloat16))


def tap_tiles(wide_ref, stream, rows):
    return [wide_ref[stream, rows, at : at + LANES] for at in range(0, wide_ref.shape[2], LANES)]


def in_hbm(*arrays):
    return [pltpu.with_memory_space_constraint(array, pltpu.HBM) for array in arrays]


def tables_kernel(count, *refs):
    sources, skip_ref = refs[:count], refs[count]
    outs, column_ref = refs[count + 2 : 2 * count + 2], refs[2 * count + 2]
    skips, sems = refs[2 * count + 3 :]
    moves = [
        pltpu.make_async_copy(source, out, sems.at[index])
        for index, (source, out) in enumerate(zip(sources, outs))
    ]
    moves.append(pltpu.make_async_copy(skip_ref, skips, sems.at[count]))
    for move in moves:
        move.start()
    moves[count].wait()
    column_ref[...] = jnp.broadcast_to(skips[...].reshape(1, -1), (LANES, skips.shape[0])).T
    for move in moves[:count]:
        move.wait()


def near_tables(rows, skip_gain, out_weight, after):
    tables = [out_weight] + [jnp.asarray(table) for table in dft_tables(rows)]
    count = len(tables)
    far = pl.BlockSpec(memory_space=pltpu.HBM)
    near = pl.BlockSpec(memory_space=pltpu.VMEM)
    return pl.pallas_call(
        lambda *refs: tables_kernel(count, *refs),
        out_shape=[jax.ShapeDtypeStruct(table.shape, table.dtype) for table in tables]
        + [jax.ShapeDtypeStruct((skip_gain.shape[0], LANES), jnp.float32)],
        in_specs=[far] * (count + 1) + [near],
        out_specs=[near] * (count + 1),
        scratch_shapes=[
            pltpu.VMEM(skip_gain.shape, jnp.float32),
            pltpu.SemaphoreType.DMA((count + 1,)),
        ],
        compiler_params=pltpu.CompilerParams(vmem_limit_bytes=16 << 20),
        name="near_tables",
    )(*in_hbm(*tables, skip_gain), after)


def pack_kernel(nodes, chans, qkv_ref, filter_ref, flat_ref, *refs):
    outs = refs[:nodes]
    query_ref, first_ref, wide_ref = refs[nodes : nodes + 3]
    filters, streams, flat, sems = refs[nodes + 3 :]
    place = lax.axis_index("ctx")
    block = qkv_ref.shape[2]
    rim = flat_ref.shape[1] - 1
    shares = [
        pl.ds(pl.multiple_of((place ^ mask) * chans, chans), chans) for mask in range(nodes)
    ]
    flat_move = pltpu.make_async_copy(flat_ref, flat, sems.at[0])
    query_move = pltpu.make_async_copy(qkv_ref.at[0], query_ref, sems.at[1])
    filter_move = pltpu.make_async_copy(filter_ref, filters, sems.at[2])
    stream_move = pltpu.make_async_copy(qkv_ref.at[pl.ds(1, 2)], streams, sems.at[3])
    for move in (flat_move, stream_move, query_move, filter_move):
        move.start()
    lane = lax.broadcasted_iota(jnp.int32, (chans, LANES), 1)

    flat_move.wait()
    for stream in range(2):
        wide_ref[stream] = widened(flat[1 + stream])
    first_ref[...] = flat[0]
    query_move.wait()
    edges = jnp.zeros((chans, LANES), jnp.bfloat16)
    for share in range(nodes):
        tile = query_ref[share * chans : (share + 1) * chans, block - LANES :]
        moved = pltpu.roll(tile, LANE_Q + (share + 1) * rim, 1)
        edges = jnp.where(lane >= LANE_Q + share * rim, moved, edges)
    stream_move.wait()
    for mask, rows in reversed(list(enumerate(shares))):
        edge = edges
        raws = [streams[stream, rows, :] for stream in range(2)]
        wides = [tap_tiles(wide_ref, stream, rows) for stream in range(2)]
        for stream in reversed(range(2)):
            ends = jnp.where(lane < rim, raws[stream][:, :LANES], raws[stream][:, block - LANES :])
            at = stream * LANE_V
            moved = pltpu.roll(ends, at + rim, 1)
            edge = jnp.where(lane < at + LANE_V, moved, edge)
        outs[mask][:, 2 * block :] = edge
        before = [None, None]
        for index in range(block // LANES):
            product = None
            for stream in range(2):
                tile = raws[stream][:, index * LANES : (index + 1) * LANES]
                wide = wides[stream]
                moved = [pltpu.roll(tile, shift, 1) for shift in range(1, rim + 1)]
                behind = before[stream] or moved
                total = wide[0] * tile.astype(jnp.float32)
                for shift in range(1, rim + 1):
                    joined = jnp.where(lane < shift, behind[shift - 1], moved[shift - 1])
                    total = total + wide[shift] * joined.astype(jnp.float32)
                before[stream] = moved
                product = total if product is None else product * total
            outs[mask][:, index * LANES : (index + 1) * LANES] = product.astype(jnp.bfloat16)
    filter_move.wait()
    for mask, rows in enumerate(shares):
        outs[mask][:, block : 2 * block] = filters[rows, :].astype(jnp.bfloat16)


def pack(qkv, long_filter, short_taps, nodes, chans):
    _, every, block = qkv.shape
    far = pl.BlockSpec(memory_space=pltpu.HBM)
    near = pl.BlockSpec(memory_space=pltpu.VMEM)
    flat = jnp.swapaxes(short_taps, 1, 2)
    *pieces, query, first, wide = pl.pallas_call(
        lambda *refs: pack_kernel(nodes, chans, *refs),
        out_shape=[jax.ShapeDtypeStruct((chans, 2 * block + LANES), jnp.bfloat16)] * nodes
        + [
            jax.ShapeDtypeStruct((every, block), jnp.bfloat16),
            jax.ShapeDtypeStruct(flat.shape[1:], jnp.float32),
            jax.ShapeDtypeStruct((2, every, short_taps.shape[2] * LANES), jnp.float32),
        ],
        in_specs=[far] * 3,
        out_specs=[near] * (nodes + 3),
        scratch_shapes=[
            pltpu.VMEM((every, block), jnp.float32),
            pltpu.VMEM((2, every, block), jnp.bfloat16),
            pltpu.VMEM(flat.shape, jnp.float32),
            pltpu.SemaphoreType.DMA((4,)),
        ],
        compiler_params=pltpu.CompilerParams(vmem_limit_bytes=16 << 20),
        name="pack",
    )(*in_hbm(qkv, long_filter, flat))
    return pieces, (query, first), wide


def query_kernel(nodes, query_ref, flat_ref, *refs):
    pieces = refs[:nodes]
    out_ref, wide_ref = refs[nodes:]
    wide_ref[0] = widened(flat_ref[...])
    place = lax.axis_index("ctx")
    _, chans, block = out_ref.shape
    rim = wide_ref.shape[2] // LANES - 1
    lane = lax.broadcasted_iota(jnp.int32, (chans, LANES), 1)
    edge = jnp.zeros((chans, LANES), jnp.float32)
    for mask in range(1, nodes):
        before = (place ^ mask) == place - 1
        found = pieces[mask][:, pieces[mask].shape[1] - LANES :].astype(jnp.float32)
        edge = jnp.where(before, found, edge)
    for mask in range(nodes):
        share = place ^ mask
        rows = pl.ds(pl.multiple_of(share * chans, chans), chans)
        weights = [tile[:, :1] for tile in tap_tiles(wide_ref, 0, rows)]
        values = query_ref[rows, :].astype(jnp.float32)
        history = pltpu.roll(edge, LANES - LANE_Q - (share + 1) * rim, 1)
        first = weights[0] * values[:, :LANES]
        for shift in range(1, rim + 1):
            joined = jnp.where(lane >= LANES - shift, history, values[:, :LANES])
            first = first + weights[shift] * pltpu.roll(joined, shift, 1)
        out_ref[nodes - 1 - mask] = rolled_taps(values, weights)
        out_ref[nodes - 1 - mask, :, :LANES] = first


def query_features(query, flat, pieces, nodes, chans):
    near = pl.BlockSpec(memory_space=pltpu.VMEM)
    return pl.pallas_call(
        lambda *refs: query_kernel(nodes, *refs),
        out_shape=jax.ShapeDtypeStruct((nodes, chans, query.shape[1]), jnp.float32),
        in_specs=[near] * (2 + nodes),
        out_specs=near,
        scratch_shapes=[pltpu.VMEM((1, flat.shape[1], flat.shape[0] * LANES), jnp.float32)],
        compiler_params=pltpu.CompilerParams(vmem_limit_bytes=16 << 20),
        name="query_features",
    )(query, flat, *pieces)


def long_kernel(
    nodes, chans, per_node, rim, wide_ref, first_ref, twist_ref, second_ref, last_ref, skip_ref, *refs
):
    pieces = refs[:nodes][::-1]
    outs = refs[nodes : 2 * nodes]
    raw, edges, final = refs[2 * nodes :]
    rows = nodes * per_node
    pitch = rows + PAD
    place = lax.axis_index("ctx")
    base = place * chans
    block = per_node * LANES

    if rim:
        lane = lax.broadcasted_iota(jnp.int32, (chans, LANES), 1)
        own = pl.ds(pl.multiple_of(base, chans), chans)
        edges[0] = jnp.zeros((chans, LANES), jnp.bfloat16)
        for mask in range(nodes):
            edges[(place ^ mask) + 1] = pieces[mask][:, 2 * block :]
        wide = [tap_tiles(wide_ref, stream, own) for stream in range(2)]

    def repaired(mask, tile):
        before, now = edges[place ^ mask], pieces[mask][:, 2 * block :]
        product = None
        for stream in range(2):
            back = (LANES - stream * LANE_V) % LANES
            joined = jnp.where(lane < stream * LANE_V + rim, before, now)
            if back:
                joined = pltpu.roll(joined, back, 1)
            featured = wide[stream][0] * joined.astype(jnp.float32)
            for shift in range(1, rim + 1):
                moved = pltpu.roll(joined, shift, 1).astype(jnp.float32)
                featured = featured + wide[stream][shift] * moved
            product = featured if product is None else product * featured
        product = pltpu.roll(product, LANES - rim, 1).astype(jnp.bfloat16).astype(jnp.float32)
        return jnp.where(lane < rim, product, tile)

    for part in reversed(range(2)):
        for mask in range(nodes):
            start = (place ^ mask) * per_node
            for tile in range(per_node):
                at = part * block + tile * LANES
                values = pieces[mask][:, at : at + LANES].astype(jnp.float32)
                if rim and at == 0:
                    values = repaired(mask, values)
                raw[part, pl.ds(start + tile, chans, stride=pitch), :] = values

    cos_twist = twist_ref[:, :LANES]
    sin_twist = twist_ref[:, LANES:]
    skips = skip_ref[pl.ds(pl.multiple_of(base, chans), chans), :]

    def inner(parts):
        high, low = halves(jnp.concatenate(parts, axis=0))
        return dot(jnp.concatenate([high, low, high], axis=1), second_ref[...])

    def turn(real, imag, axis):
        return jnp.concatenate(
            [real * cos_twist + imag * sin_twist, imag * cos_twist - real * sin_twist], axis=axis
        )

    spectra = [[], []]
    for chan in range(chans):
        span = slice(chan * pitch, chan * pitch + rows)
        both = jnp.concatenate([raw[0, span, :], raw[1, span, :]], axis=1).astype(jnp.bfloat16)
        section = dot(first_ref[...], jnp.concatenate([both, both], axis=0))
        for part in range(2):
            cols = slice(part * LANES, (part + 1) * LANES)
            spectra[part].append(turn(section[:rows, cols], section[rows:, cols], 1))
    spectra = spectra[0] + spectra[1]
    fil_spec = inner(spectra[chans:])
    sig_spec = inner(spectra[:chans])
    def product(chan):
        sig = sig_spec[chan * rows : (chan + 1) * rows, :]
        fil = fil_spec[chan * rows : (chan + 1) * rows, :]
        sig_real, sig_imag = sig[:, :LANES], sig[:, LANES:]
        fil_real, fil_imag = fil[:, :LANES], fil[:, LANES:]
        return jnp.concatenate(
            [
                sig_real * fil_real - sig_imag * fil_imag,
                -(sig_real * fil_imag + sig_imag * fil_real),
            ],
            axis=1,
        )

    group = max(chans // 4, 1)
    groups = [range(begin, begin + group) for begin in range(0, chans, group)]
    turned = []
    for members in groups:
        back = inner([product(chan) for chan in members])
        for index in range(group):
            at = slice(index * rows, (index + 1) * rows)
            turned.append(turn(back[at, :LANES], back[at, LANES:], 0))
    for members in groups:
        high, low = halves(jnp.concatenate([turned[chan] for chan in members], axis=1))
        convolved = dot(last_ref[...], jnp.concatenate([high, low, high], axis=0))
        for index, chan in enumerate(members):
            span = slice(chan * pitch, chan * pitch + rows)
            final[span, :] = (
                convolved[:, index * LANES : (index + 1) * LANES]
                + skips[chan : chan + 1, :] * raw[0, span, :]
            )
    for mask in range(nodes):
        start = (place ^ mask) * per_node
        for tile in range(per_node):
            outs[mask][:, tile * LANES : (tile + 1) * LANES] = final[
                pl.ds(start + tile, chans, stride=pitch), :
            ].astype(jnp.bfloat16)


def long_mix(pieces, wide, tables, block):
    nodes = len(pieces)
    chans, width = pieces[0].shape
    per_node = block // LANES
    rows = nodes * per_node
    rim = wide.shape[2] // LANES - 1 if width > 2 * block else 0
    near = pl.BlockSpec(memory_space=pltpu.VMEM)
    return pl.pallas_call(
        lambda *refs: long_kernel(nodes, chans, per_node, rim, *refs),
        out_shape=[jax.ShapeDtypeStruct((chans, block), jnp.bfloat16)] * nodes,
        in_specs=[near] * (1 + len(tables) + nodes),
        out_specs=[near] * nodes,
        scratch_shapes=[
            pltpu.VMEM((2, (chans + 1) * (rows + PAD), LANES), jnp.float32),
            pltpu.VMEM((nodes + 1, chans, LANES), jnp.bfloat16),
            pltpu.VMEM(((chans + 1) * (rows + PAD), LANES), jnp.float32),
        ],
        compiler_params=pltpu.CompilerParams(vmem_limit_bytes=24 << 20),
        name="long_mix",
    )(wide, *tables, *pieces[::-1])


def gather_blocks(depths, blocks, gathered):
    place = lax.axis_index("ctx")
    spot = lax.axis_index("ch")
    level, core = spot // 2, spot % 2
    for index, block in enumerate(blocks):
        nodes, chans, _ = block.shape
        side = core ^ (index % 2)
        for mask in range(nodes):
            row = ((2 * (index // 2) + side) * nodes + (place ^ mask)) * chans
            gathered[pl.ds(pl.multiple_of(row, chans), chans), :] = block[nodes - 1 - mask]
    width = 2 * nodes * chans
    return [pl.ds(pl.multiple_of((level ^ depth) * width, width), width) for depth in depths]


def partial_kernel(depths, rows, weight_ref, *refs):
    blocks = refs[: 2 * len(depths)]
    out_ref, gathered = refs[2 * len(depths) :]
    columns = gather_blocks(depths, blocks, gathered)
    for begin in range(0, out_ref.shape[0], rows):
        weight = jnp.concatenate([weight_ref[begin : begin + rows, at] for at in columns], axis=1)
        out_ref[begin : begin + rows, :] = dot(weight, gathered[...])


def final_kernel(depths, cuts, weight_ref, partial_ref, *refs):
    blocks = refs[: 2 * len(depths)]
    out_ref, gathered, held, sems = refs[2 * len(depths) :]
    columns = gather_blocks(depths, blocks, gathered)
    copies = []
    for part, (begin, end) in enumerate(zip(cuts, cuts[1:])):
        weight = jnp.concatenate([weight_ref[begin:end, at] for at in columns], axis=1)
        total = partial_ref[begin:end, :] + dot(weight, gathered[...])
        held[begin:end, :] = total.astype(jnp.bfloat16)
        rows = pl.ds(begin, end - begin)
        copies.append(
            pltpu.make_async_copy(held.at[rows, :], out_ref.at[rows, :], sems.at[part])
        )
        copies[-1].start()
    for copy in copies:
        copy.wait()


def project_early(early, out_weight):
    features, _ = out_weight.shape
    near = pl.BlockSpec(memory_space=pltpu.VMEM)
    blocks = [block for pair in early.values() for block in pair]
    nodes, chans, block = blocks[0].shape
    depth = nodes * chans * len(blocks)
    cost = pl.CostEstimate(
        flops=0, bytes_accessed=0, transcendentals=0
    )
    return pl.pallas_call(
        lambda *refs: partial_kernel(tuple(early), features // 4, *refs),
        out_shape=jax.ShapeDtypeStruct((features, block), jnp.float32),
        in_specs=[near] * (1 + len(blocks)),
        out_specs=near,
        scratch_shapes=[pltpu.VMEM((depth, block), jnp.bfloat16)],
        compiler_params=pltpu.CompilerParams(vmem_limit_bytes=16 << 20),
        cost_estimate=cost,
        name="project_early",
    )(out_weight, *blocks)


def project_late(partial, late, out_weight):
    features, _ = out_weight.shape
    near = pl.BlockSpec(memory_space=pltpu.VMEM)
    blocks = [block for pair in late.values() for block in pair]
    nodes, chans, block = blocks[0].shape
    depth = nodes * chans * len(blocks)
    cuts = tuple(range(0, features + 1, features // 8))
    return pl.pallas_call(
        lambda *refs: final_kernel(tuple(late), cuts, *refs),
        out_shape=jax.ShapeDtypeStruct((features, block), jnp.bfloat16),
        in_specs=[near] * (2 + len(blocks)),
        out_specs=pl.BlockSpec(memory_space=pl.ANY),
        scratch_shapes=[
            pltpu.VMEM((depth, block), jnp.bfloat16),
            pltpu.VMEM((features, block), jnp.bfloat16),
            pltpu.SemaphoreType.DMA((len(cuts) - 1,)),
        ],
        compiler_params=pltpu.CompilerParams(vmem_limit_bytes=16 << 20),
        name="project_late",
    )(out_weight, partial, *blocks)


def project_plain(blocks, out_weight):
    nodes, chans, block = blocks[0].shape
    stacks = len(blocks) // 2
    place = lax.axis_index("ctx")
    spot = lax.axis_index("ch")
    found = jnp.stack(blocks).reshape(2, stacks, nodes, chans, block)
    index = jnp.arange(2 * stacks, dtype=jnp.int32) ^ spot
    found = found[index % 2, index // 2]
    found = found[:, nodes - 1 - (jnp.arange(nodes, dtype=jnp.int32) ^ place)]
    summed = jnp.dot(
        out_weight, found.reshape(-1, block), preferred_element_type=jnp.float32
    )
    return summed.astype(jnp.bfloat16)


def features_plain(qkv, short_taps):
    block = qkv.shape[2]
    tap_count = short_taps.shape[2]
    devices = lax.axis_size("ctx")
    route = [(i, i + 1) for i in range(devices - 1)]
    history = lax.ppermute(qkv[:, :, block - (tap_count - 1) :], "ctx", route)
    extended = jnp.concatenate([history, qkv], axis=2).astype(jnp.float32)
    result = jnp.zeros(qkv.shape, jnp.float32)
    for offset in range(tap_count):
        begin = tap_count - 1 - offset
        result = (
            result
            + short_taps[:, :, offset : offset + 1] * extended[:, :, begin : begin + block]
        )
    return result


def swapped(block, mask, axis):
    if mask == 0:
        return block
    return lax.ppermute(block, axis, [(i, i ^ mask) for i in range(lax.axis_size(axis))])


def local(qkv, short_taps, long_filter, skip_gain, out_weight):
    nodes = lax.axis_size("ctx")
    spread = lax.axis_size("ch")
    stacks = spread // 2
    place = lax.axis_index("ctx")
    _, every, block = qkv.shape
    chans = every // nodes
    fits = chans % 16 == 0

    if fits:
        pieces, query, wide = pack(qkv, long_filter, short_taps, nodes, chans)
    else:
        wide = short_taps
        query, key, value = features_plain(qkv, short_taps)
        both = jnp.concatenate([key * value, long_filter], axis=1).astype(jnp.bfloat16)
        both = both.reshape(nodes, chans, 2 * block)
        pieces = [lax.dynamic_index_in_dim(both, place ^ mask, 0, False) for mask in range(nodes)]
    pieces = [swapped(pieces[mask], mask, "ctx") for mask in range(nodes)]
    out_weight, *tables = near_tables(
        nodes * block // LANES, skip_gain, out_weight, pieces[0]
    )
    mixed = long_mix(pieces, wide, tables, block)

    if fits:
        tied = lax.optimization_barrier((mixed[0], *pieces[::-1]))[:0:-1]
        featured = query_features(*query, tied, nodes, chans)
    else:
        featured = query.reshape(nodes, chans, block)[jnp.arange(nodes, dtype=jnp.int32) ^ place][::-1]
    mixed = [swapped(mixed[mask], mask, "ctx") for mask in range(nodes)]
    mixed = jnp.stack(mixed[::-1])
    gated = (featured * mixed.astype(jnp.float32)).astype(jnp.bfloat16)

    column = [swapped(gated, 2 * depth, "ch") for depth in range(stacks)]
    if not fits:
        return project_plain(column + [swapped(part, 1, "ch") for part in column], out_weight)
    pairs = {depth: (part, swapped(part, 1, "ch")) for depth, part in enumerate(column)}
    late = {depth: pairs.pop(depth) for depth in (3, 1)}
    return project_late(project_early(pairs, out_weight), late, out_weight)


def solution(mesh):
    placed = (P(None, "ch", "ctx"), P(None, "ch", None), P("ch", "ctx"), P("ch"), P("ch", None))
    return jax.shard_map(
        local, mesh=mesh, in_specs=placed, out_specs=P("ch", "ctx"), check_vma=False
    )
```
